512 devices in a mesh: cfg: 2 (over x_lo), blk: 32 (over z, core), uly: 8 (over x_hi, y).
Axes of the slice: x: 4 (x_hi: 2, x_lo: 2; x = x_hi * 2 + x_lo), y: 4, z: 16, core: 2. Of those that a mesh axis runs over, the one named last changes fastest.
Arguments:
- latent_qkv: bfloat16 [2, 12288, 3, 1536], P('cfg', ('blk', 'uly')), may hold values from -8 to 8
- text_kv: bfloat16 [2, 333, 2, 1536], P('cfg', None, None, 'uly'), may hold values from -8 to 8
- hidden_in: bfloat16 [2, 12288, 1536], P('cfg', ('blk', 'uly')), may hold values from -4 to 4
- modulation: float32 [2, 3, 1536], P('cfg'), may hold values from -4 to 4
- out_weight: bfloat16 [1536, 1536], P('uly'), may hold values from -0.875 to 0.875
- out_bias: float32 [1536], replicated, may hold values from -3 to 3
- proj_weight: bfloat16 [1536, 64], replicated, may hold values from -0.15625 to 0.15625
- proj_bias: float32 [64], replicated, may hold values from -3 to 3
- guidance: float32 [1], replicated, may hold values from 2 to 5
- sigma: float32 [1], replicated, may hold values from 0.05 to 0.2
- sample: float32 [256, 3072], P(('blk', 'uly'), 'cfg'), may hold values from -6 to 6
Outputs:
- velocity: float32 [256, 3072], P(('blk', 'uly'), 'cfg')
- denoised: float32 [256, 3072], P(('blk', 'uly'), 'cfg')
The draws below stay inside these ranges and needn't reach their ends.
All inputs are finite; a program needn't handle non-finite values.
Results may differ from the reference program's by a relative error of at most 0.017.
Values may be sent and summed in bfloat16 or wider, within the bound.
No kernel may reach another device: no remote copies, remote signals or barrier semaphores. Data moves between devices by JAX's collectives and lax.ppermute only.
A program may use at most 64 MiB of HBM per device.

```python
import math
import jax
import jax.numpy as jnp
from jax import lax

HEADS = 24
HEAD_DIM = 64
D = 1536
CHANNELS = 16
TXT = 333
PATCH_COLS = 96
PATCH_ROWS = 128
LATENT = 12288
N_BLK = 32


def draw_latent_qkv(key, part):
    key = jax.random.fold_in(key, 11)
    keys = jax.random.split(key, 3)
    shape = (2, LATENT, 3, D)
    base = jax.random.normal(keys[0], shape, jnp.float32)
    col_scale = jnp.exp(jax.random.uniform(keys[2], (2, 1, D), jnp.float32, math.log(0.3), math.log(3.0)))
    scaled_keys = base[:, :, 1, :] * col_scale
    drawn = base.at[:, :, 1, :].set(scaled_keys)
    return jnp.clip(drawn, -8.0, 8.0).astype(jnp.bfloat16)


def level_of(stream_key, dims, shards, low, high):
    def one(dim, parts):
        steps = jax.random.uniform(jax.random.fold_in(jax.random.fold_in(stream_key, 6), dim), (parts,), jnp.float32, low / len(shards), high / len(shards))
        return jnp.repeat(jnp.exp(steps), dims[dim] // parts).reshape((-1,) + (1,) * (len(dims) - dim - 1))

    level = one(*shards[0])
    for cut in shards[1:]:
        level = level * one(*cut)
    return level


def noise(stream_key, dims, scale, most, shards=(), held_as=jnp.bfloat16):
    level = level_of(stream_key, dims, shards, -0.22, 0.18) if shards else 1.0
    values = jax.random.normal(stream_key, dims, jnp.float32) * scale * level
    return jnp.minimum(jnp.maximum(values, -most), most).astype(held_as)


def setup_inputs(seed: int = 0) -> dict:
    seeds = jax.random.split(jax.random.key(seed), 12)
    return {
        "latent_qkv": draw_latent_qkv(jax.random.fold_in(seeds[11], 71), 0),
        "text_kv": noise(seeds[1], (2, TXT, 2, D), 1.5, 8.0, ((0, 2), (3, 8))),
        "hidden_in": noise(seeds[2], (2, LATENT, D), 0.5, 4.0, ((0, 2), (1, 256))),
        "modulation": noise(seeds[3], (2, 3, D), 0.7, 4.0, ((0, 2),), jnp.float32),
        "out_weight": noise(seeds[4], (D, D), (D // 32) ** -0.5, 0.875, ((0, 8),)),
        "out_bias": noise(seeds[5], (D,), 0.5, 3.0, (), jnp.float32),
        "proj_weight": noise(seeds[6], (D, 4 * CHANNELS), D ** -0.5, 0.15625),
        "proj_bias": noise(seeds[7], (4 * CHANNELS,), 0.5, 3.0, (), jnp.float32),
        "guidance": jnp.clip(jax.random.uniform(seeds[8], (1,), jnp.float32, 2.0, 5.0), 2.0, 5.0),
        "sigma": jnp.clip(jax.random.uniform(seeds[9], (1,), jnp.float32, 0.05, 0.2), 0.05, 0.2),
        "sample": noise(seeds[10], (2 * PATCH_ROWS, 2 * PATCH_COLS * CHANNELS), 1.0, 6.0, ((0, 256), (1, 2)), jnp.float32),
    }


def attend_branch(queries, keys, values):
    score_scale = HEAD_DIM ** (-0.5)
    heads_q = queries.reshape(LATENT, HEADS, HEAD_DIM).transpose(1, 0, 2)
    heads_k = keys.reshape(LATENT + TXT, HEADS, HEAD_DIM).transpose(1, 0, 2)
    heads_v = values.reshape(LATENT + TXT, HEADS, HEAD_DIM).transpose(1, 0, 2)

    def one_head(operands):
        q_head, k_head, v_head = operands
        blocks = q_head.reshape(N_BLK, LATENT // N_BLK, HEAD_DIM)

        def one_block(q_block):
            scores = jnp.dot(q_block, k_head.T, preferred_element_type=jnp.float32) * score_scale
            largest = lax.optimization_barrier(jnp.max(scores, axis=-1, keepdims=True))
            expo = jnp.exp(scores - largest)
            totals = lax.optimization_barrier(jnp.sum(expo, axis=-1, keepdims=True))
            weights = expo.astype(jnp.bfloat16)
            summed = jnp.dot(weights, v_head, preferred_element_type=jnp.float32)
            return (summed / totals).astype(jnp.bfloat16)
        return lax.map(one_block, blocks).reshape(LATENT, HEAD_DIM)
    result = lax.map(one_head, (heads_q, heads_k, heads_v))
    return result.transpose(1, 0, 2).reshape(LATENT, D)

def branch_velocity(latent_qkv, text_kv, hidden_in, modulation, out_weight, out_bias, proj_weight, proj_bias, branch):
    queries = latent_qkv[branch, :, 0, :]
    keys = jnp.concatenate([latent_qkv[branch, :, 1, :], text_kv[branch, :, 0, :]], axis=0)
    values = jnp.concatenate([latent_qkv[branch, :, 2, :], text_kv[branch, :, 1, :]], axis=0)
    attended = attend_branch(queries, keys, values)
    projected = jnp.dot(attended, out_weight, preferred_element_type=jnp.float32) + out_bias
    residual = hidden_in[branch].astype(jnp.float32) + modulation[branch, 0] * projected
    middle = lax.optimization_barrier(jnp.mean(residual, axis=-1, keepdims=True))
    centered = residual - middle
    spread = lax.optimization_barrier(jnp.mean(centered * centered, axis=-1, keepdims=True))
    normed = centered * lax.rsqrt(spread + 1e-06) * (1.0 + modulation[branch, 1]) + modulation[branch, 2]
    normed = normed.astype(jnp.bfloat16)
    return jnp.dot(normed, proj_weight, preferred_element_type=jnp.float32) + proj_bias

def reference(latent_qkv, text_kv, hidden_in, modulation, out_weight, out_bias, proj_weight, proj_bias, guidance, sigma, sample):
    cond = branch_velocity(latent_qkv, text_kv, hidden_in, modulation, out_weight, out_bias, proj_weight, proj_bias, 0)
    uncond = branch_velocity(latent_qkv, text_kv, hidden_in, modulation, out_weight, out_bias, proj_weight, proj_bias, 1)
    guided = uncond + guidance[0] * (cond - uncond)
    image = guided.reshape(PATCH_ROWS, PATCH_COLS, 2, 2, CHANNELS).transpose(0, 2, 1, 3, 4)
    velocity = image.reshape(2 * PATCH_ROWS, 2 * PATCH_COLS * CHANNELS)
    denoised = sample - sigma[0] * velocity
    return (velocity, denoised)
```

```python
import functools
import math

import jax
import jax.numpy as jnp
from jax import lax
from jax.experimental import pallas as pl
from jax.experimental.pallas import tpu as pltpu
from jax.sharding import Mesh, PartitionSpec as P

HEAD_DIM = 64
LANES = 128
ROW_TILE = 256
LOG2_SCALE = math.log2(math.e) * HEAD_DIM**-0.5
F32 = jnp.float32
BF16 = jnp.bfloat16
HEAD_AXES = ("zl", "y")
BLOCK_AXES = ("zl", "core", "xh", "y")


def params(**extra):
    return pltpu.CompilerParams(vmem_limit_bytes=32 * 1024 * 1024, **extra)


def lane_index(shape):
    return lax.broadcasted_iota(jnp.int32, shape, len(shape) - 1)


def pack_kernel(groups, heads, x_ref, out_ref):
    rows = x_ref.shape[1]
    half = rows // 2
    for group in range(groups):
        queries, pairs = [], []
        for head in range(heads):
            start = (group * heads + head) * HEAD_DIM
            cols = slice(start, start + HEAD_DIM)
            q = x_ref[0, :, cols].astype(F32)
            k = x_ref[1, :, cols].astype(F32)
            v = x_ref[2, :, cols].astype(F32)
            queries.append(jnp.concatenate([q[:half], q[half:]], axis=1))
            pairs.append(jnp.concatenate([k, v], axis=1))
        out_ref[group] = jnp.concatenate(queries + pairs, axis=0).astype(BF16)


def pack(x, groups, heads):
    rows = x.shape[1]
    return pl.pallas_call(
        functools.partial(pack_kernel, groups, heads),
        out_shape=jax.ShapeDtypeStruct((groups, heads * (rows // 2 + rows), LANES), BF16),
        compiler_params=params(),
        name="pack_heads",
    )(x)


def queries_kernel(heads, place_ref, own_ref, other_ref, out_ref, wide_ref):
    here = place_ref[0]
    cores, sources, _, half, _ = own_ref.shape
    across = sources // 2
    low = lane_index((half, LANES)) < HEAD_DIM
    for side, ref in ((here, own_ref), (1 - here, other_ref)):
        for core in range(cores):
            for source in range(sources):
                zl, y = divmod(source, across)
                first = (zl * cores + core) * 2 * across + y
                row = pl.multiple_of((first + side * across) * half, 8)
                for head in range(heads):
                    both = ref[core, source, head].astype(F32)
                    turned = pltpu.roll(both, HEAD_DIM, 1)
                    wide_ref[head, 0, pl.ds(row, half)] = jnp.where(low, both, 0.0)
                    wide_ref[head, 1, pl.ds(row, half)] = jnp.where(low, turned, 0.0)
    out_ref[...] = wide_ref[...].astype(BF16)


def unpack_queries(place, own, other):
    cores, sources, heads, half, _ = own.shape
    shape = (heads, 2, 2 * cores * sources * half, LANES)
    return pl.pallas_call(
        functools.partial(queries_kernel, heads),
        out_shape=jax.ShapeDtypeStruct(shape, BF16),
        in_specs=[
            pl.BlockSpec(memory_space=pltpu.SMEM),
            pl.BlockSpec(memory_space=pltpu.VMEM),
            pl.BlockSpec(memory_space=pltpu.VMEM),
        ],
        out_specs=pl.BlockSpec(memory_space=pltpu.VMEM),
        scratch_shapes=[pltpu.VMEM(shape, F32)],
        compiler_params=params(),
        name="unpack_queries",
    )(place, own, other)


def update(state, scores, values, flipped):
    lane = lane_index((scores[0].shape[0], LANES))
    largest = functools.reduce(jnp.maximum, [jnp.max(s, axis=1, keepdims=True) for s in scores])
    if state is not None:
        before = state[:, 32:33]
        largest = jnp.maximum(largest, before)
    offset = largest * LOG2_SCALE
    total = None
    for s, value, turn in zip(scores, values, flipped):
        weights = jnp.exp2(s * LOG2_SCALE - offset).astype(BF16)
        dims = (((1,), (1,)), ((), ())) if turn else (((1,), (0,)), ((), ()))
        term = lax.dot_general(weights, value, dims, preferred_element_type=F32)
        total = term if total is None else total + term
    if state is not None:
        total = total + state * jnp.exp2(before * LOG2_SCALE - offset)
    return jnp.where((lane >= 32) & (lane < HEAD_DIM), largest, total)


def split_block(ref, head):
    sources, _, rows, lanes = ref.shape
    block = ref[:, head].reshape(sources * rows, lanes)
    ones = jnp.ones_like(block)
    return block, jnp.where(lane_index(block.shape) < HEAD_DIM, ones, block)


def scores_of(q, block):
    return lax.dot_general(q, block, (((1,), (1,)), ((), ())), preferred_element_type=F32)


def first_kernel(heads, cut, place_ref, q_ref, block_ref, text_ref, state_ref):
    rows = 2 * q_ref.shape[2]
    for head in range(heads):
        q = q_ref[head].reshape(rows, LANES)
        block, values = split_block(block_ref, head)
        state = update(None, [scores_of(q, block)], [values], [False])
        state_ref[head] = state.reshape(state_ref.shape[1:])

    def with_text(low, high, width):
        for head in range(heads):
            q = q_ref[head].reshape(rows, LANES)
            state = state_ref[head].reshape(rows, LANES)
            features = slice(head * HEAD_DIM, (head + 1) * HEAD_DIM)
            keys = text_ref[0, features, low:high]
            values = text_ref[1, features, low:high]
            if width > high - low:
                pad = jnp.zeros((HEAD_DIM, width - (high - low)), BF16)
                keys = jnp.concatenate([keys, pad], axis=1)
                values = jnp.concatenate([values, pad], axis=1)
            stacked = jnp.concatenate([keys, values], axis=0)
            counted = jnp.concatenate([jnp.ones_like(keys), values], axis=0)
            scores = lax.dot_general(q, stacked, (((1,), (0,)), ((), ())), preferred_element_type=F32)
            scores = jnp.where(lane_index(scores.shape) < high - low, scores, -jnp.inf)
            state = update(state, [scores], [counted], [True])
            state_ref[head] = state.reshape(state_ref.shape[1:])

    count = text_ref.shape[2]

    @pl.when(place_ref[0] == 0)
    def _():
        with_text(0, cut, cut)

    @pl.when(place_ref[0] == 1)
    def _():
        with_text(cut, count, -(-(count - cut) // LANES) * LANES)


def next_kernel(heads, count, q_ref, state_ref, *refs):
    blocks, out_ref = refs[:count], refs[count]
    rows = 2 * q_ref.shape[2]
    for head in range(heads):
        q = q_ref[head].reshape(rows, LANES)
        pairs = [split_block(ref, head) for ref in blocks]
        scores = [scores_of(q, block) for block, _ in pairs]
        state = state_ref[head].reshape(rows, LANES)
        state = update(state, scores, [values for _, values in pairs], [False] * count)
        out_ref[head] = state.reshape(out_ref.shape[1:])


def last_kernel(heads, q_ref, state_ref, block_ref, out_ref):
    tile = q_ref.shape[2]
    rows = 2 * tile
    lane = lane_index((rows, LANES))
    done = []
    marks = jnp.zeros((rows, LANES), F32)
    for head in range(heads):
        q = q_ref[head].reshape(rows, LANES)
        block, values = split_block(block_ref, head)
        state = state_ref[head].reshape(rows, LANES)
        state = update(state, [scores_of(q, block)], [values], [False])
        total = state[:, 0:1]
        level = state[:, 32:33] * LOG2_SCALE + jnp.log2(total)
        coarse = level.astype(BF16).astype(F32)
        middle = (level - coarse).astype(BF16).astype(F32)
        fine = level - coarse - middle
        for place, part in enumerate((coarse, middle, fine)):
            marks = jnp.where(lane == HEAD_DIM + 3 * head + place, part, marks)
        done.append(state / total)
    low = lane < HEAD_DIM
    left = jnp.where(low, pltpu.roll(done[0], HEAD_DIM, 1), done[1]).astype(BF16)
    right = jnp.where(low, pltpu.roll(done[2], HEAD_DIM, 1), marks).astype(BF16)
    for half in range(2):
        part = slice(half * tile, (half + 1) * tile)
        out_ref[:, 2 * half * LANES : (2 * half + 1) * LANES] = left[part]
        out_ref[:, (2 * half + 1) * LANES : (2 * half + 2) * LANES] = right[part]


def attention_call(kernel, name, q, state, blocks, out, place=None, text=None):
    heads, _, rows, _ = q.shape
    tile = ROW_TILE if rows % ROW_TILE == 0 else rows
    row_spec = pl.BlockSpec((heads, 2, tile, LANES), lambda i: (0, 0, i, 0))
    whole = lambda x: pl.BlockSpec(x.shape, lambda i: (0,) * x.ndim)
    operands, specs = [], []
    if place is not None:
        operands.append(place)
        specs.append(pl.BlockSpec(memory_space=pltpu.SMEM))
    operands.append(q)
    specs.append(row_spec)
    if state is not None:
        operands.append(state)
        specs.append(row_spec)
    for block in blocks:
        operands.append(block)
        specs.append(whole(block))
    if text is not None:
        operands.append(text)
        specs.append(whole(text))
    keys = sum(b.shape[0] * b.shape[2] for b in blocks)
    pairs = heads * 2 * rows * keys
    if out == "state":
        shape = jax.ShapeDtypeStruct(q.shape, F32)
        out_spec = row_spec
    else:
        shape = jax.ShapeDtypeStruct((rows, 4 * LANES), BF16)
        out_spec = pl.BlockSpec((tile, 4 * LANES), lambda i: (i, 0))
    return pl.pallas_call(
        kernel,
        grid=(rows // tile,),
        out_shape=shape,
        in_specs=specs,
        out_specs=out_spec,
        compiler_params=params(),
        cost_estimate=pl.CostEstimate(
            flops=pairs * 4 * LANES * 2, bytes_accessed=2 * q.size * 4, transcendentals=pairs
        ),
        name=name,
    )(*operands)


def finish_kernel(
    heads, groups, partial_ref, weight_ref, hidden_ref, modulation_ref, bias_ref, final_ref, final_bias_ref, out_ref, wide_ref
):
    half = partial_ref.shape[1]
    sources = partial_ref.shape[0]
    across = groups // 2
    copies = sources // groups
    width = heads * HEAD_DIM
    low = lane_index((half, LANES)) < HEAD_DIM
    for part in range(2):
        at = part * 2 * LANES
        for group in range(groups):
            zl, y = divmod(group, across)
            members = [(zl * copies + copy) * across + y for copy in range(copies)]
            left = [partial_ref[m, :, at : at + LANES].astype(F32) for m in members]
            right = [partial_ref[m, :, at + LANES : at + 2 * LANES].astype(F32) for m in members]
            levels = [r + pltpu.roll(r, LANES - 1, 1) + pltpu.roll(r, LANES - 2, 1) for r in right]
            top = functools.reduce(jnp.maximum, levels)
            shares = [jnp.exp2(level - top) for level in levels]
            total = functools.reduce(jnp.add, shares)
            first, second = 0.0, 0.0
            for copy in range(copies):
                share = shares[copy] / total
                h0, h1, h2 = [share[:, HEAD_DIM + 3 * h : HEAD_DIM + 3 * h + 1] for h in range(3)]
                first = first + left[copy] * jnp.where(low, h0, h1)
                second = second + right[copy] * h2
            both = jnp.concatenate([first, second[:, :HEAD_DIM]], axis=1)
            wide_ref[part * half : (part + 1) * half, group * width : (group + 1) * width] = both
    attended = wide_ref[...].astype(BF16)
    weights = weight_ref.shape[0]
    projected = jnp.concatenate(
        [jnp.dot(attended, weight_ref[w], preferred_element_type=F32) for w in range(weights)], axis=1
    )
    residual = hidden_ref[...].astype(F32) + modulation_ref[0:1] * (projected + bias_ref[...])
    middle = jnp.mean(residual, axis=-1, keepdims=True)
    centered = residual - middle
    spread = jnp.mean(centered * centered, axis=-1, keepdims=True)
    normed = centered * lax.rsqrt(spread + 1e-06) * (1.0 + modulation_ref[1:2]) + modulation_ref[2:3]
    velocity = lax.dot_general(
        normed.astype(BF16), final_ref[...], (((1,), (1,)), ((), ())), preferred_element_type=F32
    )
    out_ref[...] = velocity + final_bias_ref[...]


def finish(partial, weight, hidden, modulation, bias, final_weight, final_bias, heads, groups):
    tokens, width = hidden.shape
    return pl.pallas_call(
        functools.partial(finish_kernel, heads, groups),
        out_shape=jax.ShapeDtypeStruct((tokens, final_weight.shape[0]), F32),
        scratch_shapes=[pltpu.VMEM((tokens, width), F32)],
        compiler_params=params(),
        name="project_and_norm",
    )(partial, weight, hidden, modulation, bias, final_weight, final_bias)


def local(
    latent_qkv,
    text_kv,
    hidden_in,
    modulation,
    out_weight,
    out_bias,
    proj_weight,
    proj_bias,
    guidance,
    sigma,
    sample,
):
    groups = lax.axis_size("zl") * lax.axis_size("y")
    ring = lax.axis_size("zh")
    tokens = latent_qkv.shape[1]
    half = tokens // 2
    width = latent_qkv.shape[3] // groups
    heads = width // HEAD_DIM
    zl, core, xh = (lax.axis_index(a) for a in ("zl", "core", "xh"))

    columns = out_weight.shape[1] // 2
    own_columns = lax.dynamic_slice_in_dim(out_weight, core * columns, columns, 1)
    weight = lax.all_gather(own_columns, ("core", "xh", "y"), axis=0, tiled=True)
    weight = weight.reshape(2, groups * width, columns)

    slabs = pack(latent_qkv[0].transpose(1, 0, 2), groups, heads)
    slabs = lax.all_to_all(slabs, HEAD_AXES, split_axis=0, concat_axis=0, tiled=True)
    own = slabs[:, heads * half :].reshape(groups, heads, tokens, LANES)
    up = [(i, (i + 1) % ring) for i in range(ring)]
    down = [(i, (i - 1) % ring) for i in range(ring)]
    right, left = lax.ppermute(own, "zh", up), lax.ppermute(own, "zh", down)

    packed = slabs[:, : heads * half].reshape(groups, heads, half, LANES)
    packed = lax.all_gather(packed, "core", axis=0)
    opposite = lax.ppermute(packed, "xh", [(0, 1), (1, 0)])
    q = unpack_queries(xh.reshape(1), packed, opposite)

    count = text_kv.shape[1]
    cut = min(2 * LANES, count)
    has_text = jnp.where(xh == zl, core, 2).reshape(1)
    text = text_kv[0].transpose(1, 2, 0)
    state = attention_call(
        functools.partial(first_kernel, heads, cut), "own_block", q, None, [own], "state", has_text, text
    )
    for _ in range(ring // 2 - 2):
        further_right = lax.ppermute(right, "zh", up)
        further_left = lax.ppermute(left, "zh", down)
        state = attention_call(
            functools.partial(next_kernel, heads, 2), "two_blocks", q, state, [right, left], "state"
        )
        right, left = further_right, further_left
    route = []
    for i in range(ring):
        route += [(2 * i, 2 * ((i + 1) % ring)), (2 * i + 1, 2 * ((i - 1) % ring) + 1)]
    farthest = lax.ppermute(jnp.where(core == 0, right, left), ("zh", "core"), route)
    state = attention_call(
        functools.partial(next_kernel, heads, 2), "two_blocks", q, state, [right, left], "state"
    )
    partial = attention_call(functools.partial(last_kernel, heads), "last_block", q, state, [farthest], "partial")
    partial = partial.reshape(4 * groups, half, 4 * LANES)
    partial = lax.all_to_all(partial, BLOCK_AXES, split_axis=0, concat_axis=0, tiled=True)

    velocity = finish(
        partial,
        weight,
        hidden_in[0],
        modulation[0],
        out_bias[None],
        proj_weight.T,
        proj_bias[None],
        heads,
        groups,
    )

    tiles = velocity.reshape(tokens, 2, -1).transpose(1, 0, 2).reshape(2, -1)
    branch, parity = lax.axis_index("cfg"), lax.axis_index("y") % 2
    across = lax.axis_size("y")
    same, swap = [], []
    for s in range(2):
        for y in range(across):
            a = y % 2
            same.append((s * across + y, a * across + y - a + s))
            swap.append((s * across + y, a * across + y - a + 1 - s))
    kept = lax.ppermute(lax.dynamic_index_in_dim(tiles, branch, 0, keepdims=False), ("cfg", "y"), same)
    crossed = lax.ppermute(lax.dynamic_index_in_dim(tiles, 1 - branch, 0, keepdims=False), ("cfg", "y"), swap)
    conditional = jnp.where(parity == 0, kept, crossed)
    unconditional = jnp.where(parity == 0, crossed, kept)
    guided = unconditional + guidance[0] * (conditional - unconditional)
    result = guided.reshape(1, guided.shape[0])
    denoised = sample - sigma[0] * result
    return (result, denoised)


def solution(mesh):
    sizes = dict(zip(mesh.axis_names, mesh.devices.shape))
    ring = sizes["blk"] // 4
    fine = Mesh(
        mesh.devices.reshape(sizes["cfg"], ring, 2, 2, 2, sizes["uly"] // 2),
        ("cfg", "zh", "zl", "core", "xh", "y"),
    )
    rows = ("zh", "zl", "core", "xh", "y")
    heads = ("xh", "y")
    return jax.shard_map(
        local,
        mesh=fine,
        in_specs=(
            P("cfg", rows, None, None),
            P("cfg", None, None, heads),
            P("cfg", rows, None),
            P("cfg", None, None),
            P(heads, None),
            P(),
            P(),
            P(),
            P(),
            P(),
            P(rows, "cfg"),
        ),
        out_specs=(P(rows, "cfg"), P(rows, "cfg")),
        check_vma=False,
    )
```

```python
import functools
import math

import jax
import jax.numpy as jnp
from jax import lax
from jax.experimental import pallas as pl
from jax.experimental.pallas import tpu as pltpu
from jax.sharding import Mesh, PartitionSpec as P

HEAD_DIM = 64
LANES = 128
ROW_TILE = 256
LOG2_SCALE = math.log2(math.e) * HEAD_DIM**-0.5
F32 = jnp.float32
BF16 = jnp.bfloat16
GUARD = HEAD_DIM + 3
MARKS = 8
SAFE = 2.0**100
HEAD_AXES = ("zl", "y")
BLOCK_AXES = ("zl", "core", "xh", "y")


def params(**extra):
    return pltpu.CompilerParams(vmem_limit_bytes=32 * 1024 * 1024, **extra)


def lane_index(shape):
    return lax.broadcasted_iota(jnp.int32, shape, len(shape) - 1)


def pack_kernel(groups, heads, x_ref, out_ref):
    rows = x_ref.shape[1]
    half = rows // 2
    for group in range(groups):
        queries, pairs = [], []
        for head in range(heads):
            start = (group * heads + head) * HEAD_DIM
            cols = slice(start, start + HEAD_DIM)
            q = x_ref[0, :, cols].astype(F32)
            k = x_ref[1, :, cols].astype(F32)
            v = x_ref[2, :, cols].astype(F32)
            queries.append(jnp.concatenate([q[:half], q[half:]], axis=1))
            pairs.append(jnp.concatenate([k, v], axis=1))
        out_ref[group] = jnp.concatenate(queries + pairs, axis=0).astype(BF16)


def pack(x, groups, heads):
    rows = x.shape[1]
    return pl.pallas_call(
        functools.partial(pack_kernel, groups, heads),
        out_shape=jax.ShapeDtypeStruct((groups, heads * (rows // 2 + rows), LANES), BF16),
        compiler_params=params(),
        name="pack_heads",
    )(x)


def wide_keys(block, valid=None):
    lane = lane_index(block.shape)
    ones = jnp.ones_like(block)
    marked = jnp.where(lane < HEAD_DIM, block, ones)
    if valid is not None:
        row = lax.broadcasted_iota(jnp.int32, block.shape, 0)
        marked = jnp.where((lane == GUARD) & (row >= valid), jnp.full_like(block, -1e30), marked)
    return jnp.concatenate([block, marked], axis=1), jnp.where(lane < HEAD_DIM, ones, block)


def queries_kernel(heads, place_ref, own_ref, other_ref, out_ref, wide_ref):
    here = place_ref[0]
    cores, sources, _, half, _ = own_ref.shape
    across = sources // 2
    lane = lane_index((half, LANES))
    low = lane < HEAD_DIM
    guard = jnp.where(lane == GUARD, 1.0, 0.0)
    for side, ref in ((here, own_ref), (1 - here, other_ref)):
        for core in range(cores):
            for source in range(sources):
                zl, y = divmod(source, across)
                first = (zl * cores + core) * 2 * across + y
                row = pl.multiple_of((first + side * across) * half, 8)
                for head in range(heads):
                    both = ref[core, source, head].astype(F32) * LOG2_SCALE
                    for part, value in enumerate((both, pltpu.roll(both, HEAD_DIM, 1))):
                        lead = value.astype(BF16).astype(F32)
                        wide_ref[head, part, pl.ds(row, half), 0:LANES] = jnp.where(low, lead, 0.0)
                        wide_ref[head, part, pl.ds(row, half), LANES:] = jnp.where(low, value - lead, guard)
    out_ref[...] = wide_ref[...].astype(BF16)


def unpack_queries(place, own, other):
    cores, sources, heads, half, _ = own.shape
    shape = (heads, 2, 2 * cores * sources * half, 2 * LANES)
    return pl.pallas_call(
        functools.partial(queries_kernel, heads),
        out_shape=jax.ShapeDtypeStruct(shape, BF16),
        in_specs=[
            pl.BlockSpec(memory_space=pltpu.SMEM),
            pl.BlockSpec(memory_space=pltpu.VMEM),
            pl.BlockSpec(memory_space=pltpu.VMEM),
        ],
        out_specs=pl.BlockSpec(memory_space=pltpu.VMEM),
        scratch_shapes=[pltpu.VMEM(shape, F32)],
        compiler_params=params(),
        name="unpack_queries",
    )(place, own, other)


def rows_of(ref, head):
    sources, _, rows, lanes = ref.shape
    return ref[:, head].reshape(sources * rows, lanes)


def scores_of(q, keys):
    return lax.dot_general(q, keys, (((1,), (1,)), ((), ())), preferred_element_type=F32)


def weighted(scores, values):
    return jnp.dot(jnp.exp2(scores).astype(BF16), values, preferred_element_type=F32)


def first_kernel(heads, valid_ref, q_ref, block_ref, text_ref, full_ref, state_ref):
    rows = 2 * q_ref.shape[2]
    lane = lane_index((rows, LANES))
    for head in range(heads):
        q = q_ref[head].reshape(rows, 2 * LANES)
        keys, values = wide_keys(rows_of(block_ref, head))
        more_keys, more_values = wide_keys(text_ref[head], valid_ref[0])
        scores = scores_of(q, jnp.concatenate([keys, more_keys], axis=0))
        offset = jnp.max(scores, axis=1, keepdims=True)
        state = weighted(scores - offset, jnp.concatenate([values, more_values], axis=0))
        state_ref[head] = state.reshape(state_ref.shape[1:])
        offset = jnp.broadcast_to(-offset, (rows, LANES))
        coarse = offset.astype(BF16).astype(F32)
        middle = (offset - coarse).astype(BF16).astype(F32)
        upper = q[:, LANES:].astype(F32)
        for place, term in enumerate((coarse, middle, offset - coarse - middle)):
            upper = jnp.where(lane == HEAD_DIM + place, term, upper)
        full_ref[head, :, :, :LANES] = q_ref[head, :, :, :LANES]
        full_ref[head, :, :, LANES:] = upper.astype(BF16).reshape(state_ref.shape[1:])


def next_kernel(heads, count, q_ref, state_ref, *refs):
    blocks, out_ref = refs[:count], refs[count]
    rows = 2 * q_ref.shape[2]
    for head in range(heads):
        q = q_ref[head].reshape(rows, 2 * LANES)
        keys, values = wide_keys(jnp.concatenate([rows_of(ref, head) for ref in blocks], axis=0))
        state = weighted(scores_of(q, keys), values)
        out_ref[head] = state_ref[head] + state.reshape(out_ref.shape[1:])


def last_kernel(heads, count, valid_ref, q_ref, state_ref, block_ref, text_ref, *refs):
    kept, out_ref, done_ref, top_ref, spare_ref, sem = refs[:count], *refs[count:]
    tile = q_ref.shape[2]
    rows = 2 * tile
    lane = lane_index((rows, LANES))
    safe = True
    for head in range(heads):
        q = q_ref[head].reshape(rows, 2 * LANES)
        keys, values = wide_keys(rows_of(block_ref, head))
        state = weighted(scores_of(q, keys), values) + state_ref[head].reshape(rows, LANES)
        done_ref[head] = state
        top_ref[head] = q[:, LANES:].astype(F32)
        largest = jnp.max(jnp.where(state[:, :HEAD_DIM] < SAFE, 0.0, 1.0))
        safe = jnp.logical_and(safe, largest == 0.0)

    @pl.when(jnp.logical_not(safe))
    def _():
        for at, ref in enumerate(kept):
            copy = pltpu.make_async_copy(ref, spare_ref.at[at], sem)
            copy.start()
            copy.wait()
        spare_ref[count] = block_ref[...]
        for head in range(heads):
            q = q_ref[head].reshape(rows, 2 * LANES)
            spared = (lane >= HEAD_DIM) & (lane < GUARD)
            plain = jnp.concatenate([q[:, :LANES], jnp.where(spared, jnp.zeros_like(q[:, LANES:]), q[:, LANES:])], axis=1)

            def absorb(keys, values, largest, state):
                scores = scores_of(plain, keys)
                higher = jnp.maximum(largest, jnp.max(scores, axis=1, keepdims=True))
                return higher, state * jnp.exp2(largest - higher) + weighted(scores - higher, values)

            def step(at, carry):
                return absorb(*wide_keys(spare_ref[at, :, head].reshape(-1, LANES)), *carry)

            carry = (jnp.full((rows, 1), -1e30, F32), jnp.zeros((rows, LANES), F32))
            carry = lax.fori_loop(0, count + 1, step, carry)
            largest, state = absorb(*wide_keys(text_ref[head], valid_ref[0]), *carry)
            done_ref[head] = state
            offset = jnp.broadcast_to(-largest, (rows, LANES))
            coarse = offset.astype(BF16).astype(F32)
            middle = (offset - coarse).astype(BF16).astype(F32)
            upper = jnp.zeros((rows, LANES), F32)
            for place, term in enumerate((coarse, middle, offset - coarse - middle)):
                upper = jnp.where(lane == HEAD_DIM + place, term, upper)
            top_ref[head] = upper

    marks = jnp.zeros((rows, LANES), F32)
    done = []
    for head in range(heads):
        state = done_ref[head]
        total = pltpu.roll(state, HEAD_DIM, 1)
        done.append(state / total)
        terms = top_ref[head] if head == 0 else pltpu.roll(top_ref[head], MARKS * head, 1)
        place = HEAD_DIM + MARKS * head
        lead = total.astype(BF16).astype(F32)
        marks = jnp.where((lane >= place) & (lane < place + 3), terms, marks)
        marks = jnp.where(lane == place + 3, lead, marks)
        marks = jnp.where(lane == place + 4, total - lead, marks)
    low = lane < HEAD_DIM
    left = jnp.where(low, pltpu.roll(done[0], HEAD_DIM, 1), done[1]).astype(BF16)
    right = jnp.where(low, pltpu.roll(done[2], HEAD_DIM, 1), marks).astype(BF16)
    for half in range(2):
        part = slice(half * tile, (half + 1) * tile)
        out_ref[:, 2 * half * LANES : (2 * half + 1) * LANES] = left[part]
        out_ref[:, (2 * half + 1) * LANES : (2 * half + 2) * LANES] = right[part]


def attention_call(kernel, name, operands, whole, kept, out_shape, out_axes, scratch=()):
    q = operands[-1] if len(operands[-1].shape) == 4 and operands[-1].dtype == BF16 else operands[-2]
    heads, _, rows, _ = q.shape
    tile = ROW_TILE if rows % ROW_TILE == 0 else rows

    def tiled(shape, axis):
        block = tuple(tile if d == axis else n for d, n in enumerate(shape))
        return pl.BlockSpec(block, lambda i: tuple(i if d == axis else 0 for d in range(len(shape))))

    specs = []
    for x in operands:
        specs.append(tiled(x.shape, 2) if x.ndim == 4 else pl.BlockSpec(memory_space=pltpu.SMEM))
    for x in whole:
        specs.append(pl.BlockSpec(x.shape, lambda i, n=x.ndim: (0,) * n))
    specs += [pl.BlockSpec(memory_space=pl.ANY)] * len(kept)
    keys = sum(x.shape[0] * x.shape[2] if x.ndim == 4 else x.shape[1] for x in whole)
    pairs = heads * 2 * rows * keys
    out_specs = [tiled(s.shape, a) for s, a in zip(out_shape, out_axes)]
    return pl.pallas_call(
        kernel,
        grid=(rows // tile,),
        out_shape=out_shape,
        in_specs=specs,
        out_specs=out_specs,
        scratch_shapes=scratch,
        compiler_params=params(),
        cost_estimate=pl.CostEstimate(flops=pairs * 6 * LANES, bytes_accessed=4 * q.size, transcendentals=pairs),
        name=name,
    )(*operands, *whole, *kept)


def state_shape(q):
    return jax.ShapeDtypeStruct(q.shape[:3] + (LANES,), F32)


def first_block(valid, q, block, text):
    shapes = [jax.ShapeDtypeStruct(q.shape, BF16), state_shape(q)]
    kernel = functools.partial(first_kernel, q.shape[0])
    return attention_call(kernel, "own_block", [valid, q], [block, text], [], shapes, [2, 2])


def next_blocks(q, state, blocks):
    kernel = functools.partial(next_kernel, q.shape[0], len(blocks))
    return attention_call(kernel, "next_blocks", [q, state], blocks, [], [state_shape(q)], [2])[0]


def last_block(valid, q, state, block, text, kept):
    heads, _, rows, _ = q.shape
    tile = ROW_TILE if rows % ROW_TILE == 0 else rows
    kernel = functools.partial(last_kernel, heads, len(kept))
    shape = jax.ShapeDtypeStruct((rows, 4 * LANES), BF16)
    scratch = [
        pltpu.VMEM((heads, 2 * tile, LANES), F32),
        pltpu.VMEM((heads, 2 * tile, LANES), F32),
        pltpu.VMEM((len(kept) + 1,) + block.shape, BF16),
        pltpu.SemaphoreType.DMA,
    ]
    return attention_call(kernel, "last_block", [valid, q, state], [block, text], kept, [shape], [0], scratch)[0]


def finish_kernel(
    heads, groups, partial_ref, weight_ref, hidden_ref, modulation_ref, bias_ref, final_ref, final_bias_ref, out_ref, wide_ref
):
    half = partial_ref.shape[1]
    sources = partial_ref.shape[0]
    across = groups // 2
    copies = sources // groups
    width = heads * HEAD_DIM
    low = lane_index((half, LANES)) < HEAD_DIM
    for part in range(2):
        at = part * 2 * LANES
        for group in range(groups):
            zl, y = divmod(group, across)
            members = [(zl * copies + copy) * across + y for copy in range(copies)]
            left = [partial_ref[m, :, at : at + LANES].astype(F32) for m in members]
            right = [partial_ref[m, :, at + LANES : at + 2 * LANES].astype(F32) for m in members]
            levels = [-(r + pltpu.roll(r, LANES - 1, 1) + pltpu.roll(r, LANES - 2, 1)) for r in right]
            counts = [pltpu.roll(r, LANES - 3, 1) + pltpu.roll(r, LANES - 4, 1) for r in right]
            top = functools.reduce(jnp.maximum, levels)
            shares = [count * jnp.exp2(level - top) for count, level in zip(counts, levels)]
            total = functools.reduce(jnp.add, shares)
            first, second = 0.0, 0.0
            for copy in range(copies):
                share = shares[copy] / total
                h0, h1, h2 = [share[:, c : c + 1] for c in (HEAD_DIM, HEAD_DIM + MARKS, HEAD_DIM + 2 * MARKS)]
                first = first + left[copy] * jnp.where(low, h0, h1)
                second = second + right[copy] * h2
            both = jnp.concatenate([first, second[:, :HEAD_DIM]], axis=1)
            wide_ref[part * half : (part + 1) * half, group * width : (group + 1) * width] = both
    attended = wide_ref[...].astype(BF16)
    weights = weight_ref.shape[0]
    projected = jnp.concatenate(
        [jnp.dot(attended, weight_ref[w], preferred_element_type=F32) for w in range(weights)], axis=1
    )
    residual = hidden_ref[...].astype(F32) + modulation_ref[0:1] * (projected + bias_ref[...])
    middle = jnp.mean(residual, axis=-1, keepdims=True)
    centered = residual - middle
    spread = jnp.mean(centered * centered, axis=-1, keepdims=True)
    normed = centered * lax.rsqrt(spread + 1e-06) * (1.0 + modulation_ref[1:2]) + modulation_ref[2:3]
    velocity = lax.dot_general(
        normed.astype(BF16), final_ref[...], (((1,), (1,)), ((), ())), preferred_element_type=F32
    )
    out_ref[...] = velocity + final_bias_ref[...]


def finish(partial, weight, hidden, modulation, bias, final_weight, final_bias, heads, groups):
    tokens, width = hidden.shape
    return pl.pallas_call(
        functools.partial(finish_kernel, heads, groups),
        out_shape=jax.ShapeDtypeStruct((tokens, final_weight.shape[0]), F32),
        scratch_shapes=[pltpu.VMEM((tokens, width), F32)],
        compiler_params=params(),
        name="project_and_norm",
    )(partial, weight, hidden, modulation, bias, final_weight, final_bias)


def local(
    latent_qkv,
    text_kv,
    hidden_in,
    modulation,
    out_weight,
    out_bias,
    proj_weight,
    proj_bias,
    guidance,
    sigma,
    sample,
):
    groups = lax.axis_size("zl") * lax.axis_size("y")
    ring = lax.axis_size("zh")
    tokens = latent_qkv.shape[1]
    half = tokens // 2
    width = latent_qkv.shape[3] // groups
    heads = width // HEAD_DIM
    zl, core, xh = (lax.axis_index(a) for a in ("zl", "core", "xh"))

    columns = out_weight.shape[1] // 2
    own_columns = lax.dynamic_slice_in_dim(out_weight, core * columns, columns, 1)
    weight = lax.all_gather(own_columns, ("core", "xh", "y"), axis=0, tiled=True)
    weight = weight.reshape(2, groups * width, columns)

    slabs = pack(latent_qkv[0].transpose(1, 0, 2), groups, heads)
    slabs = lax.all_to_all(slabs, HEAD_AXES, split_axis=0, concat_axis=0, tiled=True)
    own = slabs[:, heads * half :].reshape(groups, heads, tokens, LANES)
    up = [(i, (i + 1) % ring) for i in range(ring)]
    down = [(i, (i - 1) % ring) for i in range(ring)]
    right, left = lax.ppermute(own, "zh", up), lax.ppermute(own, "zh", down)

    packed = slabs[:, : heads * half].reshape(groups, heads, half, LANES)
    packed = lax.all_gather(packed, "core", axis=0)
    opposite = lax.ppermute(packed, "xh", [(0, 1), (1, 0)])
    q = unpack_queries(xh.reshape(1), packed, opposite)

    count = text_kv.shape[1]
    share = -(-count // 32) * 16
    text = text_kv[0].reshape(count, 2, heads, HEAD_DIM).transpose(2, 0, 1, 3).reshape(heads, count, LANES)
    text = jnp.pad(text, ((0, 0), (0, 2 * share - count), (0, 0)))
    text = lax.dynamic_slice_in_dim(text, core * share, share, 1)
    valid = jnp.where(xh == zl, jnp.minimum(count - core * share, share), 0).reshape(1)
    q, state = first_block(valid, q, own, text)
    kept = [own]
    for _ in range(ring // 2 - 2):
        further_right = lax.ppermute(right, "zh", up)
        further_left = lax.ppermute(left, "zh", down)
        state = next_blocks(q, state, [right, left])
        kept += [right, left]
        right, left = further_right, further_left
    kept += [right, left]
    route = []
    for i in range(ring):
        route += [(2 * i, 2 * ((i + 1) % ring)), (2 * i + 1, 2 * ((i - 1) % ring) + 1)]
    farthest = lax.ppermute(jnp.where(core == 0, right, left), ("zh", "core"), route)
    state = next_blocks(q, state, [right, left])
    partial = last_block(valid, q, state, farthest, text, kept)
    partial = partial.reshape(4 * groups, half, 4 * LANES)
    partial = lax.all_to_all(partial, BLOCK_AXES, split_axis=0, concat_axis=0, tiled=True)

    velocity = finish(
        partial,
        weight,
        hidden_in[0],
        modulation[0],
        out_bias[None],
        proj_weight.T,
        proj_bias[None],
        heads,
        groups,
    )

    tiles = velocity.reshape(tokens, 2, -1).transpose(1, 0, 2).reshape(2, -1)
    branch, parity = lax.axis_index("cfg"), lax.axis_index("y") % 2
    across = lax.axis_size("y")
    same, swap = [], []
    for s in range(2):
        for y in range(across):
            a = y % 2
            same.append((s * across + y, a * across + y - a + s))
            swap.append((s * across + y, a * across + y - a + 1 - s))
    kept = lax.ppermute(lax.dynamic_index_in_dim(tiles, branch, 0, keepdims=False), ("cfg", "y"), same)
    crossed = lax.ppermute(lax.dynamic_index_in_dim(tiles, 1 - branch, 0, keepdims=False), ("cfg", "y"), swap)
    conditional = jnp.where(parity == 0, kept, crossed)
    unconditional = jnp.where(parity == 0, crossed, kept)
    guided = unconditional + guidance[0] * (conditional - unconditional)
    result = guided.reshape(1, guided.shape[0])
    denoised = sample - sigma[0] * result
    return (result, denoised)


def solution(mesh):
    sizes = dict(zip(mesh.axis_names, mesh.devices.shape))
    ring = sizes["blk"] // 4
    fine = Mesh(
        mesh.devices.reshape(sizes["cfg"], ring, 2, 2, 2, sizes["uly"] // 2),
        ("cfg", "zh", "zl", "core", "xh", "y"),
    )
    rows = ("zh", "zl", "core", "xh", "y")
    heads = ("xh", "y")
    return jax.shard_map(
        local,
        mesh=fine,
        in_specs=(
            P("cfg", rows, None, None),
            P("cfg", None, None, heads),
            P("cfg", rows, None),
            P("cfg", None, None),
            P(heads, None),
            P(),
            P(),
            P(),
            P(),
            P(),
            P(rows, "cfg"),
        ),
        out_specs=(P(rows, "cfg"), P(rows, "cfg")),
        check_vma=False,
    )
```

```python
import functools
import math

import jax
import jax.numpy as jnp
from jax import lax
from jax.experimental import pallas as pl
from jax.experimental.pallas import tpu as pltpu
from jax.sharding import Mesh, PartitionSpec as P

HEAD_DIM = 64
LANES = 128
ROW_TILE = 256
LOG2_SCALE = math.log2(math.e) * HEAD_DIM**-0.5
F32 = jnp.float32
BF16 = jnp.bfloat16
GUARD = HEAD_DIM + 3
MARKS = 8
SAFE = 2.0**100
HEAD_AXES = ("zl", "y")
BLOCK_AXES = ("zl", "core", "xh", "y")


def params(**extra):
    return pltpu.CompilerParams(vmem_limit_bytes=32 * 1024 * 1024, **extra)


def lane_index(shape):
    return lax.broadcasted_iota(jnp.int32, shape, len(shape) - 1)


def pack_kernel(groups, heads, x_ref, out_ref):
    rows = x_ref.shape[1]
    half = rows // 2
    for group in range(groups):
        queries, pairs = [], []
        for head in range(heads):
            start = (group * heads + head) * HEAD_DIM
            cols = slice(start, start + HEAD_DIM)
            q = x_ref[0, :, cols].astype(F32)
            k = x_ref[1, :, cols].astype(F32)
            v = x_ref[2, :, cols].astype(F32)
            queries.append(jnp.concatenate([q[:half], q[half:]], axis=1))
            pairs.append(jnp.concatenate([k, v], axis=1))
        out_ref[group] = jnp.concatenate(queries + pairs, axis=0).astype(BF16)


def pack(x, groups, heads):
    rows = x.shape[1]
    return pl.pallas_call(
        functools.partial(pack_kernel, groups, heads),
        out_shape=jax.ShapeDtypeStruct((groups, heads * (rows // 2 + rows), LANES), BF16),
        compiler_params=params(),
        name="pack_heads",
    )(x)


def wide_keys(block, valid=None):
    lane = lane_index(block.shape)
    ones = jnp.ones_like(block)
    marked = jnp.where(lane < HEAD_DIM, block, ones)
    if valid is not None:
        row = lax.broadcasted_iota(jnp.int32, block.shape, 0)
        marked = jnp.where((lane == GUARD) & (row >= valid), jnp.full_like(block, -1e30), marked)
    return jnp.concatenate([block, marked], axis=1), jnp.where(lane < HEAD_DIM, ones, block)


def queries_kernel(heads, place_ref, own_ref, other_ref, out_ref, wide_ref):
    here = place_ref[0]
    cores, sources, _, half, _ = own_ref.shape
    across = sources // 2
    lane = lane_index((half, LANES))
    low = lane < HEAD_DIM
    guard = jnp.where(lane == GUARD, 1.0, 0.0)
    for side, ref in ((here, own_ref), (1 - here, other_ref)):
        for core in range(cores):
            for source in range(sources):
                zl, y = divmod(source, across)
                first = (zl * cores + core) * 2 * across + y
                row = pl.multiple_of((first + side * across) * half, 8)
                for head in range(heads):
                    both = ref[core, source, head].astype(F32) * LOG2_SCALE
                    for part, value in enumerate((both, pltpu.roll(both, HEAD_DIM, 1))):
                        lead = value.astype(BF16).astype(F32)
                        wide_ref[head, part, pl.ds(row, half), 0:LANES] = jnp.where(low, lead, 0.0)
                        wide_ref[head, part, pl.ds(row, half), LANES:] = jnp.where(low, value - lead, guard)
    out_ref[...] = wide_ref[...].astype(BF16)


def unpack_queries(place, own, other):
    cores, sources, heads, half, _ = own.shape
    shape = (heads, 2, 2 * cores * sources * half, 2 * LANES)
    return pl.pallas_call(
        functools.partial(queries_kernel, heads),
        out_shape=jax.ShapeDtypeStruct(shape, BF16),
        in_specs=[
            pl.BlockSpec(memory_space=pltpu.SMEM),
            pl.BlockSpec(memory_space=pltpu.VMEM),
            pl.BlockSpec(memory_space=pltpu.VMEM),
        ],
        out_specs=pl.BlockSpec(memory_space=pltpu.VMEM),
        scratch_shapes=[pltpu.VMEM(shape, F32)],
        compiler_params=params(),
        name="unpack_queries",
    )(place, own, other)


def rows_of(ref, head):
    lanes = ref.shape[-1]
    if len(ref.shape) == 4:
        return ref[:, head].reshape(-1, lanes)
    return jnp.concatenate([ref[n, :, head].reshape(-1, lanes) for n in range(ref.shape[0])], axis=0)


def scores_of(q, keys):
    return lax.dot_general(q, keys, (((1,), (1,)), ((), ())), preferred_element_type=F32)


def weighted(scores, values):
    return jnp.dot(jnp.exp2(scores).astype(BF16), values, preferred_element_type=F32)


def first_kernel(heads, valid_ref, q_ref, block_ref, text_ref, full_ref, state_ref):
    rows = 2 * q_ref.shape[2]
    lane = lane_index((rows, LANES))
    for head in range(heads):
        q = q_ref[head].reshape(rows, 2 * LANES)
        keys, values = wide_keys(rows_of(block_ref, head))
        more_keys, more_values = wide_keys(text_ref[head], valid_ref[0])
        scores = scores_of(q, jnp.concatenate([keys, more_keys], axis=0))
        offset = jnp.max(scores, axis=1, keepdims=True)
        state = weighted(scores - offset, jnp.concatenate([values, more_values], axis=0))
        state_ref[head] = state.reshape(state_ref.shape[1:])
        offset = jnp.broadcast_to(-offset, (rows, LANES))
        coarse = offset.astype(BF16).astype(F32)
        middle = (offset - coarse).astype(BF16).astype(F32)
        upper = q[:, LANES:].astype(F32)
        for place, term in enumerate((coarse, middle, offset - coarse - middle)):
            upper = jnp.where(lane == HEAD_DIM + place, term, upper)
        full_ref[head, :, :, :LANES] = q_ref[head, :, :, :LANES]
        full_ref[head, :, :, LANES:] = upper.astype(BF16).reshape(state_ref.shape[1:])


def next_kernel(heads, q_ref, state_ref, blocks_ref, out_ref):
    rows = 2 * q_ref.shape[2]
    for head in range(heads):
        q = q_ref[head].reshape(rows, 2 * LANES)
        keys, values = wide_keys(rows_of(blocks_ref, head))
        state = weighted(scores_of(q, keys), values)
        out_ref[head] = state_ref[head] + state.reshape(out_ref.shape[1:])


def last_kernel(heads, count, valid_ref, q_ref, state_ref, block_ref, text_ref, *refs):
    kept, out_ref, done_ref, top_ref, spare_ref, sem = refs[:count], *refs[count:]
    parts = []
    for ref in kept:
        parts += [ref] if len(ref.shape) == 4 else [ref.at[n] for n in range(ref.shape[0])]
    tile = q_ref.shape[2]
    rows = 2 * tile
    lane = lane_index((rows, LANES))
    safe = True
    for head in range(heads):
        q = q_ref[head].reshape(rows, 2 * LANES)
        keys, values = wide_keys(rows_of(block_ref, head))
        state = weighted(scores_of(q, keys), values) + state_ref[head].reshape(rows, LANES)
        done_ref[head] = state
        top_ref[head] = q[:, LANES:].astype(F32)
        largest = jnp.max(jnp.where(state[:, :HEAD_DIM] < SAFE, 0.0, 1.0))
        safe = jnp.logical_and(safe, largest == 0.0)

    @pl.when(jnp.logical_not(safe))
    def _():
        for at, ref in enumerate(parts):
            copy = pltpu.make_async_copy(ref, spare_ref.at[at], sem)
            copy.start()
            copy.wait()
        spare_ref[len(parts)] = block_ref[...]
        for head in range(heads):
            q = q_ref[head].reshape(rows, 2 * LANES)
            spared = (lane >= HEAD_DIM) & (lane < GUARD)
            plain = jnp.concatenate([q[:, :LANES], jnp.where(spared, jnp.zeros_like(q[:, LANES:]), q[:, LANES:])], axis=1)

            def absorb(keys, values, largest, state):
                scores = scores_of(plain, keys)
                higher = jnp.maximum(largest, jnp.max(scores, axis=1, keepdims=True))
                return higher, state * jnp.exp2(largest - higher) + weighted(scores - higher, values)

            def step(at, carry):
                return absorb(*wide_keys(spare_ref[at, :, head].reshape(-1, LANES)), *carry)

            carry = (jnp.full((rows, 1), -1e30, F32), jnp.zeros((rows, LANES), F32))
            carry = lax.fori_loop(0, len(parts) + 1, step, carry)
            largest, state = absorb(*wide_keys(text_ref[head], valid_ref[0]), *carry)
            done_ref[head] = state
            offset = jnp.broadcast_to(-largest, (rows, LANES))
            coarse = offset.astype(BF16).astype(F32)
            middle = (offset - coarse).astype(BF16).astype(F32)
            upper = jnp.zeros((rows, LANES), F32)
            for place, term in enumerate((coarse, middle, offset - coarse - middle)):
                upper = jnp.where(lane == HEAD_DIM + place, term, upper)
            top_ref[head] = upper

    marks = jnp.zeros((rows, LANES), F32)
    done = []
    for head in range(heads):
        state = done_ref[head]
        total = pltpu.roll(state, HEAD_DIM, 1)
        done.append(state / total)
        terms = top_ref[head] if head == 0 else pltpu.roll(top_ref[head], MARKS * head, 1)
        place = HEAD_DIM + MARKS * head
        lead = total.astype(BF16).astype(F32)
        marks = jnp.where((lane >= place) & (lane < place + 3), terms, marks)
        marks = jnp.where(lane == place + 3, lead, marks)
        marks = jnp.where(lane == place + 4, total - lead, marks)
    low = lane < HEAD_DIM
    left = jnp.where(low, pltpu.roll(done[0], HEAD_DIM, 1), done[1]).astype(BF16)
    right = jnp.where(low, pltpu.roll(done[2], HEAD_DIM, 1), marks).astype(BF16)
    for half in range(2):
        part = slice(half * tile, (half + 1) * tile)
        out_ref[:, 2 * half * LANES : (2 * half + 1) * LANES] = left[part]
        out_ref[:, (2 * half + 1) * LANES : (2 * half + 2) * LANES] = right[part]


def attention_call(kernel, name, operands, whole, kept, out_shape, out_axes, scratch=()):
    q = operands[-1] if len(operands[-1].shape) == 4 and operands[-1].dtype == BF16 else operands[-2]
    heads, _, rows, _ = q.shape
    tile = ROW_TILE if rows % ROW_TILE == 0 else rows

    def tiled(shape, axis):
        block = tuple(tile if d == axis else n for d, n in enumerate(shape))
        return pl.BlockSpec(block, lambda i: tuple(i if d == axis else 0 for d in range(len(shape))))

    specs = []
    for x in operands:
        specs.append(tiled(x.shape, 2) if x.ndim == 4 else pl.BlockSpec(memory_space=pltpu.SMEM))
    for x in whole:
        specs.append(pl.BlockSpec(x.shape, lambda i, n=x.ndim: (0,) * n))
    specs += [pl.BlockSpec(memory_space=pl.ANY)] * len(kept)
    keys = sum(x.size // (heads * LANES) for x in whole)
    pairs = heads * 2 * rows * keys
    out_specs = [tiled(s.shape, a) for s, a in zip(out_shape, out_axes)]
    return pl.pallas_call(
        kernel,
        grid=(rows // tile,),
        out_shape=out_shape,
        in_specs=specs,
        out_specs=out_specs,
        scratch_shapes=scratch,
        compiler_params=params(),
        cost_estimate=pl.CostEstimate(flops=pairs * 6 * LANES, bytes_accessed=4 * q.size, transcendentals=pairs),
        name=name,
    )(*operands, *whole, *kept)


def state_shape(q):
    return jax.ShapeDtypeStruct(q.shape[:3] + (LANES,), F32)


def first_block(valid, q, block, text):
    shapes = [jax.ShapeDtypeStruct(q.shape, BF16), state_shape(q)]
    kernel = functools.partial(first_kernel, q.shape[0])
    return attention_call(kernel, "own_block", [valid, q], [block, text], [], shapes, [2, 2])


def next_blocks(q, state, blocks):
    kernel = functools.partial(next_kernel, q.shape[0])
    return attention_call(kernel, "next_blocks", [q, state], [blocks], [], [state_shape(q)], [2])[0]


def last_block(valid, q, state, block, text, kept):
    heads, _, rows, _ = q.shape
    tile = ROW_TILE if rows % ROW_TILE == 0 else rows
    kernel = functools.partial(last_kernel, heads, len(kept))
    shape = jax.ShapeDtypeStruct((rows, 4 * LANES), BF16)
    scratch = [
        pltpu.VMEM((heads, 2 * tile, LANES), F32),
        pltpu.VMEM((heads, 2 * tile, LANES), F32),
        pltpu.VMEM((2 * len(kept),) + block.shape, BF16),
        pltpu.SemaphoreType.DMA,
    ]
    return attention_call(kernel, "last_block", [valid, q, state], [block, text], kept, [shape], [0], scratch)[0]


def finish_kernel(
    heads,
    groups,
    place_ref,
    partial_ref,
    own_weight_ref,
    other_weight_ref,
    hidden_ref,
    modulation_ref,
    bias_ref,
    final_ref,
    final_bias_ref,
    out_ref,
    wide_ref,
    weight_ref,
    sems,
):
    copies_in = [
        pltpu.make_async_copy(ref, weight_ref.at[n], sems.at[n])
        for n, ref in enumerate((own_weight_ref, other_weight_ref))
    ]
    for copy in copies_in:
        copy.start()
    half = partial_ref.shape[1]
    sources = partial_ref.shape[0]
    across = groups // 2
    copies = sources // groups
    width = heads * HEAD_DIM
    low = lane_index((half, LANES)) < HEAD_DIM
    for part in range(2):
        at = part * 2 * LANES
        for group in range(groups):
            zl, y = divmod(group, across)
            members = [(zl * copies + copy) * across + y for copy in range(copies)]
            left = [partial_ref[m, :, at : at + LANES].astype(F32) for m in members]
            right = [partial_ref[m, :, at + LANES : at + 2 * LANES].astype(F32) for m in members]
            levels = [-(r + pltpu.roll(r, LANES - 1, 1) + pltpu.roll(r, LANES - 2, 1)) for r in right]
            counts = [pltpu.roll(r, LANES - 3, 1) + pltpu.roll(r, LANES - 4, 1) for r in right]
            top = functools.reduce(jnp.maximum, levels)
            shares = [count * jnp.exp2(level - top) for count, level in zip(counts, levels)]
            total = functools.reduce(jnp.add, shares)
            first, second = 0.0, 0.0
            for copy in range(copies):
                share = shares[copy] / total
                h0, h1, h2 = [share[:, c : c + 1] for c in (HEAD_DIM, HEAD_DIM + MARKS, HEAD_DIM + 2 * MARKS)]
                first = first + left[copy] * jnp.where(low, h0, h1)
                second = second + right[copy] * h2
            both = jnp.concatenate([first, second[:, :HEAD_DIM]], axis=1)
            wide_ref[part * half : (part + 1) * half, group * width : (group + 1) * width] = both
    core, x, y = place_ref[0], place_ref[1], place_ref[2]
    attended = wide_ref[...].astype(BF16)
    for copy in copies_in:
        copy.wait()
    sides = []
    for side in range(2):
        total = 0.0
        for group in range(groups):
            at_x, at_y = divmod(group, across)
            piece = lax.rem(at_y - y + across, across) * 2 + lax.rem(at_x + x, 2)
            own = attended[:, group * width : (group + 1) * width]
            total = total + jnp.dot(own, weight_ref[side, piece], preferred_element_type=F32)
        sides.append(total)
    first = core == 0
    projected = jnp.concatenate(
        [jnp.where(first, sides[0], sides[1]), jnp.where(first, sides[1], sides[0])], axis=1
    )
    residual = hidden_ref[...].astype(F32) + modulation_ref[0:1] * (projected + bias_ref[...])
    middle = jnp.mean(residual, axis=-1, keepdims=True)
    centered = residual - middle
    spread = jnp.mean(centered * centered, axis=-1, keepdims=True)
    normed = centered * lax.rsqrt(spread + 1e-06) * (1.0 + modulation_ref[1:2]) + modulation_ref[2:3]
    velocity = lax.dot_general(
        normed.astype(BF16), final_ref[...], (((1,), (1,)), ((), ())), preferred_element_type=F32
    )
    out_ref[...] = velocity + final_bias_ref[...]


def finish(place, partial, own_weight, other_weight, hidden, modulation, bias, final_weight, final_bias, heads, groups):
    tokens, width = hidden.shape
    vmem = pl.BlockSpec(memory_space=pltpu.VMEM)
    far = pl.BlockSpec(memory_space=pl.ANY)
    return pl.pallas_call(
        functools.partial(finish_kernel, heads, groups),
        out_shape=jax.ShapeDtypeStruct((tokens, final_weight.shape[0]), F32),
        in_specs=[pl.BlockSpec(memory_space=pltpu.SMEM), vmem, far, far, vmem, vmem, vmem, vmem, vmem],
        out_specs=vmem,
        scratch_shapes=[
            pltpu.VMEM((tokens, width), F32),
            pltpu.VMEM((2,) + own_weight.shape, BF16),
            pltpu.SemaphoreType.DMA((2,)),
        ],
        compiler_params=params(),
        name="project_and_norm",
    )(place, partial, own_weight, other_weight, hidden, modulation, bias, final_weight, final_bias)


def local(
    latent_qkv,
    text_kv,
    hidden_in,
    modulation,
    out_weight,
    out_bias,
    proj_weight,
    proj_bias,
    guidance,
    sigma,
    sample,
):
    groups = lax.axis_size("zl") * lax.axis_size("y")
    ring = lax.axis_size("zh")
    tokens = latent_qkv.shape[1]
    half = tokens // 2
    width = latent_qkv.shape[3] // groups
    heads = width // HEAD_DIM
    across = lax.axis_size("y")
    zl, core, xh, y = (lax.axis_index(a) for a in ("zl", "core", "xh", "y"))
    after = lax.optimization_barrier

    slabs = pack(latent_qkv[0].transpose(1, 0, 2), groups, heads)
    slabs = lax.all_to_all(slabs, HEAD_AXES, split_axis=0, concat_axis=0, tiled=True)
    own = slabs[:, heads * half :].reshape(groups, heads, tokens, LANES)
    route = []
    for i in range(ring):
        route += [(2 * i, 2 * ((i + 1) % ring)), (2 * i + 1, 2 * ((i - 1) % ring) + 1)]
    pass_on = lambda x: lax.ppermute(x, ("zh", "core"), route)
    arrived = pass_on(lax.all_gather(own, "core", axis=0))

    packed = slabs[:, : heads * half].reshape(groups, heads, half, LANES)
    packed = lax.all_gather(packed, "core", axis=0)
    opposite = lax.ppermute(packed, "xh", [(0, 1), (1, 0)])
    q = unpack_queries(xh.reshape(1), packed, opposite)

    columns = out_weight.shape[1] // 2
    piece, _ = after((out_weight, packed))
    piece = lax.dynamic_slice_in_dim(piece, core * columns, columns, 1)
    pair = jnp.stack([piece, lax.ppermute(piece, "xh", [(0, 1), (1, 0)])])

    count = text_kv.shape[1]
    share = -(-count // 32) * 16
    text = text_kv[0].reshape(count, 2, heads, HEAD_DIM).transpose(2, 0, 1, 3).reshape(heads, count, LANES)
    text = jnp.pad(text, ((0, 0), (0, 2 * share - count), (0, 0)))
    text = lax.dynamic_slice_in_dim(text, core * share, share, 1)
    valid = jnp.where(xh == zl, jnp.minimum(count - core * share, share), 0).reshape(1)
    q, state = first_block(valid, q, own, text)
    kept = [own, arrived]
    for _ in range(ring // 2 - 2):
        arrived, state = after((arrived, state))
        further = pass_on(arrived)
        state = next_blocks(q, state, arrived)
        arrived = further
        kept.append(arrived)
    arrived, state = after((arrived, state))
    farthest = pass_on(lax.dynamic_index_in_dim(arrived, core, 0, keepdims=False))
    turn = lambda d: lax.ppermute(pair, "y", [(i, (i - d) % across) for i in range(across)])
    own_weight = jnp.concatenate([pair] + [turn(d) for d in range(1, across)], axis=0)
    other_weight = lax.ppermute(own_weight, "core", [(0, 1), (1, 0)])
    state = next_blocks(q, state, arrived)
    partial = last_block(valid, q, state, farthest, text, kept)
    partial = partial.reshape(4 * groups, half, 4 * LANES)
    partial = lax.all_to_all(partial, BLOCK_AXES, split_axis=0, concat_axis=0, tiled=True)

    velocity = finish(
        jnp.stack([core, xh, y]),
        partial,
        own_weight,
        other_weight,
        hidden_in[0],
        modulation[0],
        out_bias[None],
        proj_weight.T,
        proj_bias[None],
        heads,
        groups,
    )

    tiles = velocity.reshape(tokens, 2, -1).transpose(1, 0, 2).reshape(2, -1)
    branch, parity = lax.axis_index("cfg"), y % 2
    same, swap = [], []
    for s in range(2):
        for y in range(across):
            a = y % 2
            same.append((s * across + y, a * across + y - a + s))
            swap.append((s * across + y, a * across + y - a + 1 - s))
    kept = lax.ppermute(lax.dynamic_index_in_dim(tiles, branch, 0, keepdims=False), ("cfg", "y"), same)
    crossed = lax.ppermute(lax.dynamic_index_in_dim(tiles, 1 - branch, 0, keepdims=False), ("cfg", "y"), swap)
    conditional = jnp.where(parity == 0, kept, crossed)
    unconditional = jnp.where(parity == 0, crossed, kept)
    guided = unconditional + guidance[0] * (conditional - unconditional)
    result = guided.reshape(1, guided.shape[0])
    denoised = sample - sigma[0] * result
    return (result, denoised)


def solution(mesh):
    sizes = dict(zip(mesh.axis_names, mesh.devices.shape))
    ring = sizes["blk"] // 4
    fine = Mesh(
        mesh.devices.reshape(sizes["cfg"], ring, 2, 2, 2, sizes["uly"] // 2),
        ("cfg", "zh", "zl", "core", "xh", "y"),
    )
    rows = ("zh", "zl", "core", "xh", "y")
    heads = ("xh", "y")
    return jax.shard_map(
        local,
        mesh=fine,
        in_specs=(
            P("cfg", rows, None, None),
            P("cfg", None, None, heads),
            P("cfg", rows, None),
            P("cfg", None, None),
            P(heads, None),
            P(),
            P(),
            P(),
            P(),
            P(),
            P(rows, "cfg"),
        ),
        out_specs=(P(rows, "cfg"), P(rows, "cfg")),
        check_vma=False,
    )
```

```python
import functools
import math

import jax
import jax.numpy as jnp
from jax import lax
from jax.experimental import pallas as pl
from jax.experimental.pallas import tpu as pltpu
from jax.sharding import Mesh, PartitionSpec as P

HEAD_DIM = 64
LANES = 128
ROW_TILE = 256
LOG2_SCALE = math.log2(math.e) * HEAD_DIM**-0.5
F32 = jnp.float32
BF16 = jnp.bfloat16
GUARD = HEAD_DIM + 3
MARKS = 8
SAFE = 2.0**100
HEAD_AXES = ("zl", "y")
BLOCK_AXES = ("zl", "core", "xh", "y")


def params(**extra):
    return pltpu.CompilerParams(vmem_limit_bytes=32 * 1024 * 1024, **extra)


def lane_index(shape):
    return lax.broadcasted_iota(jnp.int32, shape, len(shape) - 1)


def pack_kernel(groups, heads, x_ref, out_ref):
    rows = x_ref.shape[1]
    half = rows // 2
    for group in range(groups):
        queries, pairs = [], []
        for head in range(heads):
            start = (group * heads + head) * HEAD_DIM
            cols = slice(start, start + HEAD_DIM)
            q = x_ref[0, :, cols].astype(F32)
            k = x_ref[1, :, cols].astype(F32)
            v = x_ref[2, :, cols].astype(F32)
            queries.append(jnp.concatenate([q[:half], q[half:]], axis=1))
            pairs.append(jnp.concatenate([k, v], axis=1))
        out_ref[group] = jnp.concatenate(queries + pairs, axis=0).astype(BF16)


def pack(x, groups, heads):
    rows = x.shape[1]
    return pl.pallas_call(
        functools.partial(pack_kernel, groups, heads),
        out_shape=jax.ShapeDtypeStruct((groups, heads * (rows // 2 + rows), LANES), BF16),
        compiler_params=params(),
        name="pack_heads",
    )(x)


def wide_keys(block, valid=None):
    lane = lane_index(block.shape)
    ones = jnp.ones_like(block)
    marked = jnp.where(lane < HEAD_DIM, block, ones)
    if valid is not None:
        row = lax.broadcasted_iota(jnp.int32, block.shape, 0)
        marked = jnp.where((lane == GUARD) & (row >= valid), jnp.full_like(block, -1e30), marked)
    return jnp.concatenate([block, marked], axis=1), jnp.where(lane < HEAD_DIM, ones, block)


def queries_kernel(heads, place_ref, own_ref, other_ref, out_ref, wide_ref):
    here = place_ref[0]
    cores, sources, _, half, _ = own_ref.shape
    across = sources // 2
    lane = lane_index((half, LANES))
    low = lane < HEAD_DIM
    guard = jnp.where(lane == GUARD, 1.0, 0.0)
    for side, ref in ((here, own_ref), (1 - here, other_ref)):
        for core in range(cores):
            for source in range(sources):
                zl, y = divmod(source, across)
                first = (zl * cores + core) * 2 * across + y
                row = pl.multiple_of((first + side * across) * half, 8)
                for head in range(heads):
                    both = ref[core, source, head].astype(F32) * LOG2_SCALE
                    for part, value in enumerate((both, pltpu.roll(both, HEAD_DIM, 1))):
                        lead = value.astype(BF16).astype(F32)
                        wide_ref[head, part, pl.ds(row, half), 0:LANES] = jnp.where(low, lead, 0.0)
                        wide_ref[head, part, pl.ds(row, half), LANES:] = jnp.where(low, value - lead, guard)
    out_ref[...] = wide_ref[...].astype(BF16)


def unpack_queries(place, own, other):
    cores, sources, heads, half, _ = own.shape
    shape = (heads, 2, 2 * cores * sources * half, 2 * LANES)
    return pl.pallas_call(
        functools.partial(queries_kernel, heads),
        out_shape=jax.ShapeDtypeStruct(shape, BF16),
        in_specs=[
            pl.BlockSpec(memory_space=pltpu.SMEM),
            pl.BlockSpec(memory_space=pltpu.VMEM),
            pl.BlockSpec(memory_space=pltpu.VMEM),
        ],
        out_specs=pl.BlockSpec(memory_space=pltpu.VMEM),
        scratch_shapes=[pltpu.VMEM(shape, F32)],
        compiler_params=params(),
        name="unpack_queries",
    )(place, own, other)


def rows_of(ref, head):
    lanes = ref.shape[-1]
    if len(ref.shape) == 4:
        return ref[:, head].reshape(-1, lanes)
    return jnp.concatenate([ref[n, :, head].reshape(-1, lanes) for n in range(ref.shape[0])], axis=0)


def scores_of(q, keys):
    return lax.dot_general(q, keys, (((1,), (1,)), ((), ())), preferred_element_type=F32)


def weighted(scores, values):
    return jnp.dot(jnp.exp2(scores).astype(BF16), values, preferred_element_type=F32)


def first_kernel(heads, valid_ref, q_ref, block_ref, text_ref, full_ref, state_ref):
    rows = 2 * q_ref.shape[2]
    lane = lane_index((rows, LANES))
    for head in range(heads):
        q = q_ref[head].reshape(rows, 2 * LANES)
        keys, values = wide_keys(rows_of(block_ref, head))
        more_keys, more_values = wide_keys(text_ref[head], valid_ref[0])
        scores = scores_of(q, jnp.concatenate([keys, more_keys], axis=0))
        offset = jnp.max(scores, axis=1, keepdims=True)
        state = weighted(scores - offset, jnp.concatenate([values, more_values], axis=0))
        state_ref[head] = state.reshape(state_ref.shape[1:])
        offset = jnp.broadcast_to(-offset, (rows, LANES))
        coarse = offset.astype(BF16).astype(F32)
        middle = (offset - coarse).astype(BF16).astype(F32)
        upper = q[:, LANES:].astype(F32)
        for place, term in enumerate((coarse, middle, offset - coarse - middle)):
            upper = jnp.where(lane == HEAD_DIM + place, term, upper)
        full_ref[head, :, :, :LANES] = q_ref[head, :, :, :LANES]
        full_ref[head, :, :, LANES:] = upper.astype(BF16).reshape(state_ref.shape[1:])


def next_kernel(heads, q_ref, state_ref, blocks_ref, out_ref):
    rows = 2 * q_ref.shape[2]
    for head in range(heads):
        q = q_ref[head].reshape(rows, 2 * LANES)
        keys, values = wide_keys(rows_of(blocks_ref, head))
        state = weighted(scores_of(q, keys), values)
        out_ref[head] = state_ref[head] + state.reshape(out_ref.shape[1:])


def last_kernel(heads, count, valid_ref, q_ref, state_ref, block_ref, text_ref, *refs):
    kept, out_ref, done_ref, top_ref, spare_ref, sem = refs[:count], *refs[count:]
    parts = []
    for ref in kept:
        parts += [ref] if len(ref.shape) == 4 else [ref.at[n] for n in range(ref.shape[0])]
    tile = q_ref.shape[2]
    rows = 2 * tile
    lane = lane_index((rows, LANES))
    safe = True
    for head in range(heads):
        q = q_ref[head].reshape(rows, 2 * LANES)
        keys, values = wide_keys(rows_of(block_ref, head))
        state = weighted(scores_of(q, keys), values) + state_ref[head].reshape(rows, LANES)
        done_ref[head] = state
        top_ref[head] = q[:, LANES:].astype(F32)
        largest = jnp.max(jnp.where(state[:, :HEAD_DIM] < SAFE, 0.0, 1.0))
        safe = jnp.logical_and(safe, largest == 0.0)

    @pl.when(jnp.logical_not(safe))
    def _():
        for at, ref in enumerate(parts):
            copy = pltpu.make_async_copy(ref, spare_ref.at[at], sem)
            copy.start()
            copy.wait()
        spare_ref[len(parts)] = block_ref[...]
        for head in range(heads):
            q = q_ref[head].reshape(rows, 2 * LANES)
            spared = (lane >= HEAD_DIM) & (lane < GUARD)
            plain = jnp.concatenate([q[:, :LANES], jnp.where(spared, jnp.zeros_like(q[:, LANES:]), q[:, LANES:])], axis=1)

            def absorb(keys, values, largest, state):
                scores = scores_of(plain, keys)
                higher = jnp.maximum(largest, jnp.max(scores, axis=1, keepdims=True))
                return higher, state * jnp.exp2(largest - higher) + weighted(scores - higher, values)

            def step(at, carry):
                return absorb(*wide_keys(spare_ref[at, :, head].reshape(-1, LANES)), *carry)

            carry = (jnp.full((rows, 1), -1e30, F32), jnp.zeros((rows, LANES), F32))
            carry = lax.fori_loop(0, len(parts) + 1, step, carry)
            largest, state = absorb(*wide_keys(text_ref[head], valid_ref[0]), *carry)
            done_ref[head] = state
            offset = jnp.broadcast_to(-largest, (rows, LANES))
            coarse = offset.astype(BF16).astype(F32)
            middle = (offset - coarse).astype(BF16).astype(F32)
            upper = jnp.zeros((rows, LANES), F32)
            for place, term in enumerate((coarse, middle, offset - coarse - middle)):
                upper = jnp.where(lane == HEAD_DIM + place, term, upper)
            top_ref[head] = upper

    marks = jnp.zeros((rows, LANES), F32)
    done = []
    for head in range(heads):
        state = done_ref[head]
        total = pltpu.roll(state, HEAD_DIM, 1)
        done.append(state / total)
        terms = top_ref[head] if head == 0 else pltpu.roll(top_ref[head], MARKS * head, 1)
        place = HEAD_DIM + MARKS * head
        lead = total.astype(BF16).astype(F32)
        marks = jnp.where((lane >= place) & (lane < place + 3), terms, marks)
        marks = jnp.where(lane == place + 3, lead, marks)
        marks = jnp.where(lane == place + 4, total - lead, marks)
    low = lane < HEAD_DIM
    left = jnp.where(low, pltpu.roll(done[0], HEAD_DIM, 1), done[1]).astype(BF16)
    right = jnp.where(low, pltpu.roll(done[2], HEAD_DIM, 1), marks).astype(BF16)
    for half in range(2):
        part = slice(half * tile, (half + 1) * tile)
        out_ref[:, 2 * half * LANES : (2 * half + 1) * LANES] = left[part]
        out_ref[:, (2 * half + 1) * LANES : (2 * half + 2) * LANES] = right[part]


def attention_call(kernel, name, operands, whole, kept, out_shape, out_axes, scratch=()):
    q = operands[-1] if len(operands[-1].shape) == 4 and operands[-1].dtype == BF16 else operands[-2]
    heads, _, rows, _ = q.shape
    tile = ROW_TILE if rows % ROW_TILE == 0 else rows

    def tiled(shape, axis):
        block = tuple(tile if d == axis else n for d, n in enumerate(shape))
        return pl.BlockSpec(block, lambda i: tuple(i if d == axis else 0 for d in range(len(shape))))

    specs = []
    for x in operands:
        specs.append(tiled(x.shape, 2) if x.ndim == 4 else pl.BlockSpec(memory_space=pltpu.SMEM))
    for x in whole:
        specs.append(pl.BlockSpec(x.shape, lambda i, n=x.ndim: (0,) * n))
    specs += [pl.BlockSpec(memory_space=pl.ANY)] * len(kept)
    keys = sum(x.size // (heads * LANES) for x in whole)
    pairs = heads * 2 * rows * keys
    out_specs = [tiled(s.shape, a) for s, a in zip(out_shape, out_axes)]
    return pl.pallas_call(
        kernel,
        grid=(rows // tile,),
        out_shape=out_shape,
        in_specs=specs,
        out_specs=out_specs,
        scratch_shapes=scratch,
        compiler_params=params(),
        cost_estimate=pl.CostEstimate(flops=pairs * 6 * LANES, bytes_accessed=4 * q.size, transcendentals=pairs),
        name=name,
    )(*operands, *whole, *kept)


def state_shape(q):
    return jax.ShapeDtypeStruct(q.shape[:3] + (LANES,), F32)


def first_block(valid, q, block, text):
    shapes = [jax.ShapeDtypeStruct(q.shape, BF16), state_shape(q)]
    kernel = functools.partial(first_kernel, q.shape[0])
    return attention_call(kernel, "own_block", [valid, q], [block, text], [], shapes, [2, 2])


def next_blocks(q, state, blocks):
    kernel = functools.partial(next_kernel, q.shape[0])
    return attention_call(kernel, "next_blocks", [q, state], [blocks], [], [state_shape(q)], [2])[0]


def last_block(valid, q, state, block, text, kept):
    heads, _, rows, _ = q.shape
    tile = ROW_TILE if rows % ROW_TILE == 0 else rows
    kernel = functools.partial(last_kernel, heads, len(kept))
    shape = jax.ShapeDtypeStruct((rows, 4 * LANES), BF16)
    scratch = [
        pltpu.VMEM((heads, 2 * tile, LANES), F32),
        pltpu.VMEM((heads, 2 * tile, LANES), F32),
        pltpu.VMEM((2 * len(kept),) + block.shape, BF16),
        pltpu.SemaphoreType.DMA,
    ]
    return attention_call(kernel, "last_block", [valid, q, state], [block, text], kept, [shape], [0], scratch)[0]


def finish_kernel(
    heads,
    groups,
    partial_ref,
    weight_ref,
    hidden_ref,
    modulation_ref,
    bias_ref,
    final_ref,
    final_bias_ref,
    out_ref,
    wide_ref,
):
    half = partial_ref.shape[1]
    sources = partial_ref.shape[0]
    across = groups // 2
    copies = sources // groups
    width = heads * HEAD_DIM
    low = lane_index((half, LANES)) < HEAD_DIM
    for part in range(2):
        at = part * 2 * LANES
        for group in range(groups):
            zl, y = divmod(group, across)
            members = [(zl * copies + copy) * across + y for copy in range(copies)]
            left = [partial_ref[m, :, at : at + LANES].astype(F32) for m in members]
            right = [partial_ref[m, :, at + LANES : at + 2 * LANES].astype(F32) for m in members]
            levels = [-(r + pltpu.roll(r, LANES - 1, 1) + pltpu.roll(r, LANES - 2, 1)) for r in right]
            counts = [pltpu.roll(r, LANES - 3, 1) + pltpu.roll(r, LANES - 4, 1) for r in right]
            top = functools.reduce(jnp.maximum, levels)
            shares = [count * jnp.exp2(level - top) for count, level in zip(counts, levels)]
            total = functools.reduce(jnp.add, shares)
            first, second = 0.0, 0.0
            for copy in range(copies):
                share = shares[copy] / total
                h0, h1, h2 = [share[:, c : c + 1] for c in (HEAD_DIM, HEAD_DIM + MARKS, HEAD_DIM + 2 * MARKS)]
                first = first + left[copy] * jnp.where(low, h0, h1)
                second = second + right[copy] * h2
            both = jnp.concatenate([first, second[:, :HEAD_DIM]], axis=1)
            wide_ref[part * half : (part + 1) * half, group * width : (group + 1) * width] = both
    attended = wide_ref[...].astype(BF16)
    projected = jnp.concatenate(
        [jnp.dot(attended, weight_ref[side], preferred_element_type=F32) for side in range(2)], axis=1
    )
    residual = hidden_ref[...].astype(F32) + modulation_ref[0:1] * (projected + bias_ref[...])
    middle = jnp.mean(residual, axis=-1, keepdims=True)
    centered = residual - middle
    spread = jnp.mean(centered * centered, axis=-1, keepdims=True)
    normed = centered * lax.rsqrt(spread + 1e-06) * (1.0 + modulation_ref[1:2]) + modulation_ref[2:3]
    velocity = lax.dot_general(
        normed.astype(BF16), final_ref[...], (((1,), (1,)), ((), ())), preferred_element_type=F32
    )
    out_ref[...] = velocity + final_bias_ref[...]


def finish(partial, weight, hidden, modulation, bias, final_weight, final_bias, heads, groups):
    tokens, width = hidden.shape
    return pl.pallas_call(
        functools.partial(finish_kernel, heads, groups),
        out_shape=jax.ShapeDtypeStruct((tokens, final_weight.shape[0]), F32),
        scratch_shapes=[pltpu.VMEM((tokens, width), F32)],
        compiler_params=params(),
        name="project_and_norm",
    )(partial, weight, hidden, modulation, bias, final_weight, final_bias)


def local(
    latent_qkv,
    text_kv,
    hidden_in,
    modulation,
    out_weight,
    out_bias,
    proj_weight,
    proj_bias,
    guidance,
    sigma,
    sample,
):
    groups = lax.axis_size("zl") * lax.axis_size("y")
    ring = lax.axis_size("zh")
    tokens = latent_qkv.shape[1]
    half = tokens // 2
    width = latent_qkv.shape[3] // groups
    heads = width // HEAD_DIM
    across = lax.axis_size("y")
    zl, core, xh, y = (lax.axis_index(a) for a in ("zl", "core", "xh", "y"))
    after = lax.optimization_barrier

    slabs = pack(latent_qkv[0].transpose(1, 0, 2), groups, heads)
    slabs = lax.all_to_all(slabs, HEAD_AXES, split_axis=0, concat_axis=0, tiled=True)
    own = slabs[:, heads * half :].reshape(groups, heads, tokens, LANES)
    route = []
    for i in range(ring):
        route += [(2 * i, 2 * ((i + 1) % ring)), (2 * i + 1, 2 * ((i - 1) % ring) + 1)]
    pass_on = lambda x: lax.ppermute(x, ("zh", "core"), route)
    packed = slabs[:, : heads * half].reshape(groups, heads, half, LANES)
    both, packed = after((lax.all_gather(own, "core", axis=0), lax.all_gather(packed, "core", axis=0)))
    arrived = pass_on(both)
    opposite = lax.ppermute(packed, "xh", [(0, 1), (1, 0)])
    q = unpack_queries(xh.reshape(1), packed, opposite)

    columns = out_weight.shape[1] // 2
    piece = lax.dynamic_slice_in_dim(out_weight, core * columns, columns, 1)
    weight = lax.all_gather(piece, ("core", "xh", "y"), axis=0, tiled=True).reshape(2, groups * width, columns)

    count = text_kv.shape[1]
    share = -(-count // 32) * 16
    text = text_kv[0].reshape(count, 2, heads, HEAD_DIM).transpose(2, 0, 1, 3).reshape(heads, count, LANES)
    text = jnp.pad(text, ((0, 0), (0, 2 * share - count), (0, 0)))
    text = lax.dynamic_slice_in_dim(text, core * share, share, 1)
    valid = jnp.where(xh == zl, jnp.minimum(count - core * share, share), 0).reshape(1)
    q, state = first_block(valid, q, own, text)
    kept = [own, arrived]
    for _ in range(ring // 2 - 2):
        arrived, state = after((arrived, state))
        further = pass_on(arrived)
        state = next_blocks(q, state, arrived)
        arrived = further
        kept.append(arrived)
    arrived, state = after((arrived, state))
    farthest = pass_on(lax.dynamic_index_in_dim(arrived, core, 0, keepdims=False))
    state = next_blocks(q, state, arrived)
    partial = last_block(valid, q, state, farthest, text, kept)
    partial = partial.reshape(4 * groups, half, 4 * LANES)
    partial = lax.all_to_all(partial, BLOCK_AXES, split_axis=0, concat_axis=0, tiled=True)

    velocity = finish(
        partial,
        weight,
        hidden_in[0],
        modulation[0],
        out_bias[None],
        proj_weight.T,
        proj_bias[None],
        heads,
        groups,
    )

    tiles = velocity.reshape(tokens, 2, -1).transpose(1, 0, 2).reshape(2, -1)
    branch, parity = lax.axis_index("cfg"), y % 2
    same, swap = [], []
    for s in range(2):
        for y in range(across):
            a = y % 2
            same.append((s * across + y, a * across + y - a + s))
            swap.append((s * across + y, a * across + y - a + 1 - s))
    kept = lax.ppermute(lax.dynamic_index_in_dim(tiles, branch, 0, keepdims=False), ("cfg", "y"), same)
    crossed = lax.ppermute(lax.dynamic_index_in_dim(tiles, 1 - branch, 0, keepdims=False), ("cfg", "y"), swap)
    conditional = jnp.where(parity == 0, kept, crossed)
    unconditional = jnp.where(parity == 0, crossed, kept)
    guided = unconditional + guidance[0] * (conditional - unconditional)
    result = guided.reshape(1, guided.shape[0])
    denoised = sample - sigma[0] * result
    return (result, denoised)


def solution(mesh):
    sizes = dict(zip(mesh.axis_names, mesh.devices.shape))
    ring = sizes["blk"] // 4
    fine = Mesh(
        mesh.devices.reshape(sizes["cfg"], ring, 2, 2, 2, sizes["uly"] // 2),
        ("cfg", "zh", "zl", "core", "xh", "y"),
    )
    rows = ("zh", "zl", "core", "xh", "y")
    heads = ("xh", "y")
    return jax.shard_map(
        local,
        mesh=fine,
        in_specs=(
            P("cfg", rows, None, None),
            P("cfg", None, None, heads),
            P("cfg", rows, None),
            P("cfg", None, None),
            P(heads, None),
            P(),
            P(),
            P(),
            P(),
            P(),
            P(rows, "cfg"),
        ),
        out_specs=(P(rows, "cfg"), P(rows, "cfg")),
        check_vma=False,
    )
```

```python
import functools
import math

import jax
import jax.numpy as jnp
from jax import lax
from jax.experimental import pallas as pl
from jax.experimental.pallas import tpu as pltpu
from jax.sharding import Mesh, PartitionSpec as P

HEAD_DIM = 64
LANES = 128
ROW_TILE = 768
LOG2_SCALE = math.log2(math.e) * HEAD_DIM**-0.5
F32 = jnp.float32
BF16 = jnp.bfloat16
GUARD = HEAD_DIM + 3
MARKS = 8
SAFE = 2.0**100
HEAD_AXES = ("zl", "y")
BLOCK_AXES = ("zl", "core", "xh", "y")


def params(**extra):
    return pltpu.CompilerParams(vmem_limit_bytes=32 * 1024 * 1024, **extra)


def lane_index(shape):
    return lax.broadcasted_iota(jnp.int32, shape, len(shape) - 1)


def pack_kernel(groups, heads, x_ref, out_ref):
    rows = x_ref.shape[1]
    half = rows // 2
    for group in range(groups):
        queries, pairs = [], []
        for head in range(heads):
            start = (group * heads + head) * HEAD_DIM
            cols = slice(start, start + HEAD_DIM)
            q = x_ref[0, :, cols].astype(F32)
            k = x_ref[1, :, cols].astype(F32)
            v = x_ref[2, :, cols].astype(F32)
            queries.append(jnp.concatenate([q[:half], q[half:]], axis=1))
            pairs.append(jnp.concatenate([k, v], axis=1))
        out_ref[group] = jnp.concatenate(queries + pairs, axis=0).astype(BF16)


def pack(x, groups, heads):
    rows = x.shape[1]
    return pl.pallas_call(
        functools.partial(pack_kernel, groups, heads),
        out_shape=jax.ShapeDtypeStruct((groups, heads * (rows // 2 + rows), LANES), BF16),
        compiler_params=params(),
        name="pack_heads",
    )(x)


def wide_keys(block, valid=None):
    lane = lane_index(block.shape)
    ones = jnp.ones_like(block)
    marked = jnp.where(lane < HEAD_DIM, block, ones)
    if valid is not None:
        row = lax.broadcasted_iota(jnp.int32, block.shape, 0)
        marked = jnp.where((lane == GUARD) & (row >= valid), jnp.full_like(block, -1e30), marked)
    return jnp.concatenate([block, marked], axis=1), jnp.where(lane < HEAD_DIM, ones, block)


def queries_kernel(heads, place_ref, own_ref, other_ref, out_ref, wide_ref):
    here = place_ref[0]
    cores, sources, _, half, _ = own_ref.shape
    across = sources // 2
    lane = lane_index((half, LANES))
    low = lane < HEAD_DIM
    guard = jnp.where(lane == GUARD, 1.0, 0.0)
    for side, ref in ((here, own_ref), (1 - here, other_ref)):
        for core in range(cores):
            for source in range(sources):
                zl, y = divmod(source, across)
                first = (zl * cores + core) * 2 * across + y
                row = pl.multiple_of((first + side * across) * half, 8)
                for head in range(heads):
                    both = ref[core, source, head].astype(F32) * LOG2_SCALE
                    for part, value in enumerate((both, pltpu.roll(both, HEAD_DIM, 1))):
                        lead = value.astype(BF16).astype(F32)
                        wide_ref[head, part, pl.ds(row, half), 0:LANES] = jnp.where(low, lead, 0.0)
                        wide_ref[head, part, pl.ds(row, half), LANES:] = jnp.where(low, value - lead, guard)
    out_ref[...] = wide_ref[...].astype(BF16)


def unpack_queries(place, own, other):
    cores, sources, heads, half, _ = own.shape
    shape = (heads, 2, 2 * cores * sources * half, 2 * LANES)
    return pl.pallas_call(
        functools.partial(queries_kernel, heads),
        out_shape=jax.ShapeDtypeStruct(shape, BF16),
        in_specs=[
            pl.BlockSpec(memory_space=pltpu.SMEM),
            pl.BlockSpec(memory_space=pltpu.VMEM),
            pl.BlockSpec(memory_space=pltpu.VMEM),
        ],
        out_specs=pl.BlockSpec(memory_space=pltpu.VMEM),
        scratch_shapes=[pltpu.VMEM(shape, F32)],
        compiler_params=params(),
        name="unpack_queries",
    )(place, own, other)


def rows_of(ref, head):
    return ref[:, head].reshape(-1, ref.shape[-1])


def scores_of(q, keys):
    return lax.dot_general(q, keys, (((1,), (1,)), ((), ())), preferred_element_type=F32)


def weighted(scores, values):
    return jnp.dot(jnp.exp2(scores).astype(BF16), values, preferred_element_type=F32)


def first_kernel(heads, valid_ref, q_ref, block_ref, text_ref, full_ref, state_ref):
    rows = 2 * q_ref.shape[2]
    lane = lane_index((rows, LANES))
    for head in range(heads):
        q = q_ref[head].reshape(rows, 2 * LANES)
        keys, values = wide_keys(rows_of(block_ref, head))
        more_keys, more_values = wide_keys(text_ref[head], valid_ref[0])
        scores = scores_of(q, jnp.concatenate([keys, more_keys], axis=0))
        offset = jnp.max(scores, axis=1, keepdims=True)
        state = weighted(scores - offset, jnp.concatenate([values, more_values], axis=0))
        state_ref[head] = state.reshape(state_ref.shape[1:])
        offset = jnp.broadcast_to(-offset, (rows, LANES))
        coarse = offset.astype(BF16).astype(F32)
        middle = (offset - coarse).astype(BF16).astype(F32)
        upper = q[:, LANES:].astype(F32)
        for place, term in enumerate((coarse, middle, offset - coarse - middle)):
            upper = jnp.where(lane == HEAD_DIM + place, term, upper)
        full_ref[head, :, :, :LANES] = q_ref[head, :, :, :LANES]
        full_ref[head, :, :, LANES:] = upper.astype(BF16).reshape(state_ref.shape[1:])


def next_kernel(heads, q_ref, state_ref, *refs):
    *blocks, out_ref = refs
    rows = 2 * q_ref.shape[2]
    for head in range(heads):
        q = q_ref[head].reshape(rows, 2 * LANES)
        keys, values = wide_keys(jnp.concatenate([rows_of(ref, head) for ref in blocks], axis=0))
        state = weighted(scores_of(q, keys), values)
        out_ref[head] = state_ref[head] + state.reshape(out_ref.shape[1:])


def last_kernel(heads, count, valid_ref, q_ref, state_ref, block_ref, first_text_ref, text_ref, *refs):
    kept, out_ref, done_ref, top_ref, spare_ref, sem = refs[:count], *refs[count:]
    tile = q_ref.shape[2]
    rows = 2 * tile
    lane = lane_index((rows, LANES))
    safe = True
    for head in range(heads):
        q = q_ref[head].reshape(rows, 2 * LANES)
        keys, values = wide_keys(rows_of(block_ref, head))
        more_keys, more_values = wide_keys(text_ref[head], valid_ref[0] - first_text_ref.shape[1])
        scores = scores_of(q, jnp.concatenate([keys, more_keys], axis=0))
        state = weighted(scores, jnp.concatenate([values, more_values], axis=0))
        state = state + state_ref[head].reshape(rows, LANES)
        done_ref[head] = state
        top_ref[head] = q[:, LANES:].astype(F32)
        largest = jnp.max(jnp.where(state[:, :HEAD_DIM] < SAFE, 0.0, 1.0))
        safe = jnp.logical_and(safe, largest == 0.0)

    @pl.when(jnp.logical_not(safe))
    def _():
        for at, ref in enumerate(kept):
            copy = pltpu.make_async_copy(ref, spare_ref.at[at], sem)
            copy.start()
            copy.wait()
        spare_ref[count] = block_ref[...]
        for head in range(heads):
            q = q_ref[head].reshape(rows, 2 * LANES)
            spared = (lane >= HEAD_DIM) & (lane < GUARD)
            plain = jnp.concatenate([q[:, :LANES], jnp.where(spared, jnp.zeros_like(q[:, LANES:]), q[:, LANES:])], axis=1)

            def absorb(keys, values, largest, state):
                scores = scores_of(plain, keys)
                higher = jnp.maximum(largest, jnp.max(scores, axis=1, keepdims=True))
                return higher, state * jnp.exp2(largest - higher) + weighted(scores - higher, values)

            def step(at, carry):
                return absorb(*wide_keys(spare_ref[at, :, head].reshape(-1, LANES)), *carry)

            carry = (jnp.full((rows, 1), -1e30, F32), jnp.zeros((rows, LANES), F32))
            carry = lax.fori_loop(0, count + 1, step, carry)
            carry = absorb(*wide_keys(first_text_ref[head], valid_ref[0]), *carry)
            tail = wide_keys(text_ref[head], valid_ref[0] - first_text_ref.shape[1])
            largest, state = absorb(*tail, *carry)
            done_ref[head] = state
            offset = jnp.broadcast_to(-largest, (rows, LANES))
            coarse = offset.astype(BF16).astype(F32)
            middle = (offset - coarse).astype(BF16).astype(F32)
            upper = jnp.zeros((rows, LANES), F32)
            for place, term in enumerate((coarse, middle, offset - coarse - middle)):
                upper = jnp.where(lane == HEAD_DIM + place, term, upper)
            top_ref[head] = upper

    marks = jnp.zeros((rows, LANES), F32)
    done = []
    for head in range(heads):
        state = done_ref[head]
        total = pltpu.roll(state, HEAD_DIM, 1)
        done.append(state / total)
        terms = top_ref[head] if head == 0 else pltpu.roll(top_ref[head], MARKS * head, 1)
        place = HEAD_DIM + MARKS * head
        lead = total.astype(BF16).astype(F32)
        marks = jnp.where((lane >= place) & (lane < place + 3), terms, marks)
        marks = jnp.where(lane == place + 3, lead, marks)
        marks = jnp.where(lane == place + 4, total - lead, marks)
    low = lane < HEAD_DIM
    left = jnp.where(low, pltpu.roll(done[0], HEAD_DIM, 1), done[1]).astype(BF16)
    right = jnp.where(low, pltpu.roll(done[2], HEAD_DIM, 1), marks).astype(BF16)
    for half in range(2):
        part = slice(half * tile, (half + 1) * tile)
        out_ref[:, 2 * half * LANES : (2 * half + 1) * LANES] = left[part]
        out_ref[:, (2 * half + 1) * LANES : (2 * half + 2) * LANES] = right[part]


def attention_call(kernel, name, operands, whole, kept, out_shape, out_axes, scratch=()):
    q = operands[-1] if len(operands[-1].shape) == 4 and operands[-1].dtype == BF16 else operands[-2]
    heads, _, rows, _ = q.shape
    tile = ROW_TILE if rows % ROW_TILE == 0 else rows

    def tiled(shape, axis):
        block = tuple(tile if d == axis else n for d, n in enumerate(shape))
        return pl.BlockSpec(block, lambda i: tuple(i if d == axis else 0 for d in range(len(shape))))

    specs = []
    for x in operands:
        specs.append(tiled(x.shape, 2) if x.ndim == 4 else pl.BlockSpec(memory_space=pltpu.SMEM))
    for x in whole:
        specs.append(pl.BlockSpec(x.shape, lambda i, n=x.ndim: (0,) * n))
    specs += [pl.BlockSpec(memory_space=pl.ANY)] * len(kept)
    keys = sum(x.size // (heads * LANES) for x in whole)
    pairs = heads * 2 * rows * keys
    out_specs = [tiled(s.shape, a) for s, a in zip(out_shape, out_axes)]
    return pl.pallas_call(
        kernel,
        grid=(rows // tile,),
        out_shape=out_shape,
        in_specs=specs,
        out_specs=out_specs,
        scratch_shapes=scratch,
        compiler_params=params(),
        cost_estimate=pl.CostEstimate(flops=pairs * 6 * LANES, bytes_accessed=4 * q.size, transcendentals=pairs),
        name=name,
    )(*operands, *whole, *kept)


def state_shape(q):
    return jax.ShapeDtypeStruct(q.shape[:3] + (LANES,), F32)


def first_block(valid, q, block, text):
    shapes = [jax.ShapeDtypeStruct(q.shape, BF16), state_shape(q)]
    kernel = functools.partial(first_kernel, q.shape[0])
    return attention_call(kernel, "own_block", [valid, q], [block, text], [], shapes, [2, 2])


def next_blocks(q, state, blocks):
    kernel = functools.partial(next_kernel, q.shape[0])
    return attention_call(kernel, "next_blocks", [q, state], blocks, [], [state_shape(q)], [2])[0]


def last_block(valid, q, state, block, first_text, text, kept):
    heads, _, rows, _ = q.shape
    tile = ROW_TILE if rows % ROW_TILE == 0 else rows
    kernel = functools.partial(last_kernel, heads, len(kept))
    shape = jax.ShapeDtypeStruct((rows, 4 * LANES), BF16)
    scratch = [
        pltpu.VMEM((heads, 2 * tile, LANES), F32),
        pltpu.VMEM((heads, 2 * tile, LANES), F32),
        pltpu.VMEM((len(kept) + 1,) + block.shape, BF16),
        pltpu.SemaphoreType.DMA,
    ]
    return attention_call(kernel, "last_block", [valid, q, state], [block, first_text, text], kept, [shape], [0], scratch)[0]


def finish_kernel(
    heads,
    groups,
    partial_ref,
    weight_ref,
    hidden_ref,
    modulation_ref,
    bias_ref,
    final_ref,
    final_bias_ref,
    out_ref,
    wide_ref,
    held_ref,
    sem,
):
    brought = pltpu.make_async_copy(weight_ref, held_ref, sem)
    brought.start()
    half = partial_ref.shape[1]
    sources = partial_ref.shape[0]
    across = groups // 2
    copies = sources // groups
    width = heads * HEAD_DIM
    low = lane_index((half, LANES)) < HEAD_DIM
    for part in range(2):
        at = part * 2 * LANES
        for group in range(groups):
            zl, y = divmod(group, across)
            members = [(zl * copies + copy) * across + y for copy in range(copies)]
            left = [partial_ref[m, :, at : at + LANES].astype(F32) for m in members]
            right = [partial_ref[m, :, at + LANES : at + 2 * LANES].astype(F32) for m in members]
            levels = [-(r + pltpu.roll(r, LANES - 1, 1) + pltpu.roll(r, LANES - 2, 1)) for r in right]
            counts = [pltpu.roll(r, LANES - 3, 1) + pltpu.roll(r, LANES - 4, 1) for r in right]
            top = functools.reduce(jnp.maximum, levels)
            shares = [count * jnp.exp2(level - top) for count, level in zip(counts, levels)]
            total = functools.reduce(jnp.add, shares)
            first, second = 0.0, 0.0
            for copy in range(copies):
                share = shares[copy] / total
                h0, h1, h2 = [share[:, c : c + 1] for c in (HEAD_DIM, HEAD_DIM + MARKS, HEAD_DIM + 2 * MARKS)]
                first = first + left[copy] * jnp.where(low, h0, h1)
                second = second + right[copy] * h2
            both = jnp.concatenate([first, second[:, :HEAD_DIM]], axis=1)
            wide_ref[part * half : (part + 1) * half, group * width : (group + 1) * width] = both
    attended = wide_ref[...].astype(BF16)
    brought.wait()
    projected = jnp.concatenate(
        [jnp.dot(attended, held_ref[side], preferred_element_type=F32) for side in range(2)], axis=1
    )
    residual = hidden_ref[...].astype(F32) + modulation_ref[0:1] * (projected + bias_ref[...])
    middle = jnp.mean(residual, axis=-1, keepdims=True)
    centered = residual - middle
    spread = jnp.mean(centered * centered, axis=-1, keepdims=True)
    normed = centered * lax.rsqrt(spread + 1e-06) * (1.0 + modulation_ref[1:2]) + modulation_ref[2:3]
    velocity = lax.dot_general(
        normed.astype(BF16), final_ref[...], (((1,), (1,)), ((), ())), preferred_element_type=F32
    )
    out_ref[...] = velocity + final_bias_ref[...]


def finish(partial, weight, hidden, modulation, bias, final_weight, final_bias, heads, groups):
    tokens, width = hidden.shape
    vmem = pl.BlockSpec(memory_space=pltpu.VMEM)
    return pl.pallas_call(
        functools.partial(finish_kernel, heads, groups),
        out_shape=jax.ShapeDtypeStruct((tokens, final_weight.shape[0]), F32),
        in_specs=[vmem, pl.BlockSpec(memory_space=pl.ANY), vmem, vmem, vmem, vmem, vmem],
        out_specs=vmem,
        scratch_shapes=[
            pltpu.VMEM((tokens, width), F32),
            pltpu.VMEM(weight.shape, BF16),
            pltpu.SemaphoreType.DMA,
        ],
        compiler_params=params(),
        name="project_and_norm",
    )(partial, weight, hidden, modulation, bias, final_weight, final_bias)


def local(
    latent_qkv,
    text_kv,
    hidden_in,
    modulation,
    out_weight,
    out_bias,
    proj_weight,
    proj_bias,
    guidance,
    sigma,
    sample,
):
    groups = lax.axis_size("zl") * lax.axis_size("y")
    ring = lax.axis_size("zh")
    tokens = latent_qkv.shape[1]
    half = tokens // 2
    width = latent_qkv.shape[3] // groups
    heads = width // HEAD_DIM
    across = lax.axis_size("y")
    zl, core, xh, y = (lax.axis_index(a) for a in ("zl", "core", "xh", "y"))
    after = lax.optimization_barrier

    slabs = pack(latent_qkv[0].transpose(1, 0, 2), groups, heads)
    slabs = lax.all_to_all(slabs, HEAD_AXES, split_axis=0, concat_axis=0, tiled=True)
    own = slabs[:, heads * half :].reshape(groups, heads, tokens, LANES)
    route = []
    for i in range(ring):
        route += [(2 * i, 2 * ((i + 1) % ring)), (2 * i + 1, 2 * ((i - 1) % ring) + 1)]
    pass_on = lambda x: lax.ppermute(x, ("zh", "core"), route)
    near = pass_on(own)
    beside = lax.ppermute(own, "core", [(0, 1), (1, 0)])
    packed = slabs[:, : heads * half].reshape(groups, heads, half, LANES)
    packed = lax.all_gather(packed, "core", axis=0)
    opposite = lax.ppermute(packed, "xh", [(0, 1), (1, 0)])
    cross = pass_on(beside)
    q = unpack_queries(xh.reshape(1), packed, opposite)

    columns = out_weight.shape[1] // 2
    piece = lax.dynamic_slice_in_dim(out_weight, core * columns, columns, 1)
    weight = lax.all_gather(piece, ("core", "xh", "y"), axis=0, tiled=True).reshape(2, groups * width, columns)

    count = text_kv.shape[1]
    share = -(-count // 32) * 16
    text = text_kv[0].reshape(count, 2, heads, HEAD_DIM).transpose(2, 0, 1, 3).reshape(heads, count, LANES)
    text = jnp.pad(text, ((0, 0), (0, 2 * share - count), (0, 0)))
    text = lax.dynamic_slice_in_dim(text, core * share, share, 1)
    valid = jnp.where(xh == zl, jnp.minimum(count - core * share, share), 0).reshape(1)
    early, late = text[:, :LANES], text[:, LANES:]
    q, state = first_block(valid, q, own, early)
    kept = [own, near, cross]
    ready = None
    for _ in range(ring // 2 - 2):
        if ready is not None:
            near, ready = after((near, ready))
        nearer = pass_on(near)
        cross, state = after((cross, state))
        crosser = pass_on(cross)
        ready = state
        state = next_blocks(q, state, [near, cross])
        near, cross = nearer, crosser
        kept += [near, cross]
    near, ready = after((near, ready))
    farthest = pass_on(near)
    state = next_blocks(q, state, [near, cross])
    partial = last_block(valid, q, state, farthest, early, late, kept)
    partial = partial.reshape(4 * groups, half, 4 * LANES)
    partial = lax.all_to_all(partial, BLOCK_AXES, split_axis=0, concat_axis=0, tiled=True)

    velocity = finish(
        partial,
        weight,
        hidden_in[0],
        modulation[0],
        out_bias[None],
        proj_weight.T,
        proj_bias[None],
        heads,
        groups,
    )

    tiles = velocity.reshape(tokens, 2, -1).transpose(1, 0, 2).reshape(2, -1)
    branch, parity = lax.axis_index("cfg"), y % 2
    same, swap = [], []
    for s in range(2):
        for y in range(across):
            a = y % 2
            same.append((s * across + y, a * across + y - a + s))
            swap.append((s * across + y, a * across + y - a + 1 - s))
    kept = lax.ppermute(lax.dynamic_index_in_dim(tiles, branch, 0, keepdims=False), ("cfg", "y"), same)
    crossed = lax.ppermute(lax.dynamic_index_in_dim(tiles, 1 - branch, 0, keepdims=False), ("cfg", "y"), swap)
    conditional = jnp.where(parity == 0, kept, crossed)
    unconditional = jnp.where(parity == 0, crossed, kept)
    guided = unconditional + guidance[0] * (conditional - unconditional)
    result = guided.reshape(1, guided.shape[0])
    denoised = sample - sigma[0] * result
    return (result, denoised)


def solution(mesh):
    sizes = dict(zip(mesh.axis_names, mesh.devices.shape))
    ring = sizes["blk"] // 4
    fine = Mesh(
        mesh.devices.reshape(sizes["cfg"], ring, 2, 2, 2, sizes["uly"] // 2),
        ("cfg", "zh", "zl", "core", "xh", "y"),
    )
    rows = ("zh", "zl", "core", "xh", "y")
    heads = ("xh", "y")
    return jax.shard_map(
        local,
        mesh=fine,
        in_specs=(
            P("cfg", rows, None, None),
            P("cfg", None, None, heads),
            P("cfg", rows, None),
            P("cfg", None, None),
            P(heads, None),
            P(),
            P(),
            P(),
            P(),
            P(),
            P(rows, "cfg"),
        ),
        out_specs=(P(rows, "cfg"), P(rows, "cfg")),
        check_vma=False,
    )
```

```python
import functools
import math

import jax
import jax.numpy as jnp
from jax import lax
from jax.experimental import pallas as pl
from jax.experimental.pallas import tpu as pltpu
from jax.sharding import Mesh, PartitionSpec as P

HEAD_DIM = 64
LANES = 128
ROW_TILE = 768
LOG2_SCALE = math.log2(math.e) * HEAD_DIM**-0.5
F32 = jnp.float32
BF16 = jnp.bfloat16
GUARD = HEAD_DIM + 3
MARKS = 8
SAFE = 2.0**100
HEAD_AXES = ("zl", "y")
BLOCK_AXES = ("zl", "core", "xh", "y")


def params(**extra):
    return pltpu.CompilerParams(vmem_limit_bytes=32 * 1024 * 1024, **extra)


def lane_index(shape):
    return lax.broadcasted_iota(jnp.int32, shape, len(shape) - 1)


def pack_kernel(groups, heads, x_ref, out_ref):
    rows = x_ref.shape[1]
    half = rows // 2
    for group in range(groups):
        queries, pairs = [], []
        for head in range(heads):
            start = (group * heads + head) * HEAD_DIM
            cols = slice(start, start + HEAD_DIM)
            q = x_ref[0, :, cols].astype(F32)
            k = x_ref[1, :, cols].astype(F32)
            v = x_ref[2, :, cols].astype(F32)
            queries.append(jnp.concatenate([q[:half], q[half:]], axis=1))
            pairs.append(jnp.concatenate([k, v], axis=1))
        out_ref[group] = jnp.concatenate(queries + pairs, axis=0).astype(BF16)


def pack(x, groups, heads):
    rows = x.shape[1]
    return pl.pallas_call(
        functools.partial(pack_kernel, groups, heads),
        out_shape=jax.ShapeDtypeStruct((groups, heads * (rows // 2 + rows), LANES), BF16),
        compiler_params=params(),
        name="pack_heads",
    )(x)


def wide_keys(block, valid=None):
    lane = lane_index(block.shape)
    ones = jnp.ones_like(block)
    marked = jnp.where(lane < HEAD_DIM, block, ones)
    if valid is not None:
        row = lax.broadcasted_iota(jnp.int32, block.shape, 0)
        marked = jnp.where((lane == GUARD) & (row >= valid), jnp.full_like(block, -1e30), marked)
    return jnp.concatenate([block, marked], axis=1), jnp.where(lane < HEAD_DIM, ones, block)


def queries_kernel(heads, place_ref, own_ref, other_ref, out_ref, wide_ref):
    here = place_ref[0]
    cores, sources, _, half, _ = own_ref.shape
    across = sources // 2
    lane = lane_index((half, LANES))
    low = lane < HEAD_DIM
    guard = jnp.where(lane == GUARD, 1.0, 0.0)
    for side, ref in ((here, own_ref), (1 - here, other_ref)):
        for core in range(cores):
            for source in range(sources):
                zl, y = divmod(source, across)
                first = (zl * cores + core) * 2 * across + y
                row = pl.multiple_of((first + side * across) * half, 8)
                for head in range(heads):
                    both = ref[core, source, head].astype(F32) * LOG2_SCALE
                    for part, value in enumerate((both, pltpu.roll(both, HEAD_DIM, 1))):
                        lead = value.astype(BF16).astype(F32)
                        wide_ref[head, part, pl.ds(row, half), 0:LANES] = jnp.where(low, lead, 0.0)
                        wide_ref[head, part, pl.ds(row, half), LANES:] = jnp.where(low, value - lead, guard)
    out_ref[...] = wide_ref[...].astype(BF16)


def unpack_queries(place, own, other):
    cores, sources, heads, half, _ = own.shape
    shape = (heads, 2, 2 * cores * sources * half, 2 * LANES)
    return pl.pallas_call(
        functools.partial(queries_kernel, heads),
        out_shape=jax.ShapeDtypeStruct(shape, BF16),
        in_specs=[
            pl.BlockSpec(memory_space=pltpu.SMEM),
            pl.BlockSpec(memory_space=pltpu.VMEM),
            pl.BlockSpec(memory_space=pltpu.VMEM),
        ],
        out_specs=pl.BlockSpec(memory_space=pltpu.VMEM),
        scratch_shapes=[pltpu.VMEM(shape, F32)],
        compiler_params=params(),
        name="unpack_queries",
    )(place, own, other)


def rows_of(ref, head):
    return ref[:, head].reshape(-1, ref.shape[-1])


def scores_of(q, keys):
    return lax.dot_general(q, keys, (((1,), (1,)), ((), ())), preferred_element_type=F32)


def weighted(scores, values):
    return jnp.dot(jnp.exp2(scores).astype(BF16), values, preferred_element_type=F32)


def first_kernel(heads, valid_ref, q_ref, block_ref, text_ref, full_ref, state_ref, mark_ref):
    mark_ref[...] = jnp.zeros_like(mark_ref)
    rows = 2 * q_ref.shape[2]
    lane = lane_index((rows, LANES))
    for head in range(heads):
        q = q_ref[head].reshape(rows, 2 * LANES)
        keys, values = wide_keys(rows_of(block_ref, head))
        more_keys, more_values = wide_keys(text_ref[head], valid_ref[0])
        scores = scores_of(q, jnp.concatenate([keys, more_keys], axis=0))
        offset = jnp.max(scores, axis=1, keepdims=True)
        state = weighted(scores - offset, jnp.concatenate([values, more_values], axis=0))
        state_ref[head] = state.reshape(state_ref.shape[1:])
        offset = jnp.broadcast_to(-offset, (rows, LANES))
        coarse = offset.astype(BF16).astype(F32)
        middle = (offset - coarse).astype(BF16).astype(F32)
        upper = q[:, LANES:].astype(F32)
        for place, term in enumerate((coarse, middle, offset - coarse - middle)):
            upper = jnp.where(lane == HEAD_DIM + place, term, upper)
        full_ref[head, :, :, :LANES] = q_ref[head, :, :, :LANES]
        full_ref[head, :, :, LANES:] = upper.astype(BF16).reshape(state_ref.shape[1:])


def next_kernel(heads, q_ref, state_ref, *refs):
    *blocks, before_ref, out_ref, mark_ref = refs
    mark_ref[...] = before_ref[...]
    rows = 2 * q_ref.shape[2]
    for head in range(heads):
        q = q_ref[head].reshape(rows, 2 * LANES)
        keys, values = wide_keys(jnp.concatenate([rows_of(ref, head) for ref in blocks], axis=0))
        state = weighted(scores_of(q, keys), values)
        out_ref[head] = state_ref[head] + state.reshape(out_ref.shape[1:])


def last_kernel(heads, count, valid_ref, q_ref, state_ref, block_ref, first_text_ref, text_ref, *refs):
    kept, out_ref, done_ref, top_ref, spare_ref, sem = refs[:count], *refs[count:]
    tile = q_ref.shape[2]
    rows = 2 * tile
    lane = lane_index((rows, LANES))
    safe = True
    for head in range(heads):
        q = q_ref[head].reshape(rows, 2 * LANES)
        keys, values = wide_keys(rows_of(block_ref, head))
        more_keys, more_values = wide_keys(text_ref[head], valid_ref[0] - first_text_ref.shape[1])
        scores = scores_of(q, jnp.concatenate([keys, more_keys], axis=0))
        state = weighted(scores, jnp.concatenate([values, more_values], axis=0))
        state = state + state_ref[head].reshape(rows, LANES)
        done_ref[head] = state
        top_ref[head] = q[:, LANES:].astype(F32)
        largest = jnp.max(jnp.where(state[:, :HEAD_DIM] < SAFE, 0.0, 1.0))
        safe = jnp.logical_and(safe, largest == 0.0)

    @pl.when(jnp.logical_not(safe))
    def _():
        for at, ref in enumerate(kept):
            copy = pltpu.make_async_copy(ref, spare_ref.at[at], sem)
            copy.start()
            copy.wait()
        spare_ref[count] = block_ref[...]
        for head in range(heads):
            q = q_ref[head].reshape(rows, 2 * LANES)
            spared = (lane >= HEAD_DIM) & (lane < GUARD)
            plain = jnp.concatenate([q[:, :LANES], jnp.where(spared, jnp.zeros_like(q[:, LANES:]), q[:, LANES:])], axis=1)

            def absorb(keys, values, largest, state):
                scores = scores_of(plain, keys)
                higher = jnp.maximum(largest, jnp.max(scores, axis=1, keepdims=True))
                return higher, state * jnp.exp2(largest - higher) + weighted(scores - higher, values)

            def step(at, carry):
                return absorb(*wide_keys(spare_ref[at, :, head].reshape(-1, LANES)), *carry)

            carry = (jnp.full((rows, 1), -1e30, F32), jnp.zeros((rows, LANES), F32))
            carry = lax.fori_loop(0, count + 1, step, carry)
            carry = absorb(*wide_keys(first_text_ref[head], valid_ref[0]), *carry)
            tail = wide_keys(text_ref[head], valid_ref[0] - first_text_ref.shape[1])
            largest, state = absorb(*tail, *carry)
            done_ref[head] = state
            offset = jnp.broadcast_to(-largest, (rows, LANES))
            coarse = offset.astype(BF16).astype(F32)
            middle = (offset - coarse).astype(BF16).astype(F32)
            upper = jnp.zeros((rows, LANES), F32)
            for place, term in enumerate((coarse, middle, offset - coarse - middle)):
                upper = jnp.where(lane == HEAD_DIM + place, term, upper)
            top_ref[head] = upper

    marks = jnp.zeros((rows, LANES), F32)
    done = []
    for head in range(heads):
        state = done_ref[head]
        total = pltpu.roll(state, HEAD_DIM, 1)
        done.append(state / total)
        terms = top_ref[head] if head == 0 else pltpu.roll(top_ref[head], MARKS * head, 1)
        place = HEAD_DIM + MARKS * head
        lead = total.astype(BF16).astype(F32)
        marks = jnp.where((lane >= place) & (lane < place + 3), terms, marks)
        marks = jnp.where(lane == place + 3, lead, marks)
        marks = jnp.where(lane == place + 4, total - lead, marks)
    low = lane < HEAD_DIM
    left = jnp.where(low, pltpu.roll(done[0], HEAD_DIM, 1), done[1]).astype(BF16)
    right = jnp.where(low, pltpu.roll(done[2], HEAD_DIM, 1), marks).astype(BF16)
    for half in range(2):
        part = slice(half * tile, (half + 1) * tile)
        out_ref[:, 2 * half * LANES : (2 * half + 1) * LANES] = left[part]
        out_ref[:, (2 * half + 1) * LANES : (2 * half + 2) * LANES] = right[part]


def attention_call(kernel, name, operands, whole, kept, out_shape, out_axes, scratch=()):
    q = operands[-1] if len(operands[-1].shape) == 4 and operands[-1].dtype == BF16 else operands[-2]
    heads, _, rows, _ = q.shape
    tile = ROW_TILE if rows % ROW_TILE == 0 else rows

    def tiled(shape, axis):
        if axis is None:
            return pl.BlockSpec(shape, lambda i: (0,) * len(shape))
        block = tuple(tile if d == axis else n for d, n in enumerate(shape))
        return pl.BlockSpec(block, lambda i: tuple(i if d == axis else 0 for d in range(len(shape))))

    specs = []
    for x in operands:
        specs.append(tiled(x.shape, 2) if x.ndim == 4 else pl.BlockSpec(memory_space=pltpu.SMEM))
    for x in whole:
        specs.append(pl.BlockSpec(x.shape, lambda i, n=x.ndim: (0,) * n))
    specs += [pl.BlockSpec(memory_space=pltpu.HBM)] * len(kept)
    keys = sum(x.size // (heads * LANES) for x in whole)
    pairs = heads * 2 * rows * keys
    out_specs = [tiled(s.shape, a) for s, a in zip(out_shape, out_axes)]
    return pl.pallas_call(
        kernel,
        grid=(rows // tile,),
        out_shape=out_shape,
        in_specs=specs,
        out_specs=out_specs,
        scratch_shapes=scratch,
        compiler_params=params(),
        cost_estimate=pl.CostEstimate(flops=pairs * 6 * LANES, bytes_accessed=4 * q.size, transcendentals=pairs),
        name=name,
    )(*operands, *whole, *kept)


def state_shape(q):
    return jax.ShapeDtypeStruct(q.shape[:3] + (LANES,), F32)


MARK = jax.ShapeDtypeStruct((8, LANES), F32)


def first_block(valid, q, block, text):
    shapes = [jax.ShapeDtypeStruct(q.shape, BF16), state_shape(q), MARK]
    kernel = functools.partial(first_kernel, q.shape[0])
    return attention_call(kernel, "own_block", [valid, q], [block, text], [], shapes, [2, 2, None])


def next_blocks(q, state, blocks, mark):
    kernel = functools.partial(next_kernel, q.shape[0])
    return attention_call(kernel, "next_blocks", [q, state], blocks + [mark], [], [state_shape(q), MARK], [2, None])


def last_block(valid, q, state, block, first_text, text, kept):
    heads, _, rows, _ = q.shape
    tile = ROW_TILE if rows % ROW_TILE == 0 else rows
    kernel = functools.partial(last_kernel, heads, len(kept))
    shape = jax.ShapeDtypeStruct((rows, 4 * LANES), BF16)
    scratch = [
        pltpu.VMEM((heads, 2 * tile, LANES), F32),
        pltpu.VMEM((heads, 2 * tile, LANES), F32),
        pltpu.VMEM((len(kept) + 1,) + block.shape, BF16),
        pltpu.SemaphoreType.DMA,
    ]
    return attention_call(kernel, "last_block", [valid, q, state], [block, first_text, text], kept, [shape], [0], scratch)[0]


def finish_kernel(
    heads,
    groups,
    partial_ref,
    weight_ref,
    hidden_ref,
    modulation_ref,
    bias_ref,
    final_ref,
    final_bias_ref,
    out_ref,
    wide_ref,
    held_ref,
    input_ref,
    sems,
):
    brought = pltpu.make_async_copy(weight_ref, held_ref, sems.at[0])
    taken = pltpu.make_async_copy(hidden_ref, input_ref, sems.at[1])
    brought.start()
    taken.start()
    half = partial_ref.shape[1]
    sources = partial_ref.shape[0]
    across = groups // 2
    copies = sources // groups
    width = heads * HEAD_DIM
    low = lane_index((half, LANES)) < HEAD_DIM
    for part in range(2):
        at = part * 2 * LANES
        for group in range(groups):
            zl, y = divmod(group, across)
            members = [(zl * copies + copy) * across + y for copy in range(copies)]
            left = [partial_ref[m, :, at : at + LANES].astype(F32) for m in members]
            right = [partial_ref[m, :, at + LANES : at + 2 * LANES].astype(F32) for m in members]
            levels = [-(r + pltpu.roll(r, LANES - 1, 1) + pltpu.roll(r, LANES - 2, 1)) for r in right]
            counts = [pltpu.roll(r, LANES - 3, 1) + pltpu.roll(r, LANES - 4, 1) for r in right]
            top = functools.reduce(jnp.maximum, levels)
            shares = [count * jnp.exp2(level - top) for count, level in zip(counts, levels)]
            total = functools.reduce(jnp.add, shares)
            first, second = 0.0, 0.0
            for copy in range(copies):
                share = shares[copy] / total
                h0, h1, h2 = [share[:, c : c + 1] for c in (HEAD_DIM, HEAD_DIM + MARKS, HEAD_DIM + 2 * MARKS)]
                first = first + left[copy] * jnp.where(low, h0, h1)
                second = second + right[copy] * h2
            both = jnp.concatenate([first, second[:, :HEAD_DIM]], axis=1)
            wide_ref[part * half : (part + 1) * half, group * width : (group + 1) * width] = both
    attended = wide_ref[...].astype(BF16)
    brought.wait()
    taken.wait()
    projected = jnp.concatenate(
        [jnp.dot(attended, held_ref[side], preferred_element_type=F32) for side in range(2)], axis=1
    )
    residual = input_ref[...].astype(F32) + modulation_ref[0:1] * (projected + bias_ref[...])
    middle = jnp.mean(residual, axis=-1, keepdims=True)
    centered = residual - middle
    spread = jnp.mean(centered * centered, axis=-1, keepdims=True)
    normed = centered * lax.rsqrt(spread + 1e-06) * (1.0 + modulation_ref[1:2]) + modulation_ref[2:3]
    velocity = lax.dot_general(
        normed.astype(BF16), final_ref[...], (((1,), (1,)), ((), ())), preferred_element_type=F32
    )
    out_ref[...] = velocity + final_bias_ref[...]


def finish(partial, weight, hidden, modulation, bias, final_weight, final_bias, heads, groups):
    tokens, width = hidden.shape
    vmem = pl.BlockSpec(memory_space=pltpu.VMEM)
    hbm = pl.BlockSpec(memory_space=pltpu.HBM)
    return pl.pallas_call(
        functools.partial(finish_kernel, heads, groups),
        out_shape=jax.ShapeDtypeStruct((tokens, final_weight.shape[0]), F32),
        in_specs=[vmem, hbm, hbm, vmem, vmem, vmem, vmem],
        out_specs=vmem,
        scratch_shapes=[
            pltpu.VMEM((tokens, width), F32),
            pltpu.VMEM(weight.shape, BF16),
            pltpu.VMEM(hidden.shape, BF16),
            pltpu.SemaphoreType.DMA((2,)),
        ],
        compiler_params=params(),
        name="project_and_norm",
    )(partial, weight, hidden, modulation, bias, final_weight, final_bias)


def local(
    latent_qkv,
    text_kv,
    hidden_in,
    modulation,
    out_weight,
    out_bias,
    proj_weight,
    proj_bias,
    guidance,
    sigma,
    sample,
):
    groups = lax.axis_size("zl") * lax.axis_size("y")
    ring = lax.axis_size("zh")
    tokens = latent_qkv.shape[1]
    half = tokens // 2
    width = latent_qkv.shape[3] // groups
    heads = width // HEAD_DIM
    across = lax.axis_size("y")
    zl, core, xh, y = (lax.axis_index(a) for a in ("zl", "core", "xh", "y"))
    after = lax.optimization_barrier

    slabs = pack(latent_qkv[0].transpose(1, 0, 2), groups, heads)
    slabs = lax.all_to_all(slabs, HEAD_AXES, split_axis=0, concat_axis=0, tiled=True)
    packed = slabs[:, : heads * half].reshape(groups, heads, half, LANES)
    packed = lax.all_gather(packed, "core", axis=0)
    own, packed = after((slabs[:, heads * half :].reshape(groups, heads, tokens, LANES), packed))
    route = []
    for i in range(ring):
        route += [(2 * i, 2 * ((i + 1) % ring)), (2 * i + 1, 2 * ((i - 1) % ring) + 1)]
    pass_on = lambda x: lax.ppermute(x, ("zh", "core"), route)
    near = pass_on(own)
    beside = lax.ppermute(own, "core", [(0, 1), (1, 0)])
    opposite = lax.ppermute(packed, "xh", [(0, 1), (1, 0)])
    cross = pass_on(beside)
    q = unpack_queries(xh.reshape(1), packed, opposite)

    columns = out_weight.shape[1] // 2
    piece = lax.dynamic_slice_in_dim(out_weight, core * columns, columns, 1)
    weight = lax.all_gather(piece, ("core", "xh", "y"), axis=0, tiled=True).reshape(2, groups * width, columns)

    count = text_kv.shape[1]
    share = -(-count // 32) * 16
    text = text_kv[0].reshape(count, 2, heads, HEAD_DIM).transpose(2, 0, 1, 3).reshape(heads, count, LANES)
    text = jnp.pad(text, ((0, 0), (0, 2 * share - count), (0, 0)))
    text = lax.dynamic_slice_in_dim(text, core * share, share, 1)
    valid = jnp.where(xh == zl, jnp.minimum(count - core * share, share), 0).reshape(1)
    early, late = text[:, :LANES], text[:, LANES:]
    q, state, mark = first_block(valid, q, own, early)
    kept = [own, near, cross]
    for step in range(ring // 2 - 2):
        if step:
            near, mark = after((near, mark))
        nearer = pass_on(near)
        cross, mark = after((cross, mark))
        crosser = pass_on(cross)
        state, mark = next_blocks(q, state, [near, cross], mark)
        near, cross = nearer, crosser
        kept += [near, cross]
    near, mark = after((near, mark))
    farthest = pass_on(near)
    state, mark = next_blocks(q, state, [near, cross], mark)
    partial = last_block(valid, q, state, farthest, early, late, kept)
    partial = partial.reshape(4 * groups, half, 4 * LANES)
    partial = lax.all_to_all(partial, BLOCK_AXES, split_axis=0, concat_axis=0, tiled=True)

    velocity = finish(
        partial,
        weight,
        hidden_in[0],
        modulation[0],
        out_bias[None],
        proj_weight.T,
        proj_bias[None],
        heads,
        groups,
    )

    tiles = velocity.reshape(tokens, 2, -1).transpose(1, 0, 2).reshape(2, -1)
    branch, parity = lax.axis_index("cfg"), y % 2
    same, swap = [], []
    for s in range(2):
        for y in range(across):
            a = y % 2
            same.append((s * across + y, a * across + y - a + s))
            swap.append((s * across + y, a * across + y - a + 1 - s))
    kept = lax.ppermute(lax.dynamic_slice_in_dim(tiles, branch, 1, 0), ("cfg", "y"), same)
    crossed = lax.ppermute(lax.dynamic_slice_in_dim(tiles, 1 - branch, 1, 0), ("cfg", "y"), swap)
    conditional = jnp.where(parity == 0, kept, crossed)
    unconditional = jnp.where(parity == 0, crossed, kept)
    guided = unconditional + guidance[0] * (conditional - unconditional)
    denoised = sample - sigma[0] * guided
    return (guided, denoised)


def solution(mesh):
    sizes = dict(zip(mesh.axis_names, mesh.devices.shape))
    ring = sizes["blk"] // 4
    fine = Mesh(
        mesh.devices.reshape(sizes["cfg"], ring, 2, 2, 2, sizes["uly"] // 2),
        ("cfg", "zh", "zl", "core", "xh", "y"),
    )
    rows = ("zh", "zl", "core", "xh", "y")
    heads = ("xh", "y")
    return jax.shard_map(
        local,
        mesh=fine,
        in_specs=(
            P("cfg", rows, None, None),
            P("cfg", None, None, heads),
            P("cfg", rows, None),
            P("cfg", None, None),
            P(heads, None),
            P(),
            P(),
            P(),
            P(),
            P(),
            P(rows, "cfg"),
        ),
        out_specs=(P(rows, "cfg"), P(rows, "cfg")),
        check_vma=False,
    )
```

```python
import functools
import math

import jax
import jax.numpy as jnp
from jax import lax
from jax.experimental import pallas as pl
from jax.experimental.pallas import tpu as pltpu
from jax.sharding import Mesh, PartitionSpec as P

HEAD_DIM = 64
LANES = 128
LOG2_SCALE = math.log2(math.e) * HEAD_DIM**-0.5
F32 = jnp.float32
BF16 = jnp.bfloat16
GUARD = HEAD_DIM + 3
MARKS = 8
SAFE = 2.0**100
HEAD_AXES = ("zl", "y")
BLOCK_AXES = ("zl", "core", "xh", "y")


def params(mib=16):
    return pltpu.CompilerParams(vmem_limit_bytes=mib * 1024 * 1024)


def lane_index(shape):
    return lax.broadcasted_iota(jnp.int32, shape, len(shape) - 1)


def pack_kernel(groups, heads, x_ref, out_ref):
    rows = x_ref.shape[1]
    half = rows // 2
    for group in range(groups):
        queries, pairs = [], []
        for head in range(heads):
            start = (group * heads + head) * HEAD_DIM
            cols = slice(start, start + HEAD_DIM)
            q = x_ref[0, :, cols].astype(F32)
            k = x_ref[1, :, cols].astype(F32)
            v = x_ref[2, :, cols].astype(F32)
            queries.append(jnp.concatenate([q[:half], q[half:]], axis=1))
            pairs.append(jnp.concatenate([k, v], axis=1))
        out_ref[group] = jnp.concatenate(queries + pairs, axis=0).astype(BF16)


def pack(x, groups, heads):
    rows = x.shape[1]
    return pl.pallas_call(
        functools.partial(pack_kernel, groups, heads),
        out_shape=jax.ShapeDtypeStruct((groups, heads * (rows // 2 + rows), LANES), BF16),
        compiler_params=params(),
        name="pack_heads",
    )(x)


def wide_keys(block, valid=None):
    lane = lane_index(block.shape)
    ones = jnp.ones_like(block)
    marked = jnp.where(lane < HEAD_DIM, block, ones)
    if valid is not None:
        row = lax.broadcasted_iota(jnp.int32, block.shape, 0)
        marked = jnp.where((lane == GUARD) & (row >= valid), jnp.full_like(block, -1e30), marked)
    return jnp.concatenate([block, marked], axis=1), jnp.where(lane < HEAD_DIM, ones, block)


def queries_kernel(heads, place_ref, own_ref, other_ref, out_ref, wide_ref):
    here = place_ref[0]
    cores, sources, _, half, _ = own_ref.shape
    across = sources // 2
    lane = lane_index((half, LANES))
    low = lane < HEAD_DIM
    guard = jnp.where(lane == GUARD, 1.0, 0.0)
    for side, ref in ((here, own_ref), (1 - here, other_ref)):
        for core in range(cores):
            for source in range(sources):
                zl, y = divmod(source, across)
                first = (zl * cores + core) * 2 * across + y
                row = pl.multiple_of((first + side * across) * half, 8)
                for head in range(heads):
                    both = ref[core, source, head].astype(F32) * LOG2_SCALE
                    for part, value in enumerate((both, pltpu.roll(both, HEAD_DIM, 1))):
                        lead = value.astype(BF16).astype(F32)
                        wide_ref[head, part, pl.ds(row, half), 0:LANES] = jnp.where(low, lead, 0.0)
                        wide_ref[head, part, pl.ds(row, half), LANES:] = jnp.where(low, value - lead, guard)
    out_ref[...] = wide_ref[...].astype(BF16)


def unpack_queries(place, own, other):
    cores, sources, heads, half, _ = own.shape
    shape = (heads, 2, 2 * cores * sources * half, 2 * LANES)
    return pl.pallas_call(
        functools.partial(queries_kernel, heads),
        out_shape=jax.ShapeDtypeStruct(shape, BF16),
        in_specs=[
            pl.BlockSpec(memory_space=pltpu.SMEM),
            pl.BlockSpec(memory_space=pltpu.VMEM),
            pl.BlockSpec(memory_space=pltpu.VMEM),
        ],
        out_specs=pl.BlockSpec(memory_space=pltpu.VMEM),
        scratch_shapes=[pltpu.VMEM(shape, F32)],
        compiler_params=params(),
        name="unpack_queries",
    )(place, own, other)


def rows_of(ref):
    return ref[:, 0].reshape(-1, ref.shape[-1])


def scores_of(q, keys):
    return lax.dot_general(q, keys, (((1,), (1,)), ((), ())), preferred_element_type=F32)


def weighted(scores, values):
    return jnp.dot(jnp.exp2(scores).astype(BF16), values, preferred_element_type=F32)


def first_kernel(valid_ref, q_ref, block_ref, text_ref, full_ref, state_ref, mark_ref):
    rows = 2 * q_ref.shape[2]
    mark_ref[...] = jnp.zeros_like(mark_ref)
    q = q_ref[0].reshape(rows, 2 * LANES)
    keys, values = wide_keys(rows_of(block_ref))
    more_keys, more_values = wide_keys(text_ref[0], valid_ref[0])
    scores = scores_of(q, jnp.concatenate([keys, more_keys], axis=0))
    offset = jnp.max(scores, axis=1, keepdims=True)
    state = weighted(scores - offset, jnp.concatenate([values, more_values], axis=0))
    state_ref[0] = state.reshape(state_ref.shape[1:])
    full_ref[0, :, :, :LANES] = q_ref[0, :, :, :LANES]
    upper = with_offset(q[:, LANES:].astype(F32), -offset)
    full_ref[0, :, :, LANES:] = upper.astype(BF16).reshape(state_ref.shape[1:])


def with_offset(upper, offset):
    lane = lane_index(upper.shape)
    offset = jnp.broadcast_to(offset, upper.shape)
    coarse = offset.astype(BF16).astype(F32)
    middle = (offset - coarse).astype(BF16).astype(F32)
    for place, term in enumerate((coarse, middle, offset - coarse - middle)):
        upper = jnp.where(lane == HEAD_DIM + place, term, upper)
    return upper


def next_kernel(q_ref, state_ref, *refs):
    *blocks, before_ref, out_ref, mark_ref = refs
    mark_ref[...] = before_ref[...]
    rows = 2 * q_ref.shape[2]
    q = q_ref[0].reshape(rows, 2 * LANES)
    keys, values = wide_keys(jnp.concatenate([rows_of(ref) for ref in blocks], axis=0))
    state = weighted(scores_of(q, keys), values)
    out_ref[0] = state_ref[0] + state.reshape(out_ref.shape[1:])


def last_kernel(count, valid_ref, q_ref, state_ref, block_ref, first_text_ref, text_ref, *refs):
    kept, out_ref, done_ref, top_ref, spare_ref, sem = refs[:count], *refs[count:]
    head = pl.program_id(0)
    tile = q_ref.shape[2]
    rows = 2 * tile
    lane = lane_index((rows, LANES))
    q = q_ref[0].reshape(rows, 2 * LANES)
    keys, values = wide_keys(rows_of(block_ref))
    more_keys, more_values = wide_keys(text_ref[0], valid_ref[0] - first_text_ref.shape[1])
    scores = scores_of(q, jnp.concatenate([keys, more_keys], axis=0))
    state = weighted(scores, jnp.concatenate([values, more_values], axis=0))
    state = state + state_ref[0].reshape(rows, LANES)
    done_ref[head] = state
    top_ref[head] = q[:, LANES:].astype(F32)
    largest = jnp.max(jnp.where(state[:, :HEAD_DIM] < SAFE, 0.0, 1.0))

    @pl.when(largest > 0.0)
    def _():
        for at, ref in enumerate(kept):
            copy = pltpu.make_async_copy(ref.at[:, head], spare_ref.at[at], sem)
            copy.start()
            copy.wait()
        spare_ref[count] = block_ref[:, 0]
        spared = (lane >= HEAD_DIM) & (lane < GUARD)
        upper = jnp.where(spared, 0.0, q[:, LANES:].astype(F32)).astype(BF16)
        plain = jnp.concatenate([q[:, :LANES], upper], axis=1)

        def absorb(keys, values, largest, state):
            scores = scores_of(plain, keys)
            higher = jnp.maximum(largest, jnp.max(scores, axis=1, keepdims=True))
            return higher, state * jnp.exp2(largest - higher) + weighted(scores - higher, values)

        def step(at, carry):
            return absorb(*wide_keys(spare_ref[at].reshape(-1, LANES)), *carry)

        carry = (jnp.full((rows, 1), -1e30, F32), jnp.zeros((rows, LANES), F32))
        carry = lax.fori_loop(0, count + 1, step, carry)
        carry = absorb(*wide_keys(first_text_ref[0], valid_ref[0]), *carry)
        tail = wide_keys(text_ref[0], valid_ref[0] - first_text_ref.shape[1])
        largest, state = absorb(*tail, *carry)
        done_ref[head] = state
        top_ref[head] = with_offset(jnp.zeros((rows, LANES), F32), -largest)

    @pl.when(head == pl.num_programs(0) - 1)
    def _():
        marks = jnp.zeros((rows, LANES), F32)
        done = []
        for h in range(done_ref.shape[0]):
            state = done_ref[h]
            total = pltpu.roll(state, HEAD_DIM, 1)
            done.append(state / total)
            terms = top_ref[h] if h == 0 else pltpu.roll(top_ref[h], MARKS * h, 1)
            place = HEAD_DIM + MARKS * h
            lead = total.astype(BF16).astype(F32)
            marks = jnp.where((lane >= place) & (lane < place + 3), terms, marks)
            marks = jnp.where(lane == place + 3, lead, marks)
            marks = jnp.where(lane == place + 4, total - lead, marks)
        low = lane < HEAD_DIM
        left = jnp.where(low, pltpu.roll(done[0], HEAD_DIM, 1), done[1]).astype(BF16)
        right = jnp.where(low, pltpu.roll(done[2], HEAD_DIM, 1), marks).astype(BF16)
        for half in range(2):
            part = slice(half * tile, (half + 1) * tile)
            out_ref[:, 2 * half * LANES : (2 * half + 1) * LANES] = left[part]
            out_ref[:, (2 * half + 1) * LANES : (2 * half + 2) * LANES] = right[part]


def attention_call(kernel, name, operands, kept, out_shape, scratch=(), aliases=()):
    heads = next(x.shape[0] for x in operands if x.ndim == 4)

    def by_head(x):
        if x.ndim == 1:
            return pl.BlockSpec(memory_space=pltpu.SMEM)
        axis = 1 if x.ndim == 4 and x.shape[0] != heads else 0 if x.ndim > 2 else None
        block = tuple(1 if d == axis else n for d, n in enumerate(x.shape))
        return pl.BlockSpec(block, lambda h: tuple(h if d == axis else 0 for d in range(x.ndim)))

    specs = [by_head(x) for x in operands] + [pl.BlockSpec(memory_space=pltpu.HBM)] * len(kept)
    return pl.pallas_call(
        kernel,
        grid=(heads,),
        out_shape=out_shape,
        in_specs=specs,
        out_specs=[by_head(x) for x in out_shape],
        scratch_shapes=scratch,
        input_output_aliases=dict(aliases),
        compiler_params=params(24),
        cost_estimate=pl.CostEstimate(flops=4 * 10**9, bytes_accessed=8 * 10**6, transcendentals=3 * 10**6),
        name=name,
    )(*operands, *kept)


MARK = jax.ShapeDtypeStruct((8, LANES), F32)


def state_shape(q):
    return jax.ShapeDtypeStruct(q.shape[:3] + (LANES,), F32)


def first_block(valid, q, block, text):
    shapes = [jax.ShapeDtypeStruct(q.shape, BF16), state_shape(q), MARK]
    return attention_call(first_kernel, "own_block", [valid, q, block, text], [], shapes)


def next_blocks(q, state, blocks, mark):
    operands = [q, state, *blocks, mark]
    return attention_call(next_kernel, "next_blocks", operands, [], [state_shape(q), MARK], aliases=[(1, 0)])


def last_block(valid, q, state, block, first_text, text, kept):
    heads, _, rows, _ = q.shape
    shape = jax.ShapeDtypeStruct((rows, 4 * LANES), BF16)
    scratch = [
        pltpu.VMEM((heads, 2 * rows, LANES), F32),
        pltpu.VMEM((heads, 2 * rows, LANES), F32),
        pltpu.VMEM((len(kept) + 1, block.shape[0]) + block.shape[2:], BF16),
        pltpu.SemaphoreType.DMA,
    ]
    operands = [valid, q, state, block, first_text, text]
    return attention_call(functools.partial(last_kernel, len(kept)), "last_block", operands, kept, [shape], scratch)[0]


def finish_kernel(
    heads,
    groups,
    partial_ref,
    weight_ref,
    hidden_ref,
    modulation_ref,
    bias_ref,
    final_ref,
    final_bias_ref,
    out_ref,
    wide_ref,
    held_ref,
    input_ref,
    sems,
):
    brought = pltpu.make_async_copy(weight_ref, held_ref, sems.at[0])
    taken = pltpu.make_async_copy(hidden_ref, input_ref, sems.at[1])
    brought.start()
    taken.start()
    half = partial_ref.shape[1]
    sources = partial_ref.shape[0]
    across = groups // 2
    copies = sources // groups
    width = heads * HEAD_DIM
    low = lane_index((half, LANES)) < HEAD_DIM
    for part in range(2):
        at = part * 2 * LANES
        for group in range(groups):
            zl, y = divmod(group, across)
            members = [(zl * copies + copy) * across + y for copy in range(copies)]
            left = [partial_ref[m, :, at : at + LANES].astype(F32) for m in members]
            right = [partial_ref[m, :, at + LANES : at + 2 * LANES].astype(F32) for m in members]
            levels = [-(r + pltpu.roll(r, LANES - 1, 1) + pltpu.roll(r, LANES - 2, 1)) for r in right]
            counts = [pltpu.roll(r, LANES - 3, 1) + pltpu.roll(r, LANES - 4, 1) for r in right]
            top = functools.reduce(jnp.maximum, levels)
            shares = [count * jnp.exp2(level - top) for count, level in zip(counts, levels)]
            total = functools.reduce(jnp.add, shares)
            first, second = 0.0, 0.0
            for copy in range(copies):
                share = shares[copy] / total
                h0, h1, h2 = [share[:, c : c + 1] for c in (HEAD_DIM, HEAD_DIM + MARKS, HEAD_DIM + 2 * MARKS)]
                first = first + left[copy] * jnp.where(low, h0, h1)
                second = second + right[copy] * h2
            both = jnp.concatenate([first, second[:, :HEAD_DIM]], axis=1)
            wide_ref[part * half : (part + 1) * half, group * width : (group + 1) * width] = both
    attended = wide_ref[...].astype(BF16)
    brought.wait()
    taken.wait()
    projected = jnp.dot(attended, held_ref[...], preferred_element_type=F32)
    residual = input_ref[...].astype(F32) + modulation_ref[0:1] * (projected + bias_ref[...])
    middle = jnp.mean(residual, axis=-1, keepdims=True)
    centered = residual - middle
    spread = jnp.mean(centered * centered, axis=-1, keepdims=True)
    normed = centered * lax.rsqrt(spread + 1e-06) * (1.0 + modulation_ref[1:2]) + modulation_ref[2:3]
    velocity = lax.dot_general(
        normed.astype(BF16), final_ref[...], (((1,), (1,)), ((), ())), preferred_element_type=F32
    )
    out_ref[...] = velocity + final_bias_ref[...]


def finish(partial, weight, hidden, modulation, bias, final_weight, final_bias, heads, groups):
    tokens, width = hidden.shape
    vmem = pl.BlockSpec(memory_space=pltpu.VMEM)
    hbm = pl.BlockSpec(memory_space=pltpu.HBM)
    return pl.pallas_call(
        functools.partial(finish_kernel, heads, groups),
        out_shape=jax.ShapeDtypeStruct((tokens, final_weight.shape[0]), F32),
        in_specs=[vmem, hbm, hbm, vmem, vmem, vmem, vmem],
        out_specs=vmem,
        scratch_shapes=[
            pltpu.VMEM((tokens, width), F32),
            pltpu.VMEM(weight.shape, BF16),
            pltpu.VMEM(hidden.shape, BF16),
            pltpu.SemaphoreType.DMA((2,)),
        ],
        compiler_params=params(60),
        name="project_and_norm",
    )(partial, weight, hidden, modulation, bias, final_weight, final_bias)


def local(
    latent_qkv,
    text_kv,
    hidden_in,
    modulation,
    out_weight,
    out_bias,
    proj_weight,
    proj_bias,
    guidance,
    sigma,
    sample,
):
    groups = lax.axis_size("zl") * lax.axis_size("y")
    ring = lax.axis_size("zh")
    tokens = latent_qkv.shape[1]
    half = tokens // 2
    width = latent_qkv.shape[3] // groups
    heads = width // HEAD_DIM
    across = lax.axis_size("y")
    zl, core, xh, y = (lax.axis_index(a) for a in ("zl", "core", "xh", "y"))
    after = lax.optimization_barrier

    slabs = pack(latent_qkv[0].transpose(1, 0, 2), groups, heads)
    slabs = lax.all_to_all(slabs, HEAD_AXES, split_axis=0, concat_axis=0, tiled=True)
    packed = slabs[:, : heads * half].reshape(groups, heads, half, LANES)
    packed = lax.all_gather(packed, "core", axis=0)
    own, packed = after((slabs[:, heads * half :].reshape(groups, heads, tokens, LANES), packed))
    route = []
    for i in range(ring):
        route += [(2 * i, 2 * ((i + 1) % ring)), (2 * i + 1, 2 * ((i - 1) % ring) + 1)]
    pass_on = lambda x: lax.ppermute(x, ("zh", "core"), route)
    beside = lax.ppermute(own, "core", [(0, 1), (1, 0)])
    first, beside = after((own, beside))
    near = pass_on(first)
    opposite = lax.ppermute(packed, "xh", [(0, 1), (1, 0)])
    cross = pass_on(beside)
    q = unpack_queries(xh.reshape(1), packed, opposite)

    weight = lax.all_gather(out_weight, ("xh", "y"), axis=0, tiled=True)

    count = text_kv.shape[1]
    share = -(-count // 32) * 16
    text = text_kv[0].reshape(count, 2, heads, HEAD_DIM).transpose(2, 0, 1, 3).reshape(heads, count, LANES)
    text = jnp.pad(text, ((0, 0), (0, 2 * share - count), (0, 0)))
    text = lax.dynamic_slice_in_dim(text, core * share, share, 1)
    valid = jnp.where(xh == zl, jnp.minimum(count - core * share, share), 0).reshape(1)
    early, late = text[:, :LANES], text[:, LANES:]
    q, state, mark = first_block(valid, q, own, early)
    kept = [own, near, cross]
    for step in range(ring // 2 - 2):
        if step:
            near, mark = after((near, mark))
        nearer = pass_on(near)
        cross, mark = after((cross, mark))
        crosser = pass_on(cross)
        state, mark = next_blocks(q, state, [near, cross], mark)
        near, cross = nearer, crosser
        kept += [near, cross]
    near, mark = after((near, mark))
    farthest = pass_on(near)
    state, mark = next_blocks(q, state, [near, cross], mark)
    partial = last_block(valid, q, state, farthest, early, late, kept)
    partial = partial.reshape(4 * groups, half, 4 * LANES)
    partial = lax.all_to_all(partial, BLOCK_AXES, split_axis=0, concat_axis=0, tiled=True)

    velocity = finish(
        partial,
        weight,
        hidden_in[0],
        modulation[0],
        out_bias[None],
        proj_weight.T,
        proj_bias[None],
        heads,
        groups,
    )

    tiles = velocity.reshape(tokens, 2, -1).transpose(1, 0, 2).reshape(2, -1)
    branch, parity = lax.axis_index("cfg"), y % 2
    same, swap = [], []
    for s in range(2):
        for y in range(across):
            a = y % 2
            same.append((s * across + y, a * across + y - a + s))
            swap.append((s * across + y, a * across + y - a + 1 - s))
    kept = lax.ppermute(lax.dynamic_slice_in_dim(tiles, branch, 1, 0), ("cfg", "y"), same)
    crossed = lax.ppermute(lax.dynamic_slice_in_dim(tiles, 1 - branch, 1, 0), ("cfg", "y"), swap)
    conditional = jnp.where(parity == 0, kept, crossed)
    unconditional = jnp.where(parity == 0, crossed, kept)
    guided = unconditional + guidance[0] * (conditional - unconditional)
    denoised = sample - sigma[0] * guided
    return (guided, denoised)


def solution(mesh):
    sizes = dict(zip(mesh.axis_names, mesh.devices.shape))
    ring = sizes["blk"] // 4
    fine = Mesh(
        mesh.devices.reshape(sizes["cfg"], ring, 2, 2, 2, sizes["uly"] // 2),
        ("cfg", "zh", "zl", "core", "xh", "y"),
    )
    rows = ("zh", "zl", "core", "xh", "y")
    heads = ("xh", "y")
    return jax.shard_map(
        local,
        mesh=fine,
        in_specs=(
            P("cfg", rows, None, None),
            P("cfg", None, None, heads),
            P("cfg", rows, None),
            P("cfg", None, None),
            P(heads, None),
            P(),
            P(),
            P(),
            P(),
            P(),
            P(rows, "cfg"),
        ),
        out_specs=(P(rows, "cfg"), P(rows, "cfg")),
        check_vma=False,
    )
```

```python
import functools
import math

import jax
import jax.numpy as jnp
from jax import lax
from jax.experimental import pallas as pl
from jax.experimental.pallas import tpu as pltpu
from jax.sharding import Mesh, PartitionSpec as P

HEAD_DIM = 64
LANES = 128
ROW_TILE = 768
LOG2_SCALE = math.log2(math.e) * HEAD_DIM**-0.5
F32 = jnp.float32
BF16 = jnp.bfloat16
GUARD = HEAD_DIM + 3
MARKS = 8
SAFE = 2.0**100
HEAD_AXES = ("zl", "y")
BLOCK_AXES = ("zl", "core", "xh", "y")


def params(mib=32):
    return pltpu.CompilerParams(vmem_limit_bytes=mib * 1024 * 1024)


def lane_index(shape):
    return lax.broadcasted_iota(jnp.int32, shape, len(shape) - 1)


def pack_kernel(groups, heads, x_ref, out_ref):
    rows = x_ref.shape[1]
    half = rows // 2
    for group in range(groups):
        queries, pairs = [], []
        for head in range(heads):
            start = (group * heads + head) * HEAD_DIM
            cols = slice(start, start + HEAD_DIM)
            q = x_ref[0, :, cols].astype(F32)
            k = x_ref[1, :, cols].astype(F32)
            v = x_ref[2, :, cols].astype(F32)
            queries.append(jnp.concatenate([q[:half], q[half:]], axis=1))
            pairs.append(jnp.concatenate([k, v], axis=1))
        out_ref[group] = jnp.concatenate(queries + pairs, axis=0).astype(BF16)


def pack(x, groups, heads):
    rows = x.shape[1]
    return pl.pallas_call(
        functools.partial(pack_kernel, groups, heads),
        out_shape=jax.ShapeDtypeStruct((groups, heads * (rows // 2 + rows), LANES), BF16),
        compiler_params=params(),
        name="pack_heads",
    )(x)


def wide_keys(block, valid=None):
    lane = lane_index(block.shape)
    ones = jnp.ones_like(block)
    marked = jnp.where(lane < HEAD_DIM, block, ones)
    if valid is not None:
        row = lax.broadcasted_iota(jnp.int32, block.shape, 0)
        marked = jnp.where((lane == GUARD) & (row >= valid), jnp.full_like(block, -1e30), marked)
    return jnp.concatenate([block, marked], axis=1), jnp.where(lane < HEAD_DIM, ones, block)


def queries_kernel(heads, place_ref, own_ref, other_ref, out_ref, wide_ref):
    here = place_ref[0]
    cores, sources, _, half, _ = own_ref.shape
    across = sources // 2
    lane = lane_index((half, LANES))
    low = lane < HEAD_DIM
    guard = jnp.where(lane == GUARD, 1.0, 0.0)
    for side, ref in ((here, own_ref), (1 - here, other_ref)):
        for core in range(cores):
            for source in range(sources):
                zl, y = divmod(source, across)
                first = (zl * cores + core) * 2 * across + y
                row = pl.multiple_of((first + side * across) * half, 8)
                for head in range(heads):
                    both = ref[core, source, head].astype(F32) * LOG2_SCALE
                    for part, value in enumerate((both, pltpu.roll(both, HEAD_DIM, 1))):
                        lead = value.astype(BF16).astype(F32)
                        wide_ref[head, part, pl.ds(row, half), 0:LANES] = jnp.where(low, lead, 0.0)
                        wide_ref[head, part, pl.ds(row, half), LANES:] = jnp.where(low, value - lead, guard)
    out_ref[...] = wide_ref[...].astype(BF16)


def unpack_queries(place, own, other):
    cores, sources, heads, half, _ = own.shape
    shape = (heads, 2, 2 * cores * sources * half, 2 * LANES)
    return pl.pallas_call(
        functools.partial(queries_kernel, heads),
        out_shape=jax.ShapeDtypeStruct(shape, BF16),
        in_specs=[
            pl.BlockSpec(memory_space=pltpu.SMEM),
            pl.BlockSpec(memory_space=pltpu.VMEM),
            pl.BlockSpec(memory_space=pltpu.VMEM),
        ],
        out_specs=pl.BlockSpec(memory_space=pltpu.VMEM),
        scratch_shapes=[pltpu.VMEM(shape, F32)],
        compiler_params=params(),
        name="unpack_queries",
    )(place, own, other)


def rows_of(ref, head):
    return ref[:, head].reshape(-1, ref.shape[-1])


def scores_of(q, keys):
    return lax.dot_general(q, keys, (((1,), (1,)), ((), ())), preferred_element_type=F32)


def weighted(scores, values):
    return jnp.dot(jnp.exp2(scores).astype(BF16), values, preferred_element_type=F32)


def first_kernel(heads, valid_ref, q_ref, block_ref, text_ref, full_ref, state_ref, mark_ref):
    mark_ref[...] = jnp.zeros_like(mark_ref)
    rows = 2 * q_ref.shape[2]
    lane = lane_index((rows, LANES))
    for head in range(heads):
        q = q_ref[head].reshape(rows, 2 * LANES)
        keys, values = wide_keys(rows_of(block_ref, head))
        more_keys, more_values = wide_keys(text_ref[head], valid_ref[0])
        scores = scores_of(q, jnp.concatenate([keys, more_keys], axis=0))
        offset = jnp.max(scores, axis=1, keepdims=True)
        state = weighted(scores - offset, jnp.concatenate([values, more_values], axis=0))
        state_ref[head] = state.reshape(state_ref.shape[1:])
        offset = jnp.broadcast_to(-offset, (rows, LANES))
        coarse = offset.astype(BF16).astype(F32)
        middle = (offset - coarse).astype(BF16).astype(F32)
        upper = q[:, LANES:].astype(F32)
        for place, term in enumerate((coarse, middle, offset - coarse - middle)):
            upper = jnp.where(lane == HEAD_DIM + place, term, upper)
        full_ref[head, :, :, :LANES] = q_ref[head, :, :, :LANES]
        full_ref[head, :, :, LANES:] = upper.astype(BF16).reshape(state_ref.shape[1:])


def next_kernel(q_ref, state_ref, *refs):
    *blocks, before_ref, out_ref, mark_ref = refs
    mark_ref[...] = before_ref[...]
    rows = 2 * q_ref.shape[2]
    q = q_ref[0].reshape(rows, 2 * LANES)
    keys, values = wide_keys(jnp.concatenate([rows_of(ref, 0) for ref in blocks], axis=0))
    state = weighted(scores_of(q, keys), values)
    out_ref[0] = state_ref[0] + state.reshape(out_ref.shape[1:])


def last_kernel(heads, count, valid_ref, q_ref, state_ref, block_ref, first_text_ref, text_ref, *refs):
    kept, out_ref, done_ref, top_ref, spare_ref, sem = refs[:count], *refs[count:]
    tile = q_ref.shape[2]
    rows = 2 * tile
    lane = lane_index((rows, LANES))
    safe = True
    for head in range(heads):
        q = q_ref[head].reshape(rows, 2 * LANES)
        keys, values = wide_keys(rows_of(block_ref, head))
        more_keys, more_values = wide_keys(text_ref[head], valid_ref[0] - first_text_ref.shape[1])
        scores = scores_of(q, jnp.concatenate([keys, more_keys], axis=0))
        state = weighted(scores, jnp.concatenate([values, more_values], axis=0))
        state = state + state_ref[head].reshape(rows, LANES)
        done_ref[head] = state
        top_ref[head] = q[:, LANES:].astype(F32)
        largest = jnp.max(jnp.where(state[:, :HEAD_DIM] < SAFE, 0.0, 1.0))
        safe = jnp.logical_and(safe, largest == 0.0)

    @pl.when(jnp.logical_not(safe))
    def _():
        for at, ref in enumerate(kept):
            copy = pltpu.make_async_copy(ref, spare_ref.at[at], sem)
            copy.start()
            copy.wait()
        spare_ref[count] = block_ref[...]
        for head in range(heads):
            q = q_ref[head].reshape(rows, 2 * LANES)
            spared = (lane >= HEAD_DIM) & (lane < GUARD)
            plain = jnp.concatenate([q[:, :LANES], jnp.where(spared, jnp.zeros_like(q[:, LANES:]), q[:, LANES:])], axis=1)

            def absorb(keys, values, largest, state):
                scores = scores_of(plain, keys)
                higher = jnp.maximum(largest, jnp.max(scores, axis=1, keepdims=True))
                return higher, state * jnp.exp2(largest - higher) + weighted(scores - higher, values)

            def step(at, carry):
                return absorb(*wide_keys(spare_ref[at, :, head].reshape(-1, LANES)), *carry)

            carry = (jnp.full((rows, 1), -1e30, F32), jnp.zeros((rows, LANES), F32))
            carry = lax.fori_loop(0, count + 1, step, carry)
            carry = absorb(*wide_keys(first_text_ref[head], valid_ref[0]), *carry)
            tail = wide_keys(text_ref[head], valid_ref[0] - first_text_ref.shape[1])
            largest, state = absorb(*tail, *carry)
            done_ref[head] = state
            offset = jnp.broadcast_to(-largest, (rows, LANES))
            coarse = offset.astype(BF16).astype(F32)
            middle = (offset - coarse).astype(BF16).astype(F32)
            upper = jnp.zeros((rows, LANES), F32)
            for place, term in enumerate((coarse, middle, offset - coarse - middle)):
                upper = jnp.where(lane == HEAD_DIM + place, term, upper)
            top_ref[head] = upper

    marks = jnp.zeros((rows, LANES), F32)
    done = []
    for head in range(heads):
        state = done_ref[head]
        total = pltpu.roll(state, HEAD_DIM, 1)
        done.append(state / total)
        terms = top_ref[head] if head == 0 else pltpu.roll(top_ref[head], MARKS * head, 1)
        place = HEAD_DIM + MARKS * head
        lead = total.astype(BF16).astype(F32)
        marks = jnp.where((lane >= place) & (lane < place + 3), terms, marks)
        marks = jnp.where(lane == place + 3, lead, marks)
        marks = jnp.where(lane == place + 4, total - lead, marks)
    low = lane < HEAD_DIM
    left = jnp.where(low, pltpu.roll(done[0], HEAD_DIM, 1), done[1]).astype(BF16)
    right = jnp.where(low, pltpu.roll(done[2], HEAD_DIM, 1), marks).astype(BF16)
    for half in range(2):
        part = slice(half * tile, (half + 1) * tile)
        out_ref[:, 2 * half * LANES : (2 * half + 1) * LANES] = left[part]
        out_ref[:, (2 * half + 1) * LANES : (2 * half + 2) * LANES] = right[part]


def attention_call(kernel, name, operands, whole, kept, out_shape, out_axes, scratch=()):
    q = operands[-1] if len(operands[-1].shape) == 4 and operands[-1].dtype == BF16 else operands[-2]
    heads, _, rows, _ = q.shape
    tile = ROW_TILE if rows % ROW_TILE == 0 else rows

    def tiled(shape, axis):
        if axis is None:
            return pl.BlockSpec(shape, lambda i: (0,) * len(shape))
        block = tuple(tile if d == axis else n for d, n in enumerate(shape))
        return pl.BlockSpec(block, lambda i: tuple(i if d == axis else 0 for d in range(len(shape))))

    specs = []
    for x in operands:
        specs.append(tiled(x.shape, 2) if x.ndim == 4 else pl.BlockSpec(memory_space=pltpu.SMEM))
    for x in whole:
        specs.append(pl.BlockSpec(x.shape, lambda i, n=x.ndim: (0,) * n))
    specs += [pl.BlockSpec(memory_space=pltpu.HBM)] * len(kept)
    keys = sum(x.size // (heads * LANES) for x in whole)
    pairs = heads * 2 * rows * keys
    out_specs = [tiled(s.shape, a) for s, a in zip(out_shape, out_axes)]
    return pl.pallas_call(
        kernel,
        grid=(rows // tile,),
        out_shape=out_shape,
        in_specs=specs,
        out_specs=out_specs,
        scratch_shapes=scratch,
        compiler_params=params(),
        cost_estimate=pl.CostEstimate(flops=pairs * 6 * LANES, bytes_accessed=4 * q.size, transcendentals=pairs),
        name=name,
    )(*operands, *whole, *kept)


def state_shape(q):
    return jax.ShapeDtypeStruct(q.shape[:3] + (LANES,), F32)


MARK = jax.ShapeDtypeStruct((8, LANES), F32)


def first_block(valid, q, block, text):
    shapes = [jax.ShapeDtypeStruct(q.shape, BF16), state_shape(q), MARK]
    kernel = functools.partial(first_kernel, q.shape[0])
    return attention_call(kernel, "own_block", [valid, q], [block, text], [], shapes, [2, 2, None])


def next_blocks(q, state, blocks, mark):
    heads, _, rows, _ = q.shape
    step = lambda x: pl.BlockSpec((1,) + x.shape[1:], lambda h: (h, 0, 0, 0))
    block_step = lambda x: pl.BlockSpec((x.shape[0], 1) + x.shape[2:], lambda h: (0, h, 0, 0))
    mark_spec = pl.BlockSpec(mark.shape, lambda h: (0, 0))
    pairs = heads * 2 * rows * sum(x.size // (heads * LANES) for x in blocks)
    return pl.pallas_call(
        next_kernel,
        grid=(heads,),
        out_shape=[state_shape(q), MARK],
        in_specs=[step(q), step(state), *map(block_step, blocks), mark_spec],
        out_specs=[step(state), mark_spec],
        input_output_aliases={1: 0},
        compiler_params=params(16),
        cost_estimate=pl.CostEstimate(flops=pairs * 6 * LANES, bytes_accessed=4 * q.size, transcendentals=pairs),
        name="next_blocks",
    )(q, state, *blocks, mark)


def last_block(valid, q, state, block, first_text, text, kept):
    heads, _, rows, _ = q.shape
    tile = ROW_TILE if rows % ROW_TILE == 0 else rows
    kernel = functools.partial(last_kernel, heads, len(kept))
    shape = jax.ShapeDtypeStruct((rows, 4 * LANES), BF16)
    scratch = [
        pltpu.VMEM((heads, 2 * tile, LANES), F32),
        pltpu.VMEM((heads, 2 * tile, LANES), F32),
        pltpu.VMEM((len(kept) + 1,) + block.shape, BF16),
        pltpu.SemaphoreType.DMA,
    ]
    return attention_call(kernel, "last_block", [valid, q, state], [block, first_text, text], kept, [shape], [0], scratch)[0]


def finish_kernel(
    heads,
    groups,
    partial_ref,
    weight_ref,
    hidden_ref,
    modulation_ref,
    bias_ref,
    final_ref,
    final_bias_ref,
    out_ref,
    wide_ref,
):
    half = partial_ref.shape[1]
    sources = partial_ref.shape[0]
    across = groups // 2
    copies = sources // groups
    width = heads * HEAD_DIM
    low = lane_index((half, LANES)) < HEAD_DIM
    for part in range(2):
        at = part * 2 * LANES
        for group in range(groups):
            zl, y = divmod(group, across)
            members = [(zl * copies + copy) * across + y for copy in range(copies)]
            left = [partial_ref[m, :, at : at + LANES].astype(F32) for m in members]
            right = [partial_ref[m, :, at + LANES : at + 2 * LANES].astype(F32) for m in members]
            levels = [-(r + pltpu.roll(r, LANES - 1, 1) + pltpu.roll(r, LANES - 2, 1)) for r in right]
            counts = [pltpu.roll(r, LANES - 3, 1) + pltpu.roll(r, LANES - 4, 1) for r in right]
            top = functools.reduce(jnp.maximum, levels)
            shares = [count * jnp.exp2(level - top) for count, level in zip(counts, levels)]
            total = functools.reduce(jnp.add, shares)
            first, second = 0.0, 0.0
            for copy in range(copies):
                share = shares[copy] / total
                h0, h1, h2 = [share[:, c : c + 1] for c in (HEAD_DIM, HEAD_DIM + MARKS, HEAD_DIM + 2 * MARKS)]
                first = first + left[copy] * jnp.where(low, h0, h1)
                second = second + right[copy] * h2
            both = jnp.concatenate([first, second[:, :HEAD_DIM]], axis=1)
            wide_ref[part * half : (part + 1) * half, group * width : (group + 1) * width] = both
    attended = wide_ref[...].astype(BF16)
    projected = jnp.concatenate(
        [jnp.dot(attended, weight_ref[side], preferred_element_type=F32) for side in range(2)], axis=1
    )
    residual = hidden_ref[...].astype(F32) + modulation_ref[0:1] * (projected + bias_ref[...])
    middle = jnp.mean(residual, axis=-1, keepdims=True)
    centered = residual - middle
    spread = jnp.mean(centered * centered, axis=-1, keepdims=True)
    normed = centered * lax.rsqrt(spread + 1e-06) * (1.0 + modulation_ref[1:2]) + modulation_ref[2:3]
    velocity = lax.dot_general(
        normed.astype(BF16), final_ref[...], (((1,), (1,)), ((), ())), preferred_element_type=F32
    )
    out_ref[...] = velocity + final_bias_ref[...]


def finish(partial, weight, hidden, modulation, bias, final_weight, final_bias, heads, groups):
    tokens, width = hidden.shape
    return pl.pallas_call(
        functools.partial(finish_kernel, heads, groups),
        out_shape=jax.ShapeDtypeStruct((tokens, final_weight.shape[0]), F32),
        scratch_shapes=[pltpu.VMEM((tokens, width), F32)],
        compiler_params=params(16),
        name="project_and_norm",
    )(partial, weight, hidden, modulation, bias, final_weight, final_bias)


def local(
    latent_qkv,
    text_kv,
    hidden_in,
    modulation,
    out_weight,
    out_bias,
    proj_weight,
    proj_bias,
    guidance,
    sigma,
    sample,
):
    groups = lax.axis_size("zl") * lax.axis_size("y")
    ring = lax.axis_size("zh")
    tokens = latent_qkv.shape[1]
    half = tokens // 2
    width = latent_qkv.shape[3] // groups
    heads = width // HEAD_DIM
    across = lax.axis_size("y")
    zl, core, xh, y = (lax.axis_index(a) for a in ("zl", "core", "xh", "y"))
    after = lax.optimization_barrier

    slabs = pack(latent_qkv[0].transpose(1, 0, 2), groups, heads)
    slabs = lax.all_to_all(slabs, HEAD_AXES, split_axis=0, concat_axis=0, tiled=True)
    packed = slabs[:, : heads * half].reshape(groups, heads, half, LANES)
    packed = lax.all_gather(packed, "core", axis=0)
    own, packed = after((slabs[:, heads * half :].reshape(groups, heads, tokens, LANES), packed))
    route = []
    for i in range(ring):
        route += [(2 * i, 2 * ((i + 1) % ring)), (2 * i + 1, 2 * ((i - 1) % ring) + 1)]
    pass_on = lambda x: lax.ppermute(x, ("zh", "core"), route)
    near = pass_on(own)
    beside = lax.ppermute(own, "core", [(0, 1), (1, 0)])
    opposite = lax.ppermute(packed, "xh", [(0, 1), (1, 0)])
    cross = pass_on(beside)
    q = unpack_queries(xh.reshape(1), packed, opposite)

    columns = out_weight.shape[1] // 2
    piece = lax.dynamic_slice_in_dim(out_weight, core * columns, columns, 1)
    weight = lax.all_gather(piece, ("core", "xh", "y"), axis=0, tiled=True).reshape(2, groups * width, columns)

    count = text_kv.shape[1]
    share = -(-count // 32) * 16
    text = text_kv[0].reshape(count, 2, heads, HEAD_DIM).transpose(2, 0, 1, 3).reshape(heads, count, LANES)
    text = jnp.pad(text, ((0, 0), (0, 2 * share - count), (0, 0)))
    text = lax.dynamic_slice_in_dim(text, core * share, share, 1)
    valid = jnp.where(xh == zl, jnp.minimum(count - core * share, share), 0).reshape(1)
    early, late = text[:, :LANES], text[:, LANES:]
    q, state, mark = first_block(valid, q, own, early)
    kept = [own, near, cross]
    for step in range(ring // 2 - 2):
        if step:
            near, mark = after((near, mark))
        nearer = pass_on(near)
        cross, mark = after((cross, mark))
        crosser = pass_on(cross)
        state, mark = next_blocks(q, state, [near, cross], mark)
        near, cross = nearer, crosser
        kept += [near, cross]
    near, mark = after((near, mark))
    farthest = pass_on(near)
    state, mark = next_blocks(q, state, [near, cross], mark)
    partial = last_block(valid, q, state, farthest, early, late, kept)
    partial, weight = after((partial.reshape(4 * groups, half, 4 * LANES), weight))
    partial = lax.all_to_all(partial, BLOCK_AXES, split_axis=0, concat_axis=0, tiled=True)

    velocity = finish(
        partial,
        weight,
        hidden_in[0],
        modulation[0],
        out_bias[None],
        proj_weight.T,
        proj_bias[None],
        heads,
        groups,
    )

    tiles = velocity.reshape(tokens, 2, -1).transpose(1, 0, 2).reshape(2, -1)
    branch, parity = lax.axis_index("cfg"), y % 2
    same, swap = [], []
    for s in range(2):
        for y in range(across):
            a = y % 2
            same.append((s * across + y, a * across + y - a + s))
            swap.append((s * across + y, a * across + y - a + 1 - s))
    kept = lax.ppermute(lax.dynamic_slice_in_dim(tiles, branch, 1, 0), ("cfg", "y"), same)
    crossed = lax.ppermute(lax.dynamic_slice_in_dim(tiles, 1 - branch, 1, 0), ("cfg", "y"), swap)
    conditional = jnp.where(parity == 0, kept, crossed)
    unconditional = jnp.where(parity == 0, crossed, kept)
    guided = unconditional + guidance[0] * (conditional - unconditional)
    denoised = sample - sigma[0] * guided
    return (guided, denoised)


def solution(mesh):
    sizes = dict(zip(mesh.axis_names, mesh.devices.shape))
    ring = sizes["blk"] // 4
    fine = Mesh(
        mesh.devices.reshape(sizes["cfg"], ring, 2, 2, 2, sizes["uly"] // 2),
        ("cfg", "zh", "zl", "core", "xh", "y"),
    )
    rows = ("zh", "zl", "core", "xh", "y")
    heads = ("xh", "y")
    return jax.shard_map(
        local,
        mesh=fine,
        in_specs=(
            P("cfg", rows, None, None),
            P("cfg", None, None, heads),
            P("cfg", rows, None),
            P("cfg", None, None),
            P(heads, None),
            P(),
            P(),
            P(),
            P(),
            P(),
            P(rows, "cfg"),
        ),
        out_specs=(P(rows, "cfg"), P(rows, "cfg")),
        check_vma=False,
    )
```

```python
import functools
import math

import jax
import jax.numpy as jnp
from jax import lax
from jax.experimental import pallas as pl
from jax.experimental.pallas import tpu as pltpu
from jax.sharding import Mesh, PartitionSpec as P

HEAD_DIM = 64
LANES = 128
LOG2_SCALE = math.log2(math.e) * HEAD_DIM**-0.5
F32 = jnp.float32
BF16 = jnp.bfloat16
GUARD = HEAD_DIM + 3
MARKS = 8
SAFE = 2.0**100
HEAD_AXES = ("zl", "y")
BLOCK_AXES = ("zl", "core", "xh", "y")


def params(mib=16):
    return pltpu.CompilerParams(vmem_limit_bytes=mib * 1024 * 1024)


def lane_index(shape):
    return lax.broadcasted_iota(jnp.int32, shape, len(shape) - 1)


def pack_kernel(groups, heads, x_ref, out_ref):
    rows = x_ref.shape[1]
    half = rows // 2
    for group in range(groups):
        queries, pairs = [], []
        for head in range(heads):
            start = (group * heads + head) * HEAD_DIM
            cols = slice(start, start + HEAD_DIM)
            q = x_ref[0, :, cols].astype(F32)
            k = x_ref[1, :, cols].astype(F32)
            v = x_ref[2, :, cols].astype(F32)
            queries.append(jnp.concatenate([q[:half], q[half:]], axis=1))
            pairs.append(jnp.concatenate([k, v], axis=1))
        out_ref[group] = jnp.concatenate(queries + pairs, axis=0).astype(BF16)


def pack(x, groups, heads):
    rows = x.shape[1]
    return pl.pallas_call(
        functools.partial(pack_kernel, groups, heads),
        out_shape=jax.ShapeDtypeStruct((groups, heads * (rows // 2 + rows), LANES), BF16),
        compiler_params=params(),
        name="pack_heads",
    )(x)


def wide_keys(block, valid=None):
    lane = lane_index(block.shape)
    ones = jnp.ones_like(block)
    marked = jnp.where(lane < HEAD_DIM, block, ones)
    if valid is not None:
        row = lax.broadcasted_iota(jnp.int32, block.shape, 0)
        marked = jnp.where((lane == GUARD) & (row >= valid), jnp.full_like(block, -1e30), marked)
    return jnp.concatenate([block, marked], axis=1), jnp.where(lane < HEAD_DIM, ones, block)


def queries_kernel(heads, place_ref, own_ref, other_ref, out_ref, wide_ref):
    here = place_ref[0]
    cores, sources, _, half, _ = own_ref.shape
    across = sources // 2
    lane = lane_index((half, LANES))
    low = lane < HEAD_DIM
    guard = jnp.where(lane == GUARD, 1.0, 0.0)
    for side, ref in ((here, own_ref), (1 - here, other_ref)):
        for core in range(cores):
            for source in range(sources):
                zl, y = divmod(source, across)
                first = (zl * cores + core) * 2 * across + y
                row = pl.multiple_of((first + side * across) * half, 8)
                for head in range(heads):
                    both = ref[core, source, head].astype(F32) * LOG2_SCALE
                    for part, value in enumerate((both, pltpu.roll(both, HEAD_DIM, 1))):
                        lead = value.astype(BF16).astype(F32)
                        wide_ref[head, part, pl.ds(row, half), 0:LANES] = jnp.where(low, lead, 0.0)
                        wide_ref[head, part, pl.ds(row, half), LANES:] = jnp.where(low, value - lead, guard)
    out_ref[...] = wide_ref[...].astype(BF16)


def unpack_queries(place, own, other):
    cores, sources, heads, half, _ = own.shape
    shape = (heads, 2, 2 * cores * sources * half, 2 * LANES)
    return pl.pallas_call(
        functools.partial(queries_kernel, heads),
        out_shape=jax.ShapeDtypeStruct(shape, BF16),
        in_specs=[
            pl.BlockSpec(memory_space=pltpu.SMEM),
            pl.BlockSpec(memory_space=pltpu.VMEM),
            pl.BlockSpec(memory_space=pltpu.VMEM),
        ],
        out_specs=pl.BlockSpec(memory_space=pltpu.VMEM),
        scratch_shapes=[pltpu.VMEM(shape, F32)],
        compiler_params=params(),
        name="unpack_queries",
    )(place, own, other)


def rows_of(ref):
    return ref[:, 0].reshape(-1, ref.shape[-1])


def scores_of(q, keys):
    return lax.dot_general(q, keys, (((1,), (1,)), ((), ())), preferred_element_type=F32)


def weighted(scores, values):
    return jnp.dot(jnp.exp2(scores).astype(BF16), values, preferred_element_type=F32)


def first_kernel(valid_ref, q_ref, block_ref, text_ref, full_ref, state_ref, mark_ref):
    rows = 2 * q_ref.shape[2]
    mark_ref[...] = jnp.zeros_like(mark_ref)
    q = q_ref[0].reshape(rows, 2 * LANES)
    keys, values = wide_keys(rows_of(block_ref))
    more_keys, more_values = wide_keys(text_ref[0], valid_ref[0])
    scores = scores_of(q, jnp.concatenate([keys, more_keys], axis=0))
    offset = jnp.max(scores, axis=1, keepdims=True)
    state = weighted(scores - offset, jnp.concatenate([values, more_values], axis=0))
    state_ref[0] = state.reshape(state_ref.shape[1:])
    full_ref[0, :, :, :LANES] = q_ref[0, :, :, :LANES]
    upper = with_offset(q[:, LANES:].astype(F32), -offset)
    full_ref[0, :, :, LANES:] = upper.astype(BF16).reshape(state_ref.shape[1:])


def with_offset(upper, offset):
    lane = lane_index(upper.shape)
    offset = jnp.broadcast_to(offset, upper.shape)
    coarse = offset.astype(BF16).astype(F32)
    middle = (offset - coarse).astype(BF16).astype(F32)
    for place, term in enumerate((coarse, middle, offset - coarse - middle)):
        upper = jnp.where(lane == HEAD_DIM + place, term, upper)
    return upper


def next_kernel(q_ref, state_ref, *refs):
    *blocks, before_ref, out_ref, mark_ref = refs
    mark_ref[...] = before_ref[...]
    rows = 2 * q_ref.shape[2]
    q = q_ref[0].reshape(rows, 2 * LANES)
    keys, values = wide_keys(jnp.concatenate([rows_of(ref) for ref in blocks], axis=0))
    state = weighted(scores_of(q, keys), values)
    out_ref[0] = state_ref[0] + state.reshape(out_ref.shape[1:])


def last_kernel(count, valid_ref, q_ref, state_ref, block_ref, first_text_ref, text_ref, *refs):
    kept, out_ref, done_ref, top_ref, spare_ref, sem = refs[:count], *refs[count:]
    head = pl.program_id(0)
    tile = q_ref.shape[2]
    rows = 2 * tile
    lane = lane_index((rows, LANES))
    q = q_ref[0].reshape(rows, 2 * LANES)
    keys, values = wide_keys(rows_of(block_ref))
    more_keys, more_values = wide_keys(text_ref[0], valid_ref[0] - first_text_ref.shape[1])
    scores = scores_of(q, jnp.concatenate([keys, more_keys], axis=0))
    state = weighted(scores, jnp.concatenate([values, more_values], axis=0))
    state = state + state_ref[0].reshape(rows, LANES)
    done_ref[head] = state
    top_ref[head] = q[:, LANES:].astype(F32)
    largest = jnp.max(jnp.where(state[:, :HEAD_DIM] < SAFE, 0.0, 1.0))

    @pl.when(largest > 0.0)
    def _():
        for at, ref in enumerate(kept):
            copy = pltpu.make_async_copy(ref.at[:, head], spare_ref.at[at], sem)
            copy.start()
            copy.wait()
        spare_ref[count] = block_ref[:, 0]
        spared = (lane >= HEAD_DIM) & (lane < GUARD)
        upper = jnp.where(spared, 0.0, q[:, LANES:].astype(F32)).astype(BF16)
        plain = jnp.concatenate([q[:, :LANES], upper], axis=1)

        def absorb(keys, values, largest, state):
            scores = scores_of(plain, keys)
            higher = jnp.maximum(largest, jnp.max(scores, axis=1, keepdims=True))
            return higher, state * jnp.exp2(largest - higher) + weighted(scores - higher, values)

        def step(at, carry):
            return absorb(*wide_keys(spare_ref[at].reshape(-1, LANES)), *carry)

        carry = (jnp.full((rows, 1), -1e30, F32), jnp.zeros((rows, LANES), F32))
        carry = lax.fori_loop(0, count + 1, step, carry)
        carry = absorb(*wide_keys(first_text_ref[0], valid_ref[0]), *carry)
        tail = wide_keys(text_ref[0], valid_ref[0] - first_text_ref.shape[1])
        largest, state = absorb(*tail, *carry)
        done_ref[head] = state
        top_ref[head] = with_offset(jnp.zeros((rows, LANES), F32), -largest)

    @pl.when(head == pl.num_programs(0) - 1)
    def _():
        marks = jnp.zeros((rows, LANES), F32)
        done = []
        for h in range(done_ref.shape[0]):
            state = done_ref[h]
            total = pltpu.roll(state, HEAD_DIM, 1)
            done.append(state / total)
            terms = top_ref[h] if h == 0 else pltpu.roll(top_ref[h], MARKS * h, 1)
            place = HEAD_DIM + MARKS * h
            lead = total.astype(BF16).astype(F32)
            marks = jnp.where((lane >= place) & (lane < place + 3), terms, marks)
            marks = jnp.where(lane == place + 3, lead, marks)
            marks = jnp.where(lane == place + 4, total - lead, marks)
        low = lane < HEAD_DIM
        left = jnp.where(low, pltpu.roll(done[0], HEAD_DIM, 1), done[1]).astype(BF16)
        right = jnp.where(low, pltpu.roll(done[2], HEAD_DIM, 1), marks).astype(BF16)
        for half in range(2):
            part = slice(half * tile, (half + 1) * tile)
            out_ref[:, 2 * half * LANES : (2 * half + 1) * LANES] = left[part]
            out_ref[:, (2 * half + 1) * LANES : (2 * half + 2) * LANES] = right[part]


def attention_call(kernel, name, operands, kept, out_shape, scratch=(), aliases=()):
    heads = next(x.shape[0] for x in operands if x.ndim == 4)

    def by_head(x):
        if x.ndim == 1:
            return pl.BlockSpec(memory_space=pltpu.SMEM)
        axis = 1 if x.ndim == 4 and x.shape[0] != heads else 0 if x.ndim > 2 else None
        block = tuple(1 if d == axis else n for d, n in enumerate(x.shape))
        return pl.BlockSpec(block, lambda h: tuple(h if d == axis else 0 for d in range(x.ndim)))

    specs = [by_head(x) for x in operands] + [pl.BlockSpec(memory_space=pltpu.HBM)] * len(kept)
    return pl.pallas_call(
        kernel,
        grid=(heads,),
        out_shape=out_shape,
        in_specs=specs,
        out_specs=[by_head(x) for x in out_shape],
        scratch_shapes=scratch,
        input_output_aliases=dict(aliases),
        compiler_params=params(24),
        cost_estimate=pl.CostEstimate(flops=4 * 10**9, bytes_accessed=8 * 10**6, transcendentals=3 * 10**6),
        name=name,
    )(*operands, *kept)


MARK = jax.ShapeDtypeStruct((8, LANES), F32)


def state_shape(q):
    return jax.ShapeDtypeStruct(q.shape[:3] + (LANES,), F32)


def first_block(valid, q, block, text):
    shapes = [jax.ShapeDtypeStruct(q.shape, BF16), state_shape(q), MARK]
    return attention_call(first_kernel, "own_block", [valid, q, block, text], [], shapes)


def next_blocks(q, state, blocks, mark):
    operands = [q, state, *blocks, mark]
    return attention_call(next_kernel, "next_blocks", operands, [], [state_shape(q), MARK], aliases=[(1, 0)])


def last_block(valid, q, state, block, first_text, text, kept):
    heads, _, rows, _ = q.shape
    shape = jax.ShapeDtypeStruct((rows, 4 * LANES), BF16)
    scratch = [
        pltpu.VMEM((heads, 2 * rows, LANES), F32),
        pltpu.VMEM((heads, 2 * rows, LANES), F32),
        pltpu.VMEM((len(kept) + 1, block.shape[0]) + block.shape[2:], BF16),
        pltpu.SemaphoreType.DMA,
    ]
    operands = [valid, q, state, block, first_text, text]
    return attention_call(functools.partial(last_kernel, len(kept)), "last_block", operands, kept, [shape], scratch)[0]


def finish_kernel(
    heads,
    groups,
    partial_ref,
    weight_ref,
    hidden_ref,
    modulation_ref,
    bias_ref,
    final_ref,
    final_bias_ref,
    out_ref,
    wide_ref,
):
    half = partial_ref.shape[1]
    sources = partial_ref.shape[0]
    across = groups // 2
    copies = sources // groups
    width = heads * HEAD_DIM
    low = lane_index((half, LANES)) < HEAD_DIM
    for part in range(2):
        at = part * 2 * LANES
        for group in range(groups):
            zl, y = divmod(group, across)
            members = [(zl * copies + copy) * across + y for copy in range(copies)]
            left = [partial_ref[m, :, at : at + LANES].astype(F32) for m in members]
            right = [partial_ref[m, :, at + LANES : at + 2 * LANES].astype(F32) for m in members]
            levels = [-(r + pltpu.roll(r, LANES - 1, 1) + pltpu.roll(r, LANES - 2, 1)) for r in right]
            counts = [pltpu.roll(r, LANES - 3, 1) + pltpu.roll(r, LANES - 4, 1) for r in right]
            top = functools.reduce(jnp.maximum, levels)
            shares = [count * jnp.exp2(level - top) for count, level in zip(counts, levels)]
            total = functools.reduce(jnp.add, shares)
            first, second = 0.0, 0.0
            for copy in range(copies):
                share = shares[copy] / total
                h0, h1, h2 = [share[:, c : c + 1] for c in (HEAD_DIM, HEAD_DIM + MARKS, HEAD_DIM + 2 * MARKS)]
                first = first + left[copy] * jnp.where(low, h0, h1)
                second = second + right[copy] * h2
            both = jnp.concatenate([first, second[:, :HEAD_DIM]], axis=1)
            wide_ref[part * half : (part + 1) * half, group * width : (group + 1) * width] = both
    attended = wide_ref[...].astype(BF16)
    projected = jnp.dot(attended, weight_ref[...], preferred_element_type=F32)
    residual = hidden_ref[...].astype(F32) + modulation_ref[0:1] * (projected + bias_ref[...])
    middle = jnp.mean(residual, axis=-1, keepdims=True)
    centered = residual - middle
    spread = jnp.mean(centered * centered, axis=-1, keepdims=True)
    normed = centered * lax.rsqrt(spread + 1e-06) * (1.0 + modulation_ref[1:2]) + modulation_ref[2:3]
    velocity = lax.dot_general(
        normed.astype(BF16), final_ref[...], (((1,), (1,)), ((), ())), preferred_element_type=F32
    )
    out_ref[...] = velocity + final_bias_ref[...]


def finish(partial, weight, hidden, modulation, bias, final_weight, final_bias, heads, groups):
    tokens, width = hidden.shape
    return pl.pallas_call(
        functools.partial(finish_kernel, heads, groups),
        out_shape=jax.ShapeDtypeStruct((tokens, final_weight.shape[0]), F32),
        scratch_shapes=[pltpu.VMEM((tokens, width), F32)],
        compiler_params=params(),
        name="project_and_norm",
    )(partial, weight, hidden, modulation, bias, final_weight, final_bias)


def local(
    latent_qkv,
    text_kv,
    hidden_in,
    modulation,
    out_weight,
    out_bias,
    proj_weight,
    proj_bias,
    guidance,
    sigma,
    sample,
):
    groups = lax.axis_size("zl") * lax.axis_size("y")
    ring = lax.axis_size("zh")
    tokens = latent_qkv.shape[1]
    half = tokens // 2
    width = latent_qkv.shape[3] // groups
    heads = width // HEAD_DIM
    across = lax.axis_size("y")
    zl, core, xh, y = (lax.axis_index(a) for a in ("zl", "core", "xh", "y"))
    after = lax.optimization_barrier

    slabs = pack(latent_qkv[0].transpose(1, 0, 2), groups, heads)
    slabs = lax.all_to_all(slabs, HEAD_AXES, split_axis=0, concat_axis=0, tiled=True)
    own = slabs[:, heads * half :].reshape(groups, heads, tokens, LANES)
    route = []
    for i in range(ring):
        route += [(2 * i, 2 * ((i + 1) % ring)), (2 * i + 1, 2 * ((i - 1) % ring) + 1)]
    pass_on = lambda x: lax.ppermute(x, ("zh", "core"), route)
    beside = lax.ppermute(own, "core", [(0, 1), (1, 0)])
    near = pass_on(own)
    packed = slabs[:, : heads * half].reshape(groups, heads, half, LANES)
    packed = lax.all_gather(packed, "core", axis=0)
    opposite = lax.ppermute(packed, "xh", [(0, 1), (1, 0)])
    cross = pass_on(beside)
    q = unpack_queries(xh.reshape(1), packed, opposite)

    weight = lax.all_gather(out_weight, ("xh", "y"), axis=0, tiled=True)

    count = text_kv.shape[1]
    share = -(-count // 32) * 16
    text = text_kv[0].reshape(count, 2, heads, HEAD_DIM).transpose(2, 0, 1, 3).reshape(heads, count, LANES)
    text = jnp.pad(text, ((0, 0), (0, 2 * share - count), (0, 0)))
    text = lax.dynamic_slice_in_dim(text, core * share, share, 1)
    valid = jnp.where(xh == zl, jnp.minimum(count - core * share, share), 0).reshape(1)
    early, late = text[:, :LANES], text[:, LANES:]
    q, state, mark = first_block(valid, q, own, early)
    kept = [own, near, cross]
    for step in range(ring // 2 - 2):
        if step:
            near, mark = after((near, mark))
        nearer = pass_on(near)
        cross, mark = after((cross, mark))
        crosser = pass_on(cross)
        state, mark = next_blocks(q, state, [near, cross], mark)
        near, cross = nearer, crosser
        kept += [near, cross]
    near, mark = after((near, mark))
    farthest = pass_on(near)
    state, mark = next_blocks(q, state, [near, cross], mark)
    partial = last_block(valid, q, state, farthest, early, late, kept)
    partial = partial.reshape(4 * groups, half, 4 * LANES)
    partial = lax.all_to_all(partial, BLOCK_AXES, split_axis=0, concat_axis=0, tiled=True)

    velocity = finish(
        partial,
        weight,
        hidden_in[0],
        modulation[0],
        out_bias[None],
        proj_weight.T,
        proj_bias[None],
        heads,
        groups,
    )

    tiles = velocity.reshape(tokens, 2, -1).transpose(1, 0, 2).reshape(2, -1)
    branch, parity = lax.axis_index("cfg"), y % 2
    same, swap = [], []
    for s in range(2):
        for y in range(across):
            a = y % 2
            same.append((s * across + y, a * across + y - a + s))
            swap.append((s * across + y, a * across + y - a + 1 - s))
    kept = lax.ppermute(lax.dynamic_slice_in_dim(tiles, branch, 1, 0), ("cfg", "y"), same)
    crossed = lax.ppermute(lax.dynamic_slice_in_dim(tiles, 1 - branch, 1, 0), ("cfg", "y"), swap)
    conditional = jnp.where(parity == 0, kept, crossed)
    unconditional = jnp.where(parity == 0, crossed, kept)
    guided = unconditional + guidance[0] * (conditional - unconditional)
    denoised = sample - sigma[0] * guided
    return (guided, denoised)


def solution(mesh):
    sizes = dict(zip(mesh.axis_names, mesh.devices.shape))
    ring = sizes["blk"] // 4
    fine = Mesh(
        mesh.devices.reshape(sizes["cfg"], ring, 2, 2, 2, sizes["uly"] // 2),
        ("cfg", "zh", "zl", "core", "xh", "y"),
    )
    rows = ("zh", "zl", "core", "xh", "y")
    heads = ("xh", "y")
    return jax.shard_map(
        local,
        mesh=fine,
        in_specs=(
            P("cfg", rows, None, None),
            P("cfg", None, None, heads),
            P("cfg", rows, None),
            P("cfg", None, None),
            P(heads, None),
            P(),
            P(),
            P(),
            P(),
            P(),
            P(rows, "cfg"),
        ),
        out_specs=(P(rows, "cfg"), P(rows, "cfg")),
        check_vma=False,
    )
```

```python
import functools
import math

import jax
import jax.numpy as jnp
from jax import lax
from jax.experimental import pallas as pl
from jax.experimental.pallas import tpu as pltpu
from jax.sharding import Mesh, PartitionSpec as P

HEAD_DIM = 64
LANES = 128
LOG2_SCALE = math.log2(math.e) * HEAD_DIM**-0.5
F32 = jnp.float32
BF16 = jnp.bfloat16
GUARD = HEAD_DIM + 3
MARKS = 8
SAFE = 2.0**100
PIECES = 4
HEAD_AXES = ("zl", "y")
BLOCK_AXES = ("zl", "core", "xh", "y")


def params(mib=16):
    return pltpu.CompilerParams(vmem_limit_bytes=mib * 1024 * 1024)


def lane_index(shape):
    return lax.broadcasted_iota(jnp.int32, shape, len(shape) - 1)


def pack_kernel(groups, heads, x_ref, out_ref):
    rows = x_ref.shape[1]
    half = rows // 2
    for group in range(groups):
        queries, pairs = [], []
        for head in range(heads):
            start = (group * heads + head) * HEAD_DIM
            cols = slice(start, start + HEAD_DIM)
            q = x_ref[0, :, cols].astype(F32)
            k = x_ref[1, :, cols].astype(F32)
            v = x_ref[2, :, cols].astype(F32)
            queries.append(jnp.concatenate([q[:half], q[half:]], axis=1))
            pairs.append(jnp.concatenate([k, v], axis=1))
        out_ref[group] = jnp.concatenate(queries + pairs, axis=0).astype(BF16)


def pack(x, groups, heads):
    rows = x.shape[1]
    return pl.pallas_call(
        functools.partial(pack_kernel, groups, heads),
        out_shape=jax.ShapeDtypeStruct((groups, heads * (rows // 2 + rows), LANES), BF16),
        compiler_params=params(),
        name="pack_heads",
    )(x)


def wide_keys(block, valid=None):
    lane = lane_index(block.shape)
    ones = jnp.ones_like(block)
    marked = jnp.where(lane < HEAD_DIM, block, ones)
    if valid is not None:
        row = lax.broadcasted_iota(jnp.int32, block.shape, 0)
        marked = jnp.where((lane == GUARD) & (row >= valid), jnp.full_like(block, -1e30), marked)
    return jnp.concatenate([block, marked], axis=1), jnp.where(lane < HEAD_DIM, ones, block)


def queries_kernel(heads, place_ref, own_ref, other_ref, out_ref, wide_ref):
    here = place_ref[0]
    cores, sources, _, half, _ = own_ref.shape
    across = sources // 2
    lane = lane_index((half, LANES))
    low = lane < HEAD_DIM
    guard = jnp.where(lane == GUARD, 1.0, 0.0)
    for side, ref in ((here, own_ref), (1 - here, other_ref)):
        for core in range(cores):
            for source in range(sources):
                zl, y = divmod(source, across)
                first = (zl * cores + core) * 2 * across + y
                row = pl.multiple_of((first + side * across) * half, 8)
                for head in range(heads):
                    both = ref[core, source, head].astype(F32) * LOG2_SCALE
                    for part, value in enumerate((both, pltpu.roll(both, HEAD_DIM, 1))):
                        lead = value.astype(BF16).astype(F32)
                        wide_ref[head, part, pl.ds(row, half), 0:LANES] = jnp.where(low, lead, 0.0)
                        wide_ref[head, part, pl.ds(row, half), LANES:] = jnp.where(low, value - lead, guard)
    out_ref[...] = wide_ref[...].astype(BF16)


def unpack_queries(place, own, other):
    cores, sources, heads, half, _ = own.shape
    shape = (heads, 2, 2 * cores * sources * half, 2 * LANES)
    return pl.pallas_call(
        functools.partial(queries_kernel, heads),
        out_shape=jax.ShapeDtypeStruct(shape, BF16),
        in_specs=[
            pl.BlockSpec(memory_space=pltpu.SMEM),
            pl.BlockSpec(memory_space=pltpu.VMEM),
            pl.BlockSpec(memory_space=pltpu.VMEM),
        ],
        out_specs=pl.BlockSpec(memory_space=pltpu.VMEM),
        scratch_shapes=[pltpu.VMEM(shape, F32)],
        compiler_params=params(),
        name="unpack_queries",
    )(place, own, other)


def rows_of(ref):
    return ref[:, 0].reshape(-1, ref.shape[-1])


def scores_of(q, keys):
    return lax.dot_general(q, keys, (((1,), (1,)), ((), ())), preferred_element_type=F32)


def weighted(scores, values):
    return jnp.dot(jnp.exp2(scores).astype(BF16), values, preferred_element_type=F32)


def first_kernel(valid_ref, q_ref, block_ref, text_ref, full_ref, state_ref, mark_ref):
    rows = 2 * q_ref.shape[2]
    mark_ref[...] = jnp.zeros_like(mark_ref)
    q = q_ref[0].reshape(rows, 2 * LANES)
    keys, values = wide_keys(rows_of(block_ref))
    more_keys, more_values = wide_keys(text_ref[0], valid_ref[0])
    scores = scores_of(q, jnp.concatenate([keys, more_keys], axis=0))
    offset = jnp.max(scores, axis=1, keepdims=True)
    state = weighted(scores - offset, jnp.concatenate([values, more_values], axis=0))
    state_ref[0] = state.reshape(state_ref.shape[1:])
    full_ref[0, :, :, :LANES] = q_ref[0, :, :, :LANES]
    upper = with_offset(q[:, LANES:].astype(F32), -offset)
    full_ref[0, :, :, LANES:] = upper.astype(BF16).reshape(state_ref.shape[1:])


def with_offset(upper, offset):
    lane = lane_index(upper.shape)
    offset = jnp.broadcast_to(offset, upper.shape)
    coarse = offset.astype(BF16).astype(F32)
    middle = (offset - coarse).astype(BF16).astype(F32)
    for place, term in enumerate((coarse, middle, offset - coarse - middle)):
        upper = jnp.where(lane == HEAD_DIM + place, term, upper)
    return upper


def next_kernel(q_ref, state_ref, *refs):
    *blocks, before_ref, out_ref, mark_ref = refs
    mark_ref[...] = before_ref[...]
    rows = 2 * q_ref.shape[2]
    q = q_ref[0].reshape(rows, 2 * LANES)
    keys, values = wide_keys(jnp.concatenate([rows_of(ref) for ref in blocks], axis=0))
    state = weighted(scores_of(q, keys), values)
    out_ref[0] = state_ref[0] + state.reshape(out_ref.shape[1:])


def last_kernel(count, valid_ref, q_ref, state_ref, block_ref, first_text_ref, text_ref, *refs):
    kept, out_ref, done_ref, top_ref, spare_ref, sem = refs[:count], *refs[count:]
    head = pl.program_id(0)
    tile = q_ref.shape[2]
    rows = 2 * tile
    lane = lane_index((rows, LANES))
    q = q_ref[0].reshape(rows, 2 * LANES)
    keys, values = wide_keys(rows_of(block_ref))
    more_keys, more_values = wide_keys(text_ref[0], valid_ref[0] - first_text_ref.shape[1])
    scores = scores_of(q, jnp.concatenate([keys, more_keys], axis=0))
    state = weighted(scores, jnp.concatenate([values, more_values], axis=0))
    state = state + state_ref[0].reshape(rows, LANES)
    done_ref[head] = state
    top_ref[head] = q[:, LANES:].astype(F32)
    largest = jnp.max(jnp.where(state[:, :HEAD_DIM] < SAFE, 0.0, 1.0))

    @pl.when(largest > 0.0)
    def _():
        for at, ref in enumerate(kept):
            copy = pltpu.make_async_copy(ref.at[:, head], spare_ref.at[at], sem)
            copy.start()
            copy.wait()
        spare_ref[count] = block_ref[:, 0]
        spared = (lane >= HEAD_DIM) & (lane < GUARD)
        upper = jnp.where(spared, 0.0, q[:, LANES:].astype(F32)).astype(BF16)
        plain = jnp.concatenate([q[:, :LANES], upper], axis=1)

        def absorb(keys, values, largest, state):
            scores = scores_of(plain, keys)
            higher = jnp.maximum(largest, jnp.max(scores, axis=1, keepdims=True))
            return higher, state * jnp.exp2(largest - higher) + weighted(scores - higher, values)

        def step(at, carry):
            return absorb(*wide_keys(spare_ref[at].reshape(-1, LANES)), *carry)

        carry = (jnp.full((rows, 1), -1e30, F32), jnp.zeros((rows, LANES), F32))
        carry = lax.fori_loop(0, count + 1, step, carry)
        carry = absorb(*wide_keys(first_text_ref[0], valid_ref[0]), *carry)
        tail = wide_keys(text_ref[0], valid_ref[0] - first_text_ref.shape[1])
        largest, state = absorb(*tail, *carry)
        done_ref[head] = state
        top_ref[head] = with_offset(jnp.zeros((rows, LANES), F32), -largest)

    @pl.when(head == pl.num_programs(0) - 1)
    def _():
        marks = jnp.zeros((rows, LANES), F32)
        done = []
        for h in range(done_ref.shape[0]):
            state = done_ref[h]
            total = pltpu.roll(state, HEAD_DIM, 1)
            done.append(state / total)
            terms = top_ref[h] if h == 0 else pltpu.roll(top_ref[h], MARKS * h, 1)
            place = HEAD_DIM + MARKS * h
            lead = total.astype(BF16).astype(F32)
            marks = jnp.where((lane >= place) & (lane < place + 3), terms, marks)
            marks = jnp.where(lane == place + 3, lead, marks)
            marks = jnp.where(lane == place + 4, total - lead, marks)
        low = lane < HEAD_DIM
        left = jnp.where(low, pltpu.roll(done[0], HEAD_DIM, 1), done[1]).astype(BF16)
        right = jnp.where(low, pltpu.roll(done[2], HEAD_DIM, 1), marks).astype(BF16)
        for half in range(2):
            part = slice(half * tile, (half + 1) * tile)
            out_ref[:, 2 * half * LANES : (2 * half + 1) * LANES] = left[part]
            out_ref[:, (2 * half + 1) * LANES : (2 * half + 2) * LANES] = right[part]


def attention_call(kernel, name, operands, kept, out_shape, scratch=(), aliases=()):
    heads = next(x.shape[0] for x in operands if x.ndim == 4)

    def by_head(x):
        if x.ndim == 1:
            return pl.BlockSpec(memory_space=pltpu.SMEM)
        axis = 1 if x.ndim == 4 and x.shape[0] != heads else 0 if x.ndim > 2 else None
        block = tuple(1 if d == axis else n for d, n in enumerate(x.shape))
        return pl.BlockSpec(block, lambda h: tuple(h if d == axis else 0 for d in range(x.ndim)))

    specs = [by_head(x) for x in operands] + [pl.BlockSpec(memory_space=pltpu.HBM)] * len(kept)
    return pl.pallas_call(
        kernel,
        grid=(heads,),
        out_shape=out_shape,
        in_specs=specs,
        out_specs=[by_head(x) for x in out_shape],
        scratch_shapes=scratch,
        input_output_aliases=dict(aliases),
        compiler_params=params(24),
        cost_estimate=pl.CostEstimate(flops=4 * 10**9, bytes_accessed=8 * 10**6, transcendentals=3 * 10**6),
        name=name,
    )(*operands, *kept)


MARK = jax.ShapeDtypeStruct((8, LANES), F32)


def state_shape(q):
    return jax.ShapeDtypeStruct(q.shape[:3] + (LANES,), F32)


def first_block(valid, q, block, text):
    shapes = [jax.ShapeDtypeStruct(q.shape, BF16), state_shape(q), MARK]
    return attention_call(first_kernel, "own_block", [valid, q, block, text], [], shapes)


def next_blocks(q, state, blocks, mark):
    operands = [q, state, *blocks, mark]
    return attention_call(next_kernel, "next_blocks", operands, [], [state_shape(q), MARK], aliases=[(1, 0)])


def last_block(valid, q, state, block, first_text, text, kept):
    heads, _, rows, _ = q.shape
    shape = jax.ShapeDtypeStruct((rows, 4 * LANES), BF16)
    scratch = [
        pltpu.VMEM((heads, 2 * rows, LANES), F32),
        pltpu.VMEM((heads, 2 * rows, LANES), F32),
        pltpu.VMEM((len(kept) + 1, block.shape[0]) + block.shape[2:], BF16),
        pltpu.SemaphoreType.DMA,
    ]
    operands = [valid, q, state, block, first_text, text]
    return attention_call(functools.partial(last_kernel, len(kept)), "last_block", operands, kept, [shape], scratch)[0]


def finish_kernel(
    heads,
    groups,
    partial_ref,
    weight_ref,
    hidden_ref,
    modulation_ref,
    bias_ref,
    final_ref,
    final_bias_ref,
    out_ref,
    wide_ref,
    held_ref,
    sems,
):
    depth = held_ref.shape[1]
    copies_in = [
        pltpu.make_async_copy(weight_ref.at[pl.ds(n * depth, depth)], held_ref.at[n], sems.at[n])
        for n in range(held_ref.shape[0])
    ]
    for copy in copies_in:
        copy.start()
    half = partial_ref.shape[1]
    sources = partial_ref.shape[0]
    across = groups // 2
    copies = sources // groups
    width = heads * HEAD_DIM
    low = lane_index((half, LANES)) < HEAD_DIM
    for part in range(2):
        at = part * 2 * LANES
        for group in range(groups):
            zl, y = divmod(group, across)
            members = [(zl * copies + copy) * across + y for copy in range(copies)]
            left = [partial_ref[m, :, at : at + LANES].astype(F32) for m in members]
            right = [partial_ref[m, :, at + LANES : at + 2 * LANES].astype(F32) for m in members]
            levels = [-(r + pltpu.roll(r, LANES - 1, 1) + pltpu.roll(r, LANES - 2, 1)) for r in right]
            counts = [pltpu.roll(r, LANES - 3, 1) + pltpu.roll(r, LANES - 4, 1) for r in right]
            top = functools.reduce(jnp.maximum, levels)
            shares = [count * jnp.exp2(level - top) for count, level in zip(counts, levels)]
            total = functools.reduce(jnp.add, shares)
            first, second = 0.0, 0.0
            for copy in range(copies):
                share = shares[copy] / total
                h0, h1, h2 = [share[:, c : c + 1] for c in (HEAD_DIM, HEAD_DIM + MARKS, HEAD_DIM + 2 * MARKS)]
                first = first + left[copy] * jnp.where(low, h0, h1)
                second = second + right[copy] * h2
            both = jnp.concatenate([first, second[:, :HEAD_DIM]], axis=1)
            wide_ref[part * half : (part + 1) * half, group * width : (group + 1) * width] = both
    attended = wide_ref[...].astype(BF16)
    projected = 0.0
    for n, copy in enumerate(copies_in):
        copy.wait()
        part = attended[:, n * depth : (n + 1) * depth]
        projected = projected + jnp.dot(part, held_ref[n], preferred_element_type=F32)
    residual = hidden_ref[...].astype(F32) + modulation_ref[0:1] * (projected + bias_ref[...])
    middle = jnp.mean(residual, axis=-1, keepdims=True)
    centered = residual - middle
    spread = jnp.mean(centered * centered, axis=-1, keepdims=True)
    normed = centered * lax.rsqrt(spread + 1e-06) * (1.0 + modulation_ref[1:2]) + modulation_ref[2:3]
    velocity = lax.dot_general(
        normed.astype(BF16), final_ref[...], (((1,), (1,)), ((), ())), preferred_element_type=F32
    )
    out_ref[...] = velocity + final_bias_ref[...]


def finish(partial, weight, hidden, modulation, bias, final_weight, final_bias, heads, groups):
    tokens, width = hidden.shape
    vmem = pl.BlockSpec(memory_space=pltpu.VMEM)
    return pl.pallas_call(
        functools.partial(finish_kernel, heads, groups),
        out_shape=jax.ShapeDtypeStruct((tokens, final_weight.shape[0]), F32),
        in_specs=[vmem, pl.BlockSpec(memory_space=pltpu.HBM), vmem, vmem, vmem, vmem, vmem],
        out_specs=vmem,
        scratch_shapes=[
            pltpu.VMEM((tokens, width), F32),
            pltpu.VMEM((PIECES, weight.shape[0] // PIECES, weight.shape[1]), BF16),
            pltpu.SemaphoreType.DMA((PIECES,)),
        ],
        compiler_params=params(),
        name="project_and_norm",
    )(partial, weight, hidden, modulation, bias, final_weight, final_bias)


def local(
    latent_qkv,
    text_kv,
    hidden_in,
    modulation,
    out_weight,
    out_bias,
    proj_weight,
    proj_bias,
    guidance,
    sigma,
    sample,
):
    groups = lax.axis_size("zl") * lax.axis_size("y")
    ring = lax.axis_size("zh")
    tokens = latent_qkv.shape[1]
    half = tokens // 2
    width = latent_qkv.shape[3] // groups
    heads = width // HEAD_DIM
    across = lax.axis_size("y")
    zl, core, xh, y = (lax.axis_index(a) for a in ("zl", "core", "xh", "y"))
    after = lax.optimization_barrier

    slabs = pack(latent_qkv[0].transpose(1, 0, 2), groups, heads)
    slabs = lax.all_to_all(slabs, HEAD_AXES, split_axis=0, concat_axis=0, tiled=True)
    own = slabs[:, heads * half :].reshape(groups, heads, tokens, LANES)
    route = []
    for i in range(ring):
        route += [(2 * i, 2 * ((i + 1) % ring)), (2 * i + 1, 2 * ((i - 1) % ring) + 1)]
    pass_on = lambda x: lax.ppermute(x, ("zh", "core"), route)
    beside = lax.ppermute(own, "core", [(0, 1), (1, 0)])
    near = pass_on(own)
    packed = slabs[:, : heads * half].reshape(groups, heads, half, LANES)
    packed = lax.all_gather(packed, "core", axis=0)
    opposite = lax.ppermute(packed, "xh", [(0, 1), (1, 0)])
    cross = pass_on(beside)
    q = unpack_queries(xh.reshape(1), packed, opposite)

    weight = lax.all_gather(out_weight, ("xh", "y"), axis=0, tiled=True)

    count = text_kv.shape[1]
    share = -(-count // 32) * 16
    text = text_kv[0].reshape(count, 2, heads, HEAD_DIM).transpose(2, 0, 1, 3).reshape(heads, count, LANES)
    text = jnp.pad(text, ((0, 0), (0, 2 * share - count), (0, 0)))
    text = lax.dynamic_slice_in_dim(text, core * share, share, 1)
    valid = jnp.where(xh == zl, jnp.minimum(count - core * share, share), 0).reshape(1)
    early, late = text[:, :LANES], text[:, LANES:]
    q, state, mark = first_block(valid, q, own, early)
    kept = [own, near, cross]
    for step in range(ring // 2 - 2):
        if step:
            near, mark = after((near, mark))
        nearer = pass_on(near)
        cross, mark = after((cross, mark))
        crosser = pass_on(cross)
        state, mark = next_blocks(q, state, [near, cross], mark)
        near, cross = nearer, crosser
        kept += [near, cross]
    near, mark = after((near, mark))
    farthest = pass_on(near)
    state, mark = next_blocks(q, state, [near, cross], mark)
    partial = last_block(valid, q, state, farthest, early, late, kept)
    partial = partial.reshape(4 * groups, half, 4 * LANES)
    partial = lax.all_to_all(partial, BLOCK_AXES, split_axis=0, concat_axis=0, tiled=True)

    velocity = finish(
        partial,
        pltpu.with_memory_space_constraint(weight, pltpu.HBM),
        hidden_in[0],
        modulation[0],
        out_bias[None],
        proj_weight.T,
        proj_bias[None],
        heads,
        groups,
    )

    tiles = velocity.reshape(tokens, 2, -1).transpose(1, 0, 2).reshape(2, -1)
    branch, parity = lax.axis_index("cfg"), y % 2
    same, swap = [], []
    for s in range(2):
        for y in range(across):
            a = y % 2
            same.append((s * across + y, a * across + y - a + s))
            swap.append((s * across + y, a * across + y - a + 1 - s))
    kept = lax.ppermute(lax.dynamic_slice_in_dim(tiles, branch, 1, 0), ("cfg", "y"), same)
    crossed = lax.ppermute(lax.dynamic_slice_in_dim(tiles, 1 - branch, 1, 0), ("cfg", "y"), swap)
    conditional = jnp.where(parity == 0, kept, crossed)
    unconditional = jnp.where(parity == 0, crossed, kept)
    guided = unconditional + guidance[0] * (conditional - unconditional)
    denoised = sample - sigma[0] * guided
    return (guided, denoised)


def solution(mesh):
    sizes = dict(zip(mesh.axis_names, mesh.devices.shape))
    ring = sizes["blk"] // 4
    fine = Mesh(
        mesh.devices.reshape(sizes["cfg"], ring, 2, 2, 2, sizes["uly"] // 2),
        ("cfg", "zh", "zl", "core", "xh", "y"),
    )
    rows = ("zh", "zl", "core", "xh", "y")
    heads = ("xh", "y")
    return jax.shard_map(
        local,
        mesh=fine,
        in_specs=(
            P("cfg", rows, None, None),
            P("cfg", None, None, heads),
            P("cfg", rows, None),
            P("cfg", None, None),
            P(heads, None),
            P(),
            P(),
            P(),
            P(),
            P(),
            P(rows, "cfg"),
        ),
        out_specs=(P(rows, "cfg"), P(rows, "cfg")),
        check_vma=False,
    )
```

```python
import functools
import math

import jax
import jax.numpy as jnp
from jax import lax
from jax.experimental import pallas as pl
from jax.experimental.pallas import tpu as pltpu
from jax.sharding import Mesh, PartitionSpec as P

HEAD_DIM = 64
LANES = 128
LOG2_SCALE = math.log2(math.e) * HEAD_DIM**-0.5
F32 = jnp.float32
BF16 = jnp.bfloat16
GUARD = HEAD_DIM + 3
MARKS = 8
SAFE = 2.0**100
HEAD_AXES = ("zl", "y")
BLOCK_AXES = ("zl", "core", "xh", "y")


def params(mib=16):
    return pltpu.CompilerParams(vmem_limit_bytes=mib * 1024 * 1024)


def lane_index(shape):
    return lax.broadcasted_iota(jnp.int32, shape, len(shape) - 1)


def pack_kernel(groups, heads, x_ref, out_ref):
    rows = x_ref.shape[1]
    half = rows // 2
    for group in range(groups):
        queries, pairs = [], []
        for head in range(heads):
            start = (group * heads + head) * HEAD_DIM
            cols = slice(start, start + HEAD_DIM)
            q = x_ref[0, :, cols].astype(F32)
            k = x_ref[1, :, cols].astype(F32)
            v = x_ref[2, :, cols].astype(F32)
            queries.append(jnp.concatenate([q[:half], q[half:]], axis=1))
            pairs.append(jnp.concatenate([k, v], axis=1))
        out_ref[group] = jnp.concatenate(queries + pairs, axis=0).astype(BF16)


def pack(x, groups, heads):
    rows = x.shape[1]
    return pl.pallas_call(
        functools.partial(pack_kernel, groups, heads),
        out_shape=jax.ShapeDtypeStruct((groups, heads * (rows // 2 + rows), LANES), BF16),
        compiler_params=params(),
        name="pack_heads",
    )(x)


def wide_keys(block, valid=None):
    lane = lane_index(block.shape)
    ones = jnp.ones_like(block)
    marked = jnp.where(lane < HEAD_DIM, block, ones)
    if valid is not None:
        row = lax.broadcasted_iota(jnp.int32, block.shape, 0)
        marked = jnp.where((lane == GUARD) & (row >= valid), jnp.full_like(block, -1e30), marked)
    return jnp.concatenate([block, marked], axis=1), jnp.where(lane < HEAD_DIM, ones, block)


def queries_kernel(heads, place_ref, own_ref, other_ref, out_ref, wide_ref):
    here, here_core = place_ref[0], place_ref[1]
    cores, sources, _, half, _ = own_ref.shape
    across = sources // 2
    lane = lane_index((half, LANES))
    low = lane < HEAD_DIM
    guard = jnp.where(lane == GUARD, 1.0, 0.0)
    for side, ref in ((here, own_ref), (1 - here, other_ref)):
        for slot, core in enumerate((here_core, 1 - here_core)):
            for source in range(sources):
                zl, y = divmod(source, across)
                first = (zl * cores + core) * 2 * across + y
                row = pl.multiple_of((first + side * across) * half, 8)
                for head in range(heads):
                    both = ref[slot, source, head].astype(F32) * LOG2_SCALE
                    for part, value in enumerate((both, pltpu.roll(both, HEAD_DIM, 1))):
                        lead = value.astype(BF16).astype(F32)
                        wide_ref[head, part, pl.ds(row, half), 0:LANES] = jnp.where(low, lead, 0.0)
                        wide_ref[head, part, pl.ds(row, half), LANES:] = jnp.where(low, value - lead, guard)
    out_ref[...] = wide_ref[...].astype(BF16)


def unpack_queries(place, own, other):
    cores, sources, heads, half, _ = own.shape
    shape = (heads, 2, 2 * cores * sources * half, 2 * LANES)
    return pl.pallas_call(
        functools.partial(queries_kernel, heads),
        out_shape=jax.ShapeDtypeStruct(shape, BF16),
        in_specs=[
            pl.BlockSpec(memory_space=pltpu.SMEM),
            pl.BlockSpec(memory_space=pltpu.VMEM),
            pl.BlockSpec(memory_space=pltpu.VMEM),
        ],
        out_specs=pl.BlockSpec(memory_space=pltpu.VMEM),
        scratch_shapes=[pltpu.VMEM(shape, F32)],
        compiler_params=params(),
        name="unpack_queries",
    )(place, own, other)


def rows_of(ref):
    return ref[:, 0].reshape(-1, ref.shape[-1])


def scores_of(q, keys):
    return lax.dot_general(q, keys, (((1,), (1,)), ((), ())), preferred_element_type=F32)


def weighted(scores, values):
    return jnp.dot(jnp.exp2(scores).astype(BF16), values, preferred_element_type=F32)


def first_kernel(valid_ref, q_ref, block_ref, text_ref, full_ref, state_ref, mark_ref):
    rows = 2 * q_ref.shape[2]
    mark_ref[...] = jnp.zeros_like(mark_ref)
    q = q_ref[0].reshape(rows, 2 * LANES)
    keys, values = wide_keys(rows_of(block_ref))
    more_keys, more_values = wide_keys(text_ref[0], valid_ref[0])
    scores = scores_of(q, jnp.concatenate([keys, more_keys], axis=0))
    offset = jnp.max(scores, axis=1, keepdims=True)
    state = weighted(scores - offset, jnp.concatenate([values, more_values], axis=0))
    state_ref[0] = state.reshape(state_ref.shape[1:])
    full_ref[0, :, :, :LANES] = q_ref[0, :, :, :LANES]
    upper = with_offset(q[:, LANES:].astype(F32), -offset)
    full_ref[0, :, :, LANES:] = upper.astype(BF16).reshape(state_ref.shape[1:])


def with_offset(upper, offset):
    lane = lane_index(upper.shape)
    offset = jnp.broadcast_to(offset, upper.shape)
    coarse = offset.astype(BF16).astype(F32)
    middle = (offset - coarse).astype(BF16).astype(F32)
    for place, term in enumerate((coarse, middle, offset - coarse - middle)):
        upper = jnp.where(lane == HEAD_DIM + place, term, upper)
    return upper


def next_kernel(q_ref, state_ref, *refs):
    *blocks, before_ref, out_ref, mark_ref = refs
    mark_ref[...] = before_ref[...]
    rows = 2 * q_ref.shape[2]
    q = q_ref[0].reshape(rows, 2 * LANES)
    keys, values = wide_keys(jnp.concatenate([rows_of(ref) for ref in blocks], axis=0))
    state = weighted(scores_of(q, keys), values)
    out_ref[0] = state_ref[0] + state.reshape(out_ref.shape[1:])


def last_kernel(count, valid_ref, q_ref, state_ref, block_ref, first_text_ref, text_ref, *refs):
    kept, out_ref, done_ref, top_ref, spare_ref, sem = refs[:count], *refs[count:]
    head = pl.program_id(0)
    tile = q_ref.shape[2]
    rows = 2 * tile
    lane = lane_index((rows, LANES))
    q = q_ref[0].reshape(rows, 2 * LANES)
    keys, values = wide_keys(rows_of(block_ref))
    more_keys, more_values = wide_keys(text_ref[0], valid_ref[0] - first_text_ref.shape[1])
    scores = scores_of(q, jnp.concatenate([keys, more_keys], axis=0))
    state = weighted(scores, jnp.concatenate([values, more_values], axis=0))
    state = state + state_ref[0].reshape(rows, LANES)
    done_ref[head] = state
    top_ref[head] = q[:, LANES:].astype(F32)
    largest = jnp.max(jnp.where(state[:, :HEAD_DIM] < SAFE, 0.0, 1.0))

    @pl.when(largest > 0.0)
    def _():
        for at, ref in enumerate(kept):
            copy = pltpu.make_async_copy(ref.at[:, head], spare_ref.at[at], sem)
            copy.start()
            copy.wait()
        spare_ref[count] = block_ref[:, 0]
        spared = (lane >= HEAD_DIM) & (lane < GUARD)
        upper = jnp.where(spared, 0.0, q[:, LANES:].astype(F32)).astype(BF16)
        plain = jnp.concatenate([q[:, :LANES], upper], axis=1)

        def absorb(keys, values, largest, state):
            scores = scores_of(plain, keys)
            higher = jnp.maximum(largest, jnp.max(scores, axis=1, keepdims=True))
            return higher, state * jnp.exp2(largest - higher) + weighted(scores - higher, values)

        def step(at, carry):
            return absorb(*wide_keys(spare_ref[at].reshape(-1, LANES)), *carry)

        carry = (jnp.full((rows, 1), -1e30, F32), jnp.zeros((rows, LANES), F32))
        carry = lax.fori_loop(0, count + 1, step, carry)
        carry = absorb(*wide_keys(first_text_ref[0], valid_ref[0]), *carry)
        tail = wide_keys(text_ref[0], valid_ref[0] - first_text_ref.shape[1])
        largest, state = absorb(*tail, *carry)
        done_ref[head] = state
        top_ref[head] = with_offset(jnp.zeros((rows, LANES), F32), -largest)

    @pl.when(head == pl.num_programs(0) - 1)
    def _():
        marks = jnp.zeros((rows, LANES), F32)
        done = []
        for h in range(done_ref.shape[0]):
            state = done_ref[h]
            total = pltpu.roll(state, HEAD_DIM, 1)
            done.append(state / total)
            terms = top_ref[h] if h == 0 else pltpu.roll(top_ref[h], MARKS * h, 1)
            place = HEAD_DIM + MARKS * h
            lead = total.astype(BF16).astype(F32)
            marks = jnp.where((lane >= place) & (lane < place + 3), terms, marks)
            marks = jnp.where(lane == place + 3, lead, marks)
            marks = jnp.where(lane == place + 4, total - lead, marks)
        low = lane < HEAD_DIM
        left = jnp.where(low, pltpu.roll(done[0], HEAD_DIM, 1), done[1]).astype(BF16)
        right = jnp.where(low, pltpu.roll(done[2], HEAD_DIM, 1), marks).astype(BF16)
        for half in range(2):
            part = slice(half * tile, (half + 1) * tile)
            out_ref[:, 2 * half * LANES : (2 * half + 1) * LANES] = left[part]
            out_ref[:, (2 * half + 1) * LANES : (2 * half + 2) * LANES] = right[part]


def attention_call(kernel, name, operands, kept, out_shape, scratch=(), aliases=()):
    heads = next(x.shape[0] for x in operands if x.ndim == 4)

    def by_head(x):
        if x.ndim == 1:
            return pl.BlockSpec(memory_space=pltpu.SMEM)
        axis = 1 if x.ndim == 4 and x.shape[0] != heads else 0 if x.ndim > 2 else None
        block = tuple(1 if d == axis else n for d, n in enumerate(x.shape))
        return pl.BlockSpec(block, lambda h: tuple(h if d == axis else 0 for d in range(x.ndim)))

    specs = [by_head(x) for x in operands] + [pl.BlockSpec(memory_space=pltpu.HBM)] * len(kept)
    return pl.pallas_call(
        kernel,
        grid=(heads,),
        out_shape=out_shape,
        in_specs=specs,
        out_specs=[by_head(x) for x in out_shape],
        scratch_shapes=scratch,
        input_output_aliases=dict(aliases),
        compiler_params=params(24),
        cost_estimate=pl.CostEstimate(flops=4 * 10**9, bytes_accessed=8 * 10**6, transcendentals=3 * 10**6),
        name=name,
    )(*operands, *kept)


MARK = jax.ShapeDtypeStruct((8, LANES), F32)


def state_shape(q):
    return jax.ShapeDtypeStruct(q.shape[:3] + (LANES,), F32)


def first_block(valid, q, block, text):
    shapes = [jax.ShapeDtypeStruct(q.shape, BF16), state_shape(q), MARK]
    return attention_call(first_kernel, "own_block", [valid, q, block, text], [], shapes)


def next_blocks(q, state, blocks, mark):
    operands = [q, state, *blocks, mark]
    return attention_call(next_kernel, "next_blocks", operands, [], [state_shape(q), MARK], aliases=[(1, 0)])


def last_block(valid, q, state, block, first_text, text, kept):
    heads, _, rows, _ = q.shape
    shape = jax.ShapeDtypeStruct((rows, 4 * LANES), BF16)
    scratch = [
        pltpu.VMEM((heads, 2 * rows, LANES), F32),
        pltpu.VMEM((heads, 2 * rows, LANES), F32),
        pltpu.VMEM((len(kept) + 1, block.shape[0]) + block.shape[2:], BF16),
        pltpu.SemaphoreType.DMA,
    ]
    operands = [valid, q, state, block, first_text, text]
    return attention_call(functools.partial(last_kernel, len(kept)), "last_block", operands, kept, [shape], scratch)[0]


def finish_kernel(
    heads,
    groups,
    partial_ref,
    weight_ref,
    hidden_ref,
    modulation_ref,
    bias_ref,
    final_ref,
    final_bias_ref,
    out_ref,
    wide_ref,
):
    half = partial_ref.shape[1]
    sources = partial_ref.shape[0]
    across = groups // 2
    copies = sources // groups
    width = heads * HEAD_DIM
    low = lane_index((half, LANES)) < HEAD_DIM
    for part in range(2):
        at = part * 2 * LANES
        for group in range(groups):
            zl, y = divmod(group, across)
            members = [(zl * copies + copy) * across + y for copy in range(copies)]
            left = [partial_ref[m, :, at : at + LANES].astype(F32) for m in members]
            right = [partial_ref[m, :, at + LANES : at + 2 * LANES].astype(F32) for m in members]
            levels = [-(r + pltpu.roll(r, LANES - 1, 1) + pltpu.roll(r, LANES - 2, 1)) for r in right]
            counts = [pltpu.roll(r, LANES - 3, 1) + pltpu.roll(r, LANES - 4, 1) for r in right]
            top = functools.reduce(jnp.maximum, levels)
            shares = [count * jnp.exp2(level - top) for count, level in zip(counts, levels)]
            total = functools.reduce(jnp.add, shares)
            first, second = 0.0, 0.0
            for copy in range(copies):
                share = shares[copy] / total
                h0, h1, h2 = [share[:, c : c + 1] for c in (HEAD_DIM, HEAD_DIM + MARKS, HEAD_DIM + 2 * MARKS)]
                first = first + left[copy] * jnp.where(low, h0, h1)
                second = second + right[copy] * h2
            both = jnp.concatenate([first, second[:, :HEAD_DIM]], axis=1)
            wide_ref[part * half : (part + 1) * half, group * width : (group + 1) * width] = both
    attended = wide_ref[...].astype(BF16)
    projected = jnp.dot(attended, weight_ref[...], preferred_element_type=F32)
    residual = hidden_ref[...].astype(F32) + modulation_ref[0:1] * (projected + bias_ref[...])
    middle = jnp.mean(residual, axis=-1, keepdims=True)
    centered = residual - middle
    spread = jnp.mean(centered * centered, axis=-1, keepdims=True)
    normed = centered * lax.rsqrt(spread + 1e-06) * (1.0 + modulation_ref[1:2]) + modulation_ref[2:3]
    velocity = lax.dot_general(
        normed.astype(BF16), final_ref[...], (((1,), (1,)), ((), ())), preferred_element_type=F32
    )
    out_ref[...] = velocity + final_bias_ref[...]


def finish(partial, weight, hidden, modulation, bias, final_weight, final_bias, heads, groups):
    tokens, width = hidden.shape
    return pl.pallas_call(
        functools.partial(finish_kernel, heads, groups),
        out_shape=jax.ShapeDtypeStruct((tokens, final_weight.shape[0]), F32),
        scratch_shapes=[pltpu.VMEM((tokens, width), F32)],
        compiler_params=params(),
        name="project_and_norm",
    )(partial, weight, hidden, modulation, bias, final_weight, final_bias)


def local(
    latent_qkv,
    text_kv,
    hidden_in,
    modulation,
    out_weight,
    out_bias,
    proj_weight,
    proj_bias,
    guidance,
    sigma,
    sample,
):
    groups = lax.axis_size("zl") * lax.axis_size("y")
    ring = lax.axis_size("zh")
    tokens = latent_qkv.shape[1]
    half = tokens // 2
    width = latent_qkv.shape[3] // groups
    heads = width // HEAD_DIM
    across = lax.axis_size("y")
    zl, core, xh, y = (lax.axis_index(a) for a in ("zl", "core", "xh", "y"))
    after = lax.optimization_barrier

    slabs = pack(latent_qkv[0].transpose(1, 0, 2), groups, heads)
    slabs = lax.all_to_all(slabs, HEAD_AXES, split_axis=0, concat_axis=0, tiled=True)
    own = slabs[:, heads * half :].reshape(groups, heads, tokens, LANES)
    route = []
    for i in range(ring):
        route += [(2 * i, 2 * ((i + 1) % ring)), (2 * i + 1, 2 * ((i - 1) % ring) + 1)]
    pass_on = lambda x: lax.ppermute(x, ("zh", "core"), route)
    other_slabs = lax.ppermute(slabs, "core", [(0, 1), (1, 0)])
    beside = other_slabs[:, heads * half :].reshape(groups, heads, tokens, LANES)
    near = pass_on(own)
    packed = jnp.stack([slabs[:, : heads * half], other_slabs[:, : heads * half]])
    packed = packed.reshape(2, groups, heads, half, LANES)
    opposite = lax.ppermute(packed, "xh", [(0, 1), (1, 0)])
    cross = pass_on(beside)
    opposite, cross = after((opposite, cross))
    q = unpack_queries(jnp.stack([xh, core]), packed, opposite)

    weight = lax.all_gather(out_weight, ("xh", "y"), axis=0, tiled=True)

    count = text_kv.shape[1]
    share = -(-count // 32) * 16
    text = text_kv[0].reshape(count, 2, heads, HEAD_DIM).transpose(2, 0, 1, 3).reshape(heads, count, LANES)
    text = jnp.pad(text, ((0, 0), (0, 2 * share - count), (0, 0)))
    text = lax.dynamic_slice_in_dim(text, core * share, share, 1)
    valid = jnp.where(xh == zl, jnp.minimum(count - core * share, share), 0).reshape(1)
    early, late = text[:, :LANES], text[:, LANES:]
    q, state, mark = first_block(valid, q, own, early)
    kept = [own, near, cross]
    for step in range(ring // 2 - 2):
        if step:
            near, mark = after((near, mark))
        nearer = pass_on(near)
        cross, mark = after((cross, mark))
        crosser = pass_on(cross)
        state, mark = next_blocks(q, state, [near, cross], mark)
        near, cross = nearer, crosser
        kept += [near, cross]
    near, mark = after((near, mark))
    farthest = pass_on(near)
    state, mark = next_blocks(q, state, [near, cross], mark)
    partial = last_block(valid, q, state, farthest, early, late, kept)
    partial = partial.reshape(4 * groups, half, 4 * LANES)
    partial = lax.all_to_all(partial, BLOCK_AXES, split_axis=0, concat_axis=0, tiled=True)

    velocity = finish(
        partial,
        weight,
        hidden_in[0],
        modulation[0],
        out_bias[None],
        proj_weight.T,
        proj_bias[None],
        heads,
        groups,
    )

    tiles = velocity.reshape(tokens, 2, -1).transpose(1, 0, 2).reshape(2, -1)
    branch, parity = lax.axis_index("cfg"), y % 2
    same, swap = [], []
    for s in range(2):
        for y in range(across):
            a = y % 2
            same.append((s * across + y, a * across + y - a + s))
            swap.append((s * across + y, a * across + y - a + 1 - s))
    kept = lax.ppermute(lax.dynamic_slice_in_dim(tiles, branch, 1, 0), ("cfg", "y"), same)
    crossed = lax.ppermute(lax.dynamic_slice_in_dim(tiles, 1 - branch, 1, 0), ("cfg", "y"), swap)
    conditional = jnp.where(parity == 0, kept, crossed)
    unconditional = jnp.where(parity == 0, crossed, kept)
    guided = unconditional + guidance[0] * (conditional - unconditional)
    denoised = sample - sigma[0] * guided
    return (guided, denoised)


def solution(mesh):
    sizes = dict(zip(mesh.axis_names, mesh.devices.shape))
    ring = sizes["blk"] // 4
    fine = Mesh(
        mesh.devices.reshape(sizes["cfg"], ring, 2, 2, 2, sizes["uly"] // 2),
        ("cfg", "zh", "zl", "core", "xh", "y"),
    )
    rows = ("zh", "zl", "core", "xh", "y")
    heads = ("xh", "y")
    return jax.shard_map(
        local,
        mesh=fine,
        in_specs=(
            P("cfg", rows, None, None),
            P("cfg", None, None, heads),
            P("cfg", rows, None),
            P("cfg", None, None),
            P(heads, None),
            P(),
            P(),
            P(),
            P(),
            P(),
            P(rows, "cfg"),
        ),
        out_specs=(P(rows, "cfg"), P(rows, "cfg")),
        check_vma=False,
    )
```

```python
import functools
import math

import jax
import jax.numpy as jnp
from jax import lax
from jax.experimental import pallas as pl
from jax.experimental.pallas import tpu as pltpu
from jax.sharding import Mesh, PartitionSpec as P

HEAD_DIM = 64
LANES = 128
LOG2_SCALE = math.log2(math.e) * HEAD_DIM**-0.5
F32 = jnp.float32
BF16 = jnp.bfloat16
GUARD = HEAD_DIM + 3
MARKS = 8
SAFE = 2.0**100
HEAD_AXES = ("zl", "y")
BLOCK_AXES = ("zl", "core", "xh", "y")


def params(mib=16):
    return pltpu.CompilerParams(vmem_limit_bytes=mib * 1024 * 1024)


def lane_index(shape):
    return lax.broadcasted_iota(jnp.int32, shape, len(shape) - 1)


def pack_kernel(groups, heads, x_ref, out_ref):
    rows = x_ref.shape[1]
    half = rows // 2
    for group in range(groups):
        queries, pairs = [], []
        for head in range(heads):
            start = (group * heads + head) * HEAD_DIM
            cols = slice(start, start + HEAD_DIM)
            q = x_ref[0, :, cols].astype(F32)
            k = x_ref[1, :, cols].astype(F32)
            v = x_ref[2, :, cols].astype(F32)
            queries.append(jnp.concatenate([q[:half], q[half:]], axis=1))
            pairs.append(jnp.concatenate([k, v], axis=1))
        out_ref[group] = jnp.concatenate(queries + pairs, axis=0).astype(BF16)


def pack(x, groups, heads):
    rows = x.shape[1]
    return pl.pallas_call(
        functools.partial(pack_kernel, groups, heads),
        out_shape=jax.ShapeDtypeStruct((groups, heads * (rows // 2 + rows), LANES), BF16),
        compiler_params=params(),
        name="pack_heads",
    )(x)


def wide_keys(block, valid=None):
    lane = lane_index(block.shape)
    ones = jnp.ones_like(block)
    marked = jnp.where(lane < HEAD_DIM, block, ones)
    if valid is not None:
        row = lax.broadcasted_iota(jnp.int32, block.shape, 0)
        marked = jnp.where((lane == GUARD) & (row >= valid), jnp.full_like(block, -1e30), marked)
    return jnp.concatenate([block, marked], axis=1), jnp.where(lane < HEAD_DIM, ones, block)


def queries_kernel(heads, place_ref, own_ref, other_ref, out_ref, wide_ref):
    here = place_ref[0]
    cores, sources, _, half, _ = own_ref.shape
    across = sources // 2
    lane = lane_index((half, LANES))
    low = lane < HEAD_DIM
    guard = jnp.where(lane == GUARD, 1.0, 0.0)
    for side, ref in ((here, own_ref), (1 - here, other_ref)):
        for core in range(cores):
            for source in range(sources):
                zl, y = divmod(source, across)
                first = (zl * cores + core) * 2 * across + y
                row = pl.multiple_of((first + side * across) * half, 8)
                for head in range(heads):
                    both = ref[core, source, head].astype(F32) * LOG2_SCALE
                    for part, value in enumerate((both, pltpu.roll(both, HEAD_DIM, 1))):
                        lead = value.astype(BF16).astype(F32)
                        wide_ref[head, part, pl.ds(row, half), 0:LANES] = jnp.where(low, lead, 0.0)
                        wide_ref[head, part, pl.ds(row, half), LANES:] = jnp.where(low, value - lead, guard)
    out_ref[...] = wide_ref[...].astype(BF16)


def unpack_queries(place, own, other):
    cores, sources, heads, half, _ = own.shape
    shape = (heads, 2, 2 * cores * sources * half, 2 * LANES)
    return pl.pallas_call(
        functools.partial(queries_kernel, heads),
        out_shape=jax.ShapeDtypeStruct(shape, BF16),
        in_specs=[
            pl.BlockSpec(memory_space=pltpu.SMEM),
            pl.BlockSpec(memory_space=pltpu.VMEM),
            pl.BlockSpec(memory_space=pltpu.VMEM),
        ],
        out_specs=pl.BlockSpec(memory_space=pltpu.VMEM),
        scratch_shapes=[pltpu.VMEM(shape, F32)],
        compiler_params=params(),
        name="unpack_queries",
    )(place, own, other)


def rows_of(ref):
    return ref[:, 0].reshape(-1, ref.shape[-1])


def scores_of(q, keys):
    return lax.dot_general(q, keys, (((1,), (1,)), ((), ())), preferred_element_type=F32)


def weighted(scores, values):
    return jnp.dot(jnp.exp2(scores).astype(BF16), values, preferred_element_type=F32)


def first_kernel(valid_ref, q_ref, block_ref, text_ref, full_ref, state_ref, mark_ref):
    rows = 2 * q_ref.shape[2]
    mark_ref[...] = jnp.zeros_like(mark_ref)
    q = q_ref[0].reshape(rows, 2 * LANES)
    keys, values = wide_keys(rows_of(block_ref))
    more_keys, more_values = wide_keys(text_ref[0], valid_ref[0])
    scores = scores_of(q, jnp.concatenate([keys, more_keys], axis=0))
    offset = jnp.max(scores, axis=1, keepdims=True)
    state = weighted(scores - offset, jnp.concatenate([values, more_values], axis=0))
    state_ref[0] = state.reshape(state_ref.shape[1:])
    full_ref[0, :, :, :LANES] = q_ref[0, :, :, :LANES]
    upper = with_offset(q[:, LANES:].astype(F32), -offset)
    full_ref[0, :, :, LANES:] = upper.astype(BF16).reshape(state_ref.shape[1:])


def with_offset(upper, offset):
    lane = lane_index(upper.shape)
    offset = jnp.broadcast_to(offset, upper.shape)
    coarse = offset.astype(BF16).astype(F32)
    middle = (offset - coarse).astype(BF16).astype(F32)
    for place, term in enumerate((coarse, middle, offset - coarse - middle)):
        upper = jnp.where(lane == HEAD_DIM + place, term, upper)
    return upper


def next_kernel(q_ref, state_ref, *refs):
    *blocks, before_ref, out_ref, mark_ref = refs
    mark_ref[...] = before_ref[...]
    rows = 2 * q_ref.shape[2]
    q = q_ref[0].reshape(rows, 2 * LANES)
    keys, values = wide_keys(jnp.concatenate([rows_of(ref) for ref in blocks], axis=0))
    state = weighted(scores_of(q, keys), values)
    out_ref[0] = state_ref[0] + state.reshape(out_ref.shape[1:])


def last_kernel(count, valid_ref, q_ref, state_ref, block_ref, first_text_ref, text_ref, *refs):
    kept, out_ref, done_ref, top_ref, spare_ref, sem = refs[:count], *refs[count:]
    head = pl.program_id(0)
    tile = q_ref.shape[2]
    rows = 2 * tile
    lane = lane_index((rows, LANES))
    q = q_ref[0].reshape(rows, 2 * LANES)
    keys, values = wide_keys(rows_of(block_ref))
    more_keys, more_values = wide_keys(text_ref[0], valid_ref[0] - first_text_ref.shape[1])
    scores = scores_of(q, jnp.concatenate([keys, more_keys], axis=0))
    state = weighted(scores, jnp.concatenate([values, more_values], axis=0))
    state = state + state_ref[0].reshape(rows, LANES)
    done_ref[head] = state
    top_ref[head] = q[:, LANES:].astype(F32)
    largest = jnp.max(jnp.where(state[:, :HEAD_DIM] < SAFE, 0.0, 1.0))

    @pl.when(largest > 0.0)
    def _():
        for at, ref in enumerate(kept):
            copy = pltpu.make_async_copy(ref.at[:, head], spare_ref.at[at], sem)
            copy.start()
            copy.wait()
        spare_ref[count] = block_ref[:, 0]
        spared = (lane >= HEAD_DIM) & (lane < GUARD)
        upper = jnp.where(spared, 0.0, q[:, LANES:].astype(F32)).astype(BF16)
        plain = jnp.concatenate([q[:, :LANES], upper], axis=1)

        def absorb(keys, values, largest, state):
            scores = scores_of(plain, keys)
            higher = jnp.maximum(largest, jnp.max(scores, axis=1, keepdims=True))
            return higher, state * jnp.exp2(largest - higher) + weighted(scores - higher, values)

        def step(at, carry):
            return absorb(*wide_keys(spare_ref[at].reshape(-1, LANES)), *carry)

        carry = (jnp.full((rows, 1), -1e30, F32), jnp.zeros((rows, LANES), F32))
        carry = lax.fori_loop(0, count + 1, step, carry)
        carry = absorb(*wide_keys(first_text_ref[0], valid_ref[0]), *carry)
        tail = wide_keys(text_ref[0], valid_ref[0] - first_text_ref.shape[1])
        largest, state = absorb(*tail, *carry)
        done_ref[head] = state
        top_ref[head] = with_offset(jnp.zeros((rows, LANES), F32), -largest)

    @pl.when(head == pl.num_programs(0) - 1)
    def _():
        marks = jnp.zeros((rows, LANES), F32)
        done = []
        for h in range(done_ref.shape[0]):
            state = done_ref[h]
            total = pltpu.roll(state, HEAD_DIM, 1)
            done.append(state / total)
            terms = top_ref[h] if h == 0 else pltpu.roll(top_ref[h], MARKS * h, 1)
            place = HEAD_DIM + MARKS * h
            lead = total.astype(BF16).astype(F32)
            marks = jnp.where((lane >= place) & (lane < place + 3), terms, marks)
            marks = jnp.where(lane == place + 3, lead, marks)
            marks = jnp.where(lane == place + 4, total - lead, marks)
        low = lane < HEAD_DIM
        left = jnp.where(low, pltpu.roll(done[0], HEAD_DIM, 1), done[1]).astype(BF16)
        right = jnp.where(low, pltpu.roll(done[2], HEAD_DIM, 1), marks).astype(BF16)
        for half in range(2):
            part = slice(half * tile, (half + 1) * tile)
            out_ref[:, 2 * half * LANES : (2 * half + 1) * LANES] = left[part]
            out_ref[:, (2 * half + 1) * LANES : (2 * half + 2) * LANES] = right[part]


def attention_call(kernel, name, operands, kept, out_shape, scratch=(), aliases=()):
    heads = next(x.shape[0] for x in operands if x.ndim == 4)

    def by_head(x):
        if x.ndim == 1:
            return pl.BlockSpec(memory_space=pltpu.SMEM)
        axis = 1 if x.ndim == 4 and x.shape[0] != heads else 0 if x.ndim > 2 else None
        block = tuple(1 if d == axis else n for d, n in enumerate(x.shape))
        return pl.BlockSpec(block, lambda h: tuple(h if d == axis else 0 for d in range(x.ndim)))

    specs = [by_head(x) for x in operands] + [pl.BlockSpec(memory_space=pltpu.HBM)] * len(kept)
    return pl.pallas_call(
        kernel,
        grid=(heads,),
        out_shape=out_shape,
        in_specs=specs,
        out_specs=[by_head(x) for x in out_shape],
        scratch_shapes=scratch,
        input_output_aliases=dict(aliases),
        compiler_params=params(24),
        cost_estimate=pl.CostEstimate(flops=4 * 10**9, bytes_accessed=8 * 10**6, transcendentals=3 * 10**6),
        name=name,
    )(*operands, *kept)


MARK = jax.ShapeDtypeStruct((8, LANES), F32)


def state_shape(q):
    return jax.ShapeDtypeStruct(q.shape[:3] + (LANES,), F32)


def first_block(valid, q, block, text):
    shapes = [jax.ShapeDtypeStruct(q.shape, BF16), state_shape(q), MARK]
    return attention_call(first_kernel, "own_block", [valid, q, block, text], [], shapes)


def next_blocks(q, state, blocks, mark):
    operands = [q, state, *blocks, mark]
    return attention_call(next_kernel, "next_blocks", operands, [], [state_shape(q), MARK], aliases=[(1, 0)])


def last_block(valid, q, state, block, first_text, text, kept):
    heads, _, rows, _ = q.shape
    shape = jax.ShapeDtypeStruct((rows, 4 * LANES), BF16)
    scratch = [
        pltpu.VMEM((heads, 2 * rows, LANES), F32),
        pltpu.VMEM((heads, 2 * rows, LANES), F32),
        pltpu.VMEM((len(kept) + 1, block.shape[0]) + block.shape[2:], BF16),
        pltpu.SemaphoreType.DMA,
    ]
    operands = [valid, q, state, block, first_text, text]
    return attention_call(functools.partial(last_kernel, len(kept)), "last_block", operands, kept, [shape], scratch)[0]


def finish_kernel(
    heads,
    groups,
    partial_ref,
    weight_ref,
    hidden_ref,
    modulation_ref,
    bias_ref,
    final_ref,
    final_bias_ref,
    out_ref,
    wide_ref,
):
    half = partial_ref.shape[1]
    sources = partial_ref.shape[0]
    across = groups // 2
    copies = sources // groups
    width = heads * HEAD_DIM
    low = lane_index((half, LANES)) < HEAD_DIM
    for part in range(2):
        at = part * 2 * LANES
        for group in range(groups):
            zl, y = divmod(group, across)
            members = [(zl * copies + copy) * across + y for copy in range(copies)]
            left = [partial_ref[m, :, at : at + LANES].astype(F32) for m in members]
            right = [partial_ref[m, :, at + LANES : at + 2 * LANES].astype(F32) for m in members]
            levels = [-(r + pltpu.roll(r, LANES - 1, 1) + pltpu.roll(r, LANES - 2, 1)) for r in right]
            counts = [pltpu.roll(r, LANES - 3, 1) + pltpu.roll(r, LANES - 4, 1) for r in right]
            top = functools.reduce(jnp.maximum, levels)
            shares = [count * jnp.exp2(level - top) for count, level in zip(counts, levels)]
            total = functools.reduce(jnp.add, shares)
            first, second = 0.0, 0.0
            for copy in range(copies):
                share = shares[copy] / total
                h0, h1, h2 = [share[:, c : c + 1] for c in (HEAD_DIM, HEAD_DIM + MARKS, HEAD_DIM + 2 * MARKS)]
                first = first + left[copy] * jnp.where(low, h0, h1)
                second = second + right[copy] * h2
            both = jnp.concatenate([first, second[:, :HEAD_DIM]], axis=1)
            wide_ref[part * half : (part + 1) * half, group * width : (group + 1) * width] = both
    attended = wide_ref[...].astype(BF16)
    projected = jnp.dot(attended, weight_ref[...], preferred_element_type=F32)
    residual = hidden_ref[...].astype(F32) + modulation_ref[0:1] * (projected + bias_ref[...])
    middle = jnp.mean(residual, axis=-1, keepdims=True)
    centered = residual - middle
    spread = jnp.mean(centered * centered, axis=-1, keepdims=True)
    normed = centered * lax.rsqrt(spread + 1e-06) * (1.0 + modulation_ref[1:2]) + modulation_ref[2:3]
    velocity = lax.dot_general(
        normed.astype(BF16), final_ref[...], (((1,), (1,)), ((), ())), preferred_element_type=F32
    )
    out_ref[...] = velocity + final_bias_ref[...]


def finish(partial, weight, hidden, modulation, bias, final_weight, final_bias, heads, groups):
    tokens, width = hidden.shape
    return pl.pallas_call(
        functools.partial(finish_kernel, heads, groups),
        out_shape=jax.ShapeDtypeStruct((tokens, final_weight.shape[0]), F32),
        scratch_shapes=[pltpu.VMEM((tokens, width), F32)],
        compiler_params=params(),
        name="project_and_norm",
    )(partial, weight, hidden, modulation, bias, final_weight, final_bias)


def local(
    latent_qkv,
    text_kv,
    hidden_in,
    modulation,
    out_weight,
    out_bias,
    proj_weight,
    proj_bias,
    guidance,
    sigma,
    sample,
):
    groups = lax.axis_size("zl") * lax.axis_size("y")
    ring = lax.axis_size("zh")
    tokens = latent_qkv.shape[1]
    half = tokens // 2
    width = latent_qkv.shape[3] // groups
    heads = width // HEAD_DIM
    across = lax.axis_size("y")
    zl, core, xh, y = (lax.axis_index(a) for a in ("zl", "core", "xh", "y"))
    after = lax.optimization_barrier

    slabs = pack(latent_qkv[0].transpose(1, 0, 2), groups, heads)
    slabs = lax.all_to_all(slabs, HEAD_AXES, split_axis=0, concat_axis=0, tiled=True)
    own = slabs[:, heads * half :].reshape(groups, heads, tokens, LANES)
    route = []
    for i in range(ring):
        route += [(2 * i, 2 * ((i + 1) % ring)), (2 * i + 1, 2 * ((i - 1) % ring) + 1)]
    pass_on = lambda x: lax.ppermute(x, ("zh", "core"), route)
    beside = lax.ppermute(own, "core", [(0, 1), (1, 0)])
    near = pass_on(own)
    packed = slabs[:, : heads * half].reshape(groups, heads, half, LANES)
    packed = lax.all_gather(packed, "core", axis=0)
    opposite = lax.ppermute(packed, "xh", [(0, 1), (1, 0)])
    cross = pass_on(beside)
    q = unpack_queries(xh.reshape(1), packed, opposite)

    weight = lax.all_gather(out_weight, ("xh", "y"), axis=0, tiled=True)

    count = text_kv.shape[1]
    share = -(-count // 32) * 16
    text = text_kv[0].reshape(count, 2, heads, HEAD_DIM).transpose(2, 0, 1, 3).reshape(heads, count, LANES)
    text = jnp.pad(text, ((0, 0), (0, 2 * share - count), (0, 0)))
    text = lax.dynamic_slice_in_dim(text, core * share, share, 1)
    valid = jnp.where(xh == zl, jnp.minimum(count - core * share, share), 0).reshape(1)
    early, late = text[:, :LANES], text[:, LANES:]
    q, state, mark = first_block(valid, q, own, early)
    kept = [own, near, cross]
    for step in range(ring // 2 - 2):
        if step:
            near, mark = after((near, mark))
        nearer = pass_on(near)
        cross, mark = after((cross, mark))
        crosser = pass_on(cross)
        state, mark = next_blocks(q, state, [near, cross], mark)
        near, cross = nearer, crosser
        kept += [near, cross]
    near, mark = after((near, mark))
    farthest = pass_on(near)
    state, mark = next_blocks(q, state, [near, cross], mark)
    partial = last_block(valid, q, state, farthest, early, late, kept)
    partial, weight = after((partial.reshape(4 * groups, half, 4 * LANES), weight))
    partial = lax.all_to_all(partial, BLOCK_AXES, split_axis=0, concat_axis=0, tiled=True)

    velocity = finish(
        partial,
        weight,
        hidden_in[0],
        modulation[0],
        out_bias[None],
        proj_weight.T,
        proj_bias[None],
        heads,
        groups,
    )

    tiles = velocity.reshape(tokens, 2, -1).transpose(1, 0, 2).reshape(2, -1)
    branch, parity = lax.axis_index("cfg"), y % 2
    same, swap = [], []
    for s in range(2):
        for y in range(across):
            a = y % 2
            same.append((s * across + y, a * across + y - a + s))
            swap.append((s * across + y, a * across + y - a + 1 - s))
    kept = lax.ppermute(lax.dynamic_slice_in_dim(tiles, branch, 1, 0), ("cfg", "y"), same)
    crossed = lax.ppermute(lax.dynamic_slice_in_dim(tiles, 1 - branch, 1, 0), ("cfg", "y"), swap)
    conditional = jnp.where(parity == 0, kept, crossed)
    unconditional = jnp.where(parity == 0, crossed, kept)
    guided = unconditional + guidance[0] * (conditional - unconditional)
    denoised = sample - sigma[0] * guided
    return (guided, denoised)


def solution(mesh):
    sizes = dict(zip(mesh.axis_names, mesh.devices.shape))
    ring = sizes["blk"] // 4
    fine = Mesh(
        mesh.devices.reshape(sizes["cfg"], ring, 2, 2, 2, sizes["uly"] // 2),
        ("cfg", "zh", "zl", "core", "xh", "y"),
    )
    rows = ("zh", "zl", "core", "xh", "y")
    heads = ("xh", "y")
    return jax.shard_map(
        local,
        mesh=fine,
        in_specs=(
            P("cfg", rows, None, None),
            P("cfg", None, None, heads),
            P("cfg", rows, None),
            P("cfg", None, None),
            P(heads, None),
            P(),
            P(),
            P(),
            P(),
            P(),
            P(rows, "cfg"),
        ),
        out_specs=(P(rows, "cfg"), P(rows, "cfg")),
        check_vma=False,
    )
```
